32 devices in a mesh: fsdp: 8 (over y, x, core), head: 4 (over z).
Axes of the slice: x: 2, y: 2, z: 4, core: 2. Of those that a mesh axis runs over, the one named last changes fastest.
Arguments:
- tokens: bfloat16 [2, 8192, 1024], P(None, ('fsdp', 'head')), may hold values from -6 to 6
- cotangent: bfloat16 [2, 8192, 1024], P(None, ('fsdp', 'head')), may hold values from -6 to 6
- lengths: int32 [2, 8], replicated, may hold values from 1 to 4096, 8192 in all within a row
- decay_rate: float32 [8], replicated, may hold values from 7.324219e-05 to 0.03
- query_weight: bfloat16 [1024, 1024], P('fsdp'), may hold values from -0.1875 to 0.1875
- key_weight: bfloat16 [1024, 1024], P('fsdp'), may hold values from -0.1875 to 0.1875
- value_weight: bfloat16 [1024, 1024], P('fsdp'), may hold values from -0.1875 to 0.1875
- gate_weight: bfloat16 [1024, 1024], P('fsdp'), may hold values from -0.1875 to 0.1875
- out_weight: bfloat16 [1024, 1024], P('fsdp'), may hold values from -0.1875 to 0.1875
- first_weight: bfloat16 [1024, 2816], P('fsdp'), may hold values from -0.1875 to 0.1875
- second_weight: bfloat16 [1024, 2816], P('fsdp'), may hold values from -0.1875 to 0.1875
- down_weight: bfloat16 [2816, 1024], P(None, 'fsdp'), may hold values from -0.109375 to 0.109375
Outputs:
- mixed: bfloat16 [2, 8192, 1024], P(None, ('fsdp', 'head'))
- grad_tokens: bfloat16 [2, 8192, 1024], P(None, ('fsdp', 'head'))
- grad_query: float32 [1024, 1024], P(('fsdp', 'head'))
- grad_key: float32 [1024, 1024], P(('fsdp', 'head'))
- grad_value: float32 [1024, 1024], P(('fsdp', 'head'))
- grad_gate: float32 [1024, 1024], P(('fsdp', 'head'))
- grad_out: float32 [1024, 1024], P(('fsdp', 'head'))
- grad_first: float32 [1024, 2816], P(('fsdp', 'head'))
- grad_second: float32 [1024, 2816], P(('fsdp', 'head'))
- grad_down: float32 [2816, 1024], P(None, ('fsdp', 'head'))
The draws below stay inside these ranges and needn't reach their ends.
Inputs may be any that keep to these rules, and one draw needn't show every extreme that they name: Each row holds 8 sequence lengths that sum to 8192; the largest is exactly 4096.
All inputs are finite; a program needn't handle non-finite values.
Results may differ from the reference program's by a relative error of at most 0.017.
Values may be sent and summed in bfloat16 or wider, within the bound.
A program may use at most 256 MiB of HBM per device.

```python
import math
import jax
import jax.numpy as jnp
import numpy as np
from jax import lax

D = 1024
H = 8
DH = 128
FF = 2816
MB = 2
BLOCK = 512
TOKENS = 8192
SEQ_MAX = 4096
NSEQ = 8


def levels(rng, shape, cuts, least, largest):
    def one(dim, shards_of):
        heights = jax.random.uniform(jax.random.fold_in(jax.random.fold_in(rng, 6), dim), (shards_of,), jnp.float32, least / len(cuts), largest / len(cuts))
        return jnp.repeat(jnp.exp(heights), shape[dim] // shards_of).reshape((-1,) + (1,) * (len(shape) - dim - 1))

    loudness = one(*cuts[0])
    for cut in cuts[1:]:
        loudness = loudness * one(*cut)
    return loudness


def length_profile(amount, total, bound, slope):
    portions = [(1 << 20) // math.isqrt(rank ** slope) + 1 for rank in range(2, amount + 1)]
    rest, counts = total - bound - (amount - 1), [1] * (amount - 1)
    while rest > 0:
        candidates = [i for i in range(amount - 1) if counts[i] < bound]
        whole, remaining = sum([portions[i] for i in candidates]), rest
        for i in candidates:
            addition = min(bound - counts[i], max(1, remaining * portions[i] // whole), rest)
            counts[i] = counts[i] + addition
            rest = rest - addition
    return np.array([bound] + counts)


def ragged_sizes(rng, count, total, most, lean):
    if count == 2:
        one = jax.random.randint(rng, (), max(1, total - most), min(most, total - 1) + 1)
        return jnp.stack([one, total - one])
    sizes = jnp.asarray(length_profile(count, total, most, lean), jnp.int32)
    twos = (count - 1) // 2
    giver, taker = sizes[1:1 + 2 * twos:2], sizes[2:2 + 2 * twos:2]
    slack = jnp.minimum(giver - 1, most - taker)
    passed = jax.random.randint(jax.random.fold_in(rng, 1), (twos,), 0, 1 << 20) % (slack + 1)
    sizes = sizes.at[1:1 + 2 * twos:2].set(giver - passed).at[2:2 + 2 * twos:2].set(taker + passed)
    return sizes[jax.random.permutation(jax.random.fold_in(rng, 2), count)]


def bell_draw(key, dims, deviation, bound, cuts=(), held_as=jnp.bfloat16):
    factor_of = levels(key, dims, cuts, -0.22, 0.18) if cuts else 1.0
    array = jax.random.normal(key, dims, jnp.float32) * deviation * factor_of
    return jnp.minimum(jnp.maximum(array, -bound), bound).astype(held_as)


def setup_inputs(seed: int = 0) -> dict:
    splits = jax.random.split(jax.random.key(seed), 13)
    tokens = bell_draw(splits[0], (MB, TOKENS, D), 1.0, 6.0, ((1, 32),))
    cotangent = bell_draw(splits[1], (MB, TOKENS, D), 1.0, 6.0, ((1, 32),))
    lengths = jax.vmap(lambda own: ragged_sizes(own, NSEQ, TOKENS, SEQ_MAX, 2))(jax.random.split(splits[2], MB)).reshape((MB, NSEQ)).astype(jnp.int32)
    decay_rate = jnp.clip(jnp.exp(jax.random.uniform(splits[3], (H,), jnp.float32, math.log(7.324219041038305e-05), math.log(0.03))), 7.324219041038305e-05, 0.03)
    query_weight = bell_draw(splits[4], (D, D), D ** -0.5, 0.1875, ((0, 8),))
    key_weight = bell_draw(splits[5], (D, D), D ** -0.5, 0.1875, ((0, 8),))
    value_weight = bell_draw(splits[6], (D, D), D ** -0.5, 0.1875, ((0, 8),))
    gate_weight = bell_draw(splits[7], (D, D), D ** -0.5, 0.1875, ((0, 8),))
    out_weight = bell_draw(splits[8], (D, D), D ** -0.5, 0.1875, ((0, 8),))
    first_weight = bell_draw(splits[9], (D, FF), D ** -0.5, 0.1875, ((0, 8),))
    second_weight = bell_draw(splits[10], (D, FF), D ** -0.5, 0.1875, ((0, 8),))
    down_weight = bell_draw(splits[11], (FF, D), FF ** -0.5, 0.109375, ((1, 8),))
    return dict(tokens=tokens, cotangent=cotangent, lengths=lengths, decay_rate=decay_rate, query_weight=query_weight, key_weight=key_weight, value_weight=value_weight, gate_weight=gate_weight, out_weight=out_weight, first_weight=first_weight, second_weight=second_weight, down_weight=down_weight)


EPSILON = 1e-06
PRECISE = lax.Precision.HIGHEST

@jax.custom_vjp
def low(v):
    return lax.optimization_barrier(v.astype(jnp.bfloat16)).astype(jnp.float32)

@jax.custom_vjp
def low_back(v):
    return v

def low_keep(v):
    return (low(v), None)

def low_pass(kept, grad):
    return (grad,)

def back_keep(v):
    return (v, None)

def back_low(kept, grad):
    return (low(grad),)
low.defvjp(low_keep, low_pass)
low_back.defvjp(back_keep, back_low)

def simple_norm(values):
    return values * lax.rsqrt(lax.optimization_barrier(jnp.mean(values * values, axis=-1, keepdims=True)) + EPSILON)

def rotate_pairs(values, cosine, sine_vals):
    half_size = values.shape[-1] // 2
    first_half = values[..., :half_size]
    second_half = values[..., half_size:]
    return jnp.concatenate([first_half * cosine - second_half * sine_vals, first_half * sine_vals + second_half * cosine], axis=-1)

def rotation_tables(positions, head_size):
    half_size = head_size // 2
    shifts = jnp.arange(half_size, dtype=jnp.int32) * 10 // half_size
    speeds = jnp.right_shift(jnp.full((half_size,), 651, jnp.int32), shifts) + 1
    phases = positions[:, None] * speeds[None, :] % 4096
    angles = phases.astype(jnp.float32) * (2.0 * math.pi / 4096.0)
    return (jnp.cos(angles)[:, None, :], jnp.sin(angles)[:, None, :])

def segment_ids(seq_lengths, positions):
    seq_ends = jnp.cumsum(seq_lengths).astype(jnp.int32)
    return lax.optimization_barrier(jnp.sum((seq_ends[None, :] <= positions[:, None]).astype(jnp.int32), axis=1)).astype(jnp.int32)

def block_mask(seg_blk, decay_here):
    row_count = seg_blk.shape[0]
    offsets = jnp.arange(row_count, dtype=jnp.float32)
    distance = offsets[:, None] - offsets[None, :]
    visible = (seg_blk[:, None] == seg_blk[None, :]) & (distance >= 0.0)
    return jnp.where(visible[None], jnp.exp(-decay_here[:, None, None] * jnp.maximum(distance, 0.0)[None]), 0.0)

def edge_terms(seg_blk, seg_before, decay_here):
    row_count = seg_blk.shape[0]
    offsets = jnp.arange(row_count, dtype=jnp.float32)
    entering = jnp.where((seg_blk == seg_before)[:, None], jnp.exp(-decay_here[None, :] * (offsets[:, None] + 1.0)), 0.0)
    leaving = jnp.where((seg_blk == seg_blk[row_count - 1])[:, None], jnp.exp(-decay_here[None, :] * (row_count - 1.0 - offsets)[:, None]), 0.0)
    through = jnp.where(seg_blk[row_count - 1] == seg_before, jnp.exp(-decay_here * row_count), 0.0)
    return (entering, leaving, through)

def attend(queries, keys_rot, values_h, segs, befores, decay_here):
    num_blocks = TOKENS // BLOCK

    def step_fn(carried, pieces):
        query_blk, key_blk, value_blk, seg_blk, before_blk = pieces
        within = block_mask(seg_blk, decay_here)
        entering, leaving, through = edge_terms(seg_blk, before_blk, decay_here)
        scores = jnp.einsum('shd,thd->hst', query_blk, key_blk, precision=PRECISE) * within
        result = jnp.einsum('hst,thd->shd', scores, value_blk, precision=PRECISE)
        result = result + entering[:, :, None] * jnp.einsum('shd,hde->she', query_blk, carried, precision=PRECISE)
        updated = through[:, None, None] * carried + jnp.einsum('thd,the->hde', key_blk * leaving[:, :, None], value_blk, precision=PRECISE)
        return (updated, result)
    zero_state = jnp.zeros((H, DH, DH), jnp.float32)
    final_state, results = lax.scan(jax.checkpoint(step_fn), zero_state, (queries.reshape(num_blocks, BLOCK, H, DH), keys_rot.reshape(num_blocks, BLOCK, H, DH), values_h.reshape(num_blocks, BLOCK, H, DH), segs.reshape(num_blocks, BLOCK), befores))
    return results.reshape(TOKENS, H, DH)

def layer(inputs, weights, cosine, sine_vals, segs, befores, decay_here):
    query_full, key_full, value_full, gate_full, out_full, first_full, second_full, down_full = weights
    act_in = low(simple_norm(inputs))
    query_pre = low_back(jnp.dot(act_in, query_full, precision=PRECISE))
    key_pre = low_back(jnp.dot(act_in, key_full, precision=PRECISE))
    value_low = low(low_back(jnp.dot(act_in, value_full, precision=PRECISE)))
    gate_vals = low_back(jnp.dot(act_in, gate_full, precision=PRECISE))
    query_low = low(low_back(rotate_pairs(jax.nn.silu(query_pre).reshape(TOKENS, H, DH), cosine, sine_vals)))
    key_low = low(low_back(rotate_pairs(jax.nn.silu(key_pre).reshape(TOKENS, H, DH), cosine, sine_vals)))
    attended = attend(query_low, key_low, value_low.reshape(TOKENS, H, DH), segs, befores, decay_here).reshape(TOKENS, D)
    attended = low(low_back(attended))
    gated = low(simple_norm(attended) * gate_vals)
    hidden = inputs + low_back(jnp.dot(gated, out_full, precision=PRECISE))
    act_mid = low(simple_norm(hidden))
    first_pre = low_back(jnp.dot(act_mid, first_full, precision=PRECISE))
    second_pre = low_back(jnp.dot(act_mid, second_full, precision=PRECISE))
    product = low(first_pre * second_pre)
    return hidden + low_back(jnp.dot(product, down_full, precision=PRECISE))

def reference(tokens, cotangent, lengths, decay_rate, query_weight, key_weight, value_weight, gate_weight, out_weight, first_weight, second_weight, down_weight):
    weights = tuple((matrix.astype(jnp.float32) for matrix in (query_weight, key_weight, value_weight, gate_weight, out_weight, first_weight, second_weight, down_weight)))
    positions = jnp.arange(TOKENS, dtype=jnp.int32)
    cosine, sine_vals = rotation_tables(positions, DH)
    mixed_list = []
    input_grads = []
    grad_totals = None
    for micro_step in range(MB):
        segs = segment_ids(lengths[micro_step], positions)
        befores = jnp.concatenate([jnp.zeros((1,), jnp.int32), segs[BLOCK - 1::BLOCK][:-1]]).astype(jnp.int32)

        def forward(inputs, weight_set):
            return layer(inputs, weight_set, cosine, sine_vals, segs, befores, decay_rate)
        result, pullback = jax.vjp(forward, tokens[micro_step].astype(jnp.float32), weights)
        grad_in, grad_set = pullback(cotangent[micro_step].astype(jnp.float32))
        mixed_list.append(result.astype(jnp.bfloat16))
        input_grads.append(grad_in.astype(jnp.bfloat16))
        grad_totals = grad_set if grad_totals is None else tuple((total + term for total, term in zip(grad_totals, grad_set)))
    return (jnp.stack(mixed_list), jnp.stack(input_grads), grad_totals[0], grad_totals[1], grad_totals[2], grad_totals[3], grad_totals[4], grad_totals[5], grad_totals[6], grad_totals[7])
```

```python
import math

import jax
import jax.numpy as jnp
from jax import lax
from jax.sharding import PartitionSpec as P

H = 8
DH = 128
EPSILON = 1e-06
AXES = ("fsdp", "head")
F32 = jnp.float32
BF16 = jnp.bfloat16


def norm_parts(values):
    inv_scale = lax.rsqrt(jnp.mean(values * values, axis=-1, keepdims=True) + EPSILON)
    return (values * inv_scale, inv_scale)


def norm_back(gradient, normed, inv_scale):
    return inv_scale * (gradient - normed * jnp.mean(gradient * normed, axis=-1, keepdims=True))


def rotate_pairs(values, cosine, sine_vals):
    half_size = values.shape[-1] // 2
    first_half = values[..., :half_size]
    second_half = values[..., half_size:]
    return jnp.concatenate(
        [
            first_half * cosine - second_half * sine_vals,
            first_half * sine_vals + second_half * cosine,
        ],
        axis=-1,
    )


def rotation_tables(positions, head_size):
    half_size = head_size // 2
    shifts = jnp.arange(half_size, dtype=jnp.int32) * 10 // half_size
    speeds = jnp.right_shift(jnp.full((half_size,), 651, jnp.int32), shifts) + 1
    phases = positions[:, None] * speeds[None, :] % 4096
    angles = phases.astype(F32) * (2.0 * math.pi / 4096.0)
    return (jnp.cos(angles)[:, None, :], jnp.sin(angles)[:, None, :])


def silu_slope(values):
    sigmoid_v = jax.nn.sigmoid(values)
    return sigmoid_v * (1.0 + values * (1.0 - sigmoid_v))


def dot(a, b):
    return jnp.dot(a, b, preferred_element_type=F32)


def dot_rows(a, b):
    return lax.dot_general(a, b, (((0,), (0,)), ((), ())), preferred_element_type=F32)


def dot_cols(a, b):
    return lax.dot_general(a, b, (((1,), (1,)), ((), ())), preferred_element_type=F32)


class Wires:
    def __init__(self):
        self.nf = lax.axis_size("fsdp")
        self.nh = lax.axis_size("head")
        self.fast = self.nf == 8 and self.nh == 4
        self.f = lax.axis_index("fsdp")
        self.h = lax.axis_index("head")

    def swap(self, values, fbits=0, hbits=0):
        pairs = []
        for f in range(self.nf):
            for h in range(self.nh):
                pairs.append((f * self.nh + h, (f ^ fbits) * self.nh + (h ^ hbits)))
        return lax.ppermute(values, AXES, pairs)

    def rel(self, values):
        if not self.fast:
            return values
        width = values.shape[1] // self.nf
        return jnp.concatenate(
            [
                lax.dynamic_slice_in_dim(values, (self.f ^ i) * width, width, 1)
                for i in range(self.nf)
            ],
            axis=1,
        )

    def gather(self, shard):
        if not self.fast:
            return lax.all_gather(shard, "fsdp", axis=0, tiled=True)
        half = shard.shape[1] // 2
        core, x, y = 1, 2, 4
        at_c = self.swap(shard, core)
        at_x = self.swap(shard, x)
        at_y = self.swap(shard, y)
        at_xy = jnp.concatenate(
            [self.swap(at_x[:, :half], y), self.swap(at_y[:, half:], x)], axis=1
        )
        at_cx = self.swap(at_x, core)
        at_cy = self.swap(at_y, core)
        at_cxy = self.swap(at_xy, core)
        return jnp.concatenate([shard, at_c, at_x, at_cx, at_y, at_cy, at_xy, at_cxy], axis=0)

    def reduce(self, grad):
        if not self.fast:
            return lax.psum_scatter(grad, AXES, scatter_dimension=0, tiled=True)
        core, x, y = 1, 2, 4
        rows, n = grad.shape[0] // 8, grad.shape[1]
        low = grad.astype(BF16).reshape(2, 2, 2, rows, n)
        merged = (low[:, :, 0].astype(F32) + self.swap(low[:, :, 1], core).astype(F32)).astype(BF16)
        half = n // 2
        a = merged[:, :, :, :half]
        a = (a[:, 0].astype(F32) + self.swap(a[:, 1], x).astype(F32)).astype(BF16)
        a = (a[0].astype(F32) + self.swap(a[1], y).astype(F32)).astype(BF16)
        b = merged[:, :, :, half:]
        b = (b[0].astype(F32) + self.swap(b[1], y).astype(F32)).astype(BF16)
        b = (b[0].astype(F32) + self.swap(b[1], x).astype(F32)).astype(BF16)
        return jnp.concatenate([self.along(a), self.along(b)], axis=1)

    def along(self, part):
        rows, n = part.shape
        part = part.reshape(2, 2, rows // 4, n)
        low, high = self.h % 2, self.h // 2
        keep = lax.dynamic_index_in_dim(part, low, 1, False)
        send = lax.dynamic_index_in_dim(part, 1 - low, 1, False)
        part = (keep.astype(F32) + self.swap(send, 0, 1).astype(F32)).astype(BF16)
        keep = lax.dynamic_index_in_dim(part, high, 0, False)
        send = lax.dynamic_index_in_dim(part, 1 - high, 0, False)
        return keep.astype(F32) + self.swap(send, 0, 2).astype(F32)

    def to_heads(self, states):
        mb, heads, d, _ = states.shape
        mine = heads // self.nh
        parts = jnp.moveaxis(states.reshape(mb, self.nh, mine, d, d), 1, 0)
        return self.scatter(parts)

    def scatter(self, parts):
        if not self.fast:
            return lax.all_to_all(parts, "head", split_axis=0, concat_axis=0, tiled=True)
        got = [lax.dynamic_index_in_dim(parts, self.h, 0, False)]
        for i in range(1, self.nh):
            got.append(self.swap(lax.dynamic_index_in_dim(parts, self.h ^ i, 0, False), 0, i))
        got = jnp.stack(got)
        order = self.h ^ jnp.arange(self.nh)
        return jnp.take(got, order, axis=0)

    def from_heads(self, parts):
        got = self.scatter(parts)
        nh, mb, mine, d, _ = got.shape
        return jnp.moveaxis(got, 0, 1).reshape(mb, nh * mine, d, d)

    def spread(self, total):
        if not self.fast:
            return lax.all_gather(total, "fsdp")
        core, x, y = 1, 2, 4
        at_c = self.swap(total, core)
        pair = jnp.stack([total, at_c])
        at_x = self.swap(pair, x)
        at_y = self.swap(pair, y)
        at_xy = self.swap(pair, x + y)
        got = jnp.concatenate([pair, at_x, at_y, at_xy])
        return jnp.take(got, self.f ^ jnp.arange(self.nf), axis=0)


def chain(wires, states, ends, decay, chunk, backward):
    nf, nh, f = wires.nf, wires.nh, wires.f
    mb, heads = states.shape[:2]
    mine = heads // nh
    rates = lax.dynamic_slice_in_dim(decay, wires.h * mine, mine)
    places = jnp.arange(nh)
    groups = jnp.arange(nf)
    at_group = lax.dynamic_slice_in_dim(ends, f * nh, nh, axis=1)
    before_group = jnp.where(
        f > 0, lax.dynamic_index_in_dim(ends, jnp.maximum(f * nh - 1, 0), 1, False), 0
    )
    before = jnp.concatenate([before_group[:, None], at_group[:, :-1]], axis=1)
    last = at_group[:, -1]
    group_last = ends.reshape(mb, nf, nh)[:, :, -1]
    group_before = jnp.concatenate([jnp.zeros_like(group_last[:, :1]), group_last[:, :-1]], axis=1)

    def factor(same, gap):
        gap = jnp.maximum(gap, 0)
        return jnp.where(
            same[..., None], jnp.exp(-rates * (chunk * gap).astype(F32)[..., None]), 0.0
        )

    own = wires.to_heads(states.astype(BF16)).astype(F32)
    if backward:
        to_total = factor(before == before_group[:, None], jnp.broadcast_to(places, (mb, nh)))
        group_same = (last[:, None] == group_before) & (groups > f)
        group_gap = jnp.broadcast_to((groups - 1 - f) * nh, (mb, nf))
        to_place = factor(at_group == last[:, None], jnp.broadcast_to(nh - 1 - places, (mb, nh)))
        same = (at_group[:, :, None] == before[:, None, :]) & (places[None, :] > places[:, None])
        gap = jnp.broadcast_to(places[None, :] - 1 - places[:, None], (mb, nh, nh))
    else:
        to_total = factor(at_group == last[:, None], jnp.broadcast_to(nh - 1 - places, (mb, nh)))
        group_same = (before_group[:, None] == group_last) & (groups < f)
        group_gap = jnp.broadcast_to((f - 1 - groups) * nh, (mb, nf))
        to_place = factor(before == before_group[:, None], jnp.broadcast_to(places, (mb, nh)))
        same = (before[:, :, None] == at_group[:, None, :]) & (places[None, :] < places[:, None])
        gap = jnp.broadcast_to(places[:, None] - 1 - places[None, :], (mb, nh, nh))
    total = sum(to_total[:, i, :, None, None] * own[i] for i in range(nh))
    totals = wires.spread(total.astype(BF16)).astype(F32)
    from_group = factor(group_same, group_gap)
    outer = sum(from_group[:, i, :, None, None] * totals[i] for i in range(nf))
    between = factor(same, gap)
    result = [
        to_place[:, i, :, None, None] * outer
        + sum(between[:, i, j, :, None, None] * own[j] for j in range(nh) if i != j)
        for i in range(nh)
    ]
    return wires.from_heads(jnp.stack(result).astype(BF16))


def masks(segs, before, last, decay):
    rows = segs.shape[1]
    offsets = jnp.arange(rows, dtype=F32)
    distance = offsets[:, None] - offsets[None, :]
    visible = (segs[:, :, None] == segs[:, None, :]) & (distance >= 0.0)
    within = jnp.where(
        visible[:, None],
        jnp.exp(-decay[:, None, None] * jnp.maximum(distance, 0.0))[None],
        0.0,
    )
    entering = jnp.where(
        (segs == before[:, None])[:, None, :],
        jnp.exp(-decay[:, None] * (offsets + 1.0))[None],
        0.0,
    )
    leaving = jnp.where(
        (segs == last[:, None])[:, None, :],
        jnp.exp(-decay[:, None] * (rows - 1.0 - offsets))[None],
        0.0,
    )
    return within, entering[..., None], leaving[..., None]


def local(
    tokens,
    cotangent,
    lengths,
    decay_rate,
    query_weight,
    key_weight,
    value_weight,
    gate_weight,
    out_weight,
    first_weight,
    second_weight,
    down_weight,
):
    wires = Wires()
    mb, chunk, width = tokens.shape
    rows = mb * chunk
    place = wires.f * wires.nh + wires.h
    count = wires.nf * wires.nh

    mix_weights = wires.gather(
        jnp.concatenate([query_weight, key_weight, value_weight, gate_weight], axis=1)
    )
    out_full = wires.gather(out_weight)
    gate_up = wires.gather(jnp.concatenate([first_weight, second_weight], axis=1))
    down_t = wires.gather(down_weight.T)
    hidden_size = down_t.shape[1]

    positions = place * chunk + jnp.arange(chunk, dtype=jnp.int32)
    cosine, sine_vals = rotation_tables(positions, DH)
    cosine, sine_vals = jnp.tile(cosine, (mb, 1, 1)), jnp.tile(sine_vals, (mb, 1, 1))
    seq_ends = jnp.cumsum(lengths, axis=1)
    segs = jnp.sum((seq_ends[:, None, :] <= positions[None, :, None]).astype(jnp.int32), axis=2)
    marks = (jnp.arange(count, dtype=jnp.int32) + 1) * chunk - 1
    ends = jnp.sum((seq_ends[:, None, :] <= marks[None, :, None]).astype(jnp.int32), axis=2)
    last = lax.dynamic_index_in_dim(ends, place, 1, False)
    before = jnp.where(
        place > 0, lax.dynamic_index_in_dim(ends, jnp.maximum(place - 1, 0), 1, False), 0
    )
    within, entering, leaving = masks(segs, before, last, decay_rate)

    def heads(values):
        return values.reshape(mb, chunk, H, DH).transpose(0, 2, 1, 3)

    def flat(values):
        return values.transpose(0, 2, 1, 3).reshape(rows, H * DH)

    def mm(spec, a, b):
        return jnp.einsum(spec, a.astype(BF16), b.astype(BF16), preferred_element_type=F32)

    inputs = tokens.reshape(rows, width).astype(F32)
    normed_in, scale_in = norm_parts(inputs)
    act_rel = wires.rel(normed_in.astype(BF16))
    mixed_pre = dot(act_rel, mix_weights)
    query_pre = mixed_pre[:, :width]
    key_pre = mixed_pre[:, width : 2 * width]
    value_low = mixed_pre[:, 2 * width : 3 * width].astype(BF16)
    gate_vals = mixed_pre[:, 3 * width :]

    def turned(values):
        return rotate_pairs(jax.nn.silu(values).reshape(rows, H, DH), cosine, sine_vals).astype(BF16)

    query_h = heads(turned(query_pre))
    key_h = heads(turned(key_pre))
    value_h = heads(value_low)
    local_state = mm("mhtd,mhte->mhde", key_h * leaving, value_h)
    state_in = chain(wires, local_state, ends, decay_rate, chunk, False)
    scores = (mm("mhsd,mhtd->mhst", query_h, key_h) * within).astype(BF16)
    attended = mm("mhst,mhte->mhse", scores, value_h)
    attended = attended + entering * mm("mhsd,mhde->mhse", query_h, state_in)
    attended = flat(attended.astype(BF16))

    normed_att, scale_att = norm_parts(attended.astype(F32))
    gated_rel = wires.rel((normed_att * gate_vals).astype(BF16))
    hidden = inputs + dot(gated_rel, out_full)
    normed_mid, scale_mid = norm_parts(hidden)
    mid_rel = wires.rel(normed_mid.astype(BF16))
    pre = dot(mid_rel, gate_up)
    first_pre, second_pre = pre[:, :hidden_size], pre[:, hidden_size:]
    product = (first_pre * second_pre).astype(BF16)
    mixed = (hidden + wires.rel(dot_cols(product, down_t))).astype(BF16)

    grad_low = cotangent.reshape(rows, width)
    grad_rel = wires.rel(grad_low)
    share_down = wires.reduce(dot_rows(grad_rel, product)).T
    grad_prod = dot(grad_rel, down_t)
    grad_pre = jnp.concatenate(
        [(grad_prod * second_pre).astype(BF16), (grad_prod * first_pre).astype(BF16)], axis=1
    )
    share_up = wires.reduce(dot_rows(mid_rel, grad_pre))
    grad_mid = wires.rel(dot_cols(grad_pre, gate_up))
    grad_hidden = grad_low.astype(F32) + norm_back(grad_mid, normed_mid, scale_mid)
    grad_hidden_low = grad_hidden.astype(BF16)
    share_out = wires.reduce(dot_rows(gated_rel, grad_hidden_low))
    grad_gated = wires.rel(dot_cols(grad_hidden_low, out_full))
    grad_gate_low = (grad_gated * normed_att).astype(BF16)
    grad_att = heads(norm_back(grad_gated * gate_vals, normed_att, scale_att).astype(BF16))

    grad_state = mm("mhsd,mhse->mhde", query_h * entering, grad_att)
    grad_end = chain(wires, grad_state, ends, decay_rate, chunk, True)
    grad_scores = (mm("mhse,mhte->mhst", grad_att, value_h) * within).astype(BF16)
    grad_q = mm("mhst,mhtd->mhsd", grad_scores, key_h)
    grad_q = grad_q + entering * mm("mhse,mhde->mhsd", grad_att, state_in)
    grad_k = mm("mhst,mhsd->mhtd", grad_scores, query_h)
    grad_k = grad_k + leaving * mm("mhte,mhde->mhtd", value_h, grad_end)
    grad_v = mm("mhst,mhse->mhte", scores, grad_att)
    grad_v = grad_v + leaving * mm("mhtd,mhde->mhte", key_h, grad_end)

    def turned_back(values, pre_values):
        back = flat(values.astype(BF16)).astype(F32).reshape(rows, H, DH)
        back = rotate_pairs(back, cosine, -sine_vals).reshape(rows, width)
        return (silu_slope(pre_values) * back).astype(BF16)

    grad_mix = jnp.concatenate(
        [
            turned_back(grad_q, query_pre),
            turned_back(grad_k, key_pre),
            flat(grad_v.astype(BF16)),
            grad_gate_low,
        ],
        axis=1,
    )
    share_mix = wires.reduce(dot_rows(act_rel, grad_mix))
    grad_act = wires.rel(dot_cols(grad_mix, mix_weights))
    grad_tokens = (grad_hidden + norm_back(grad_act, normed_in, scale_in)).astype(BF16)
    return (
        mixed.reshape(mb, chunk, width),
        grad_tokens.reshape(mb, chunk, width),
        share_mix[:, :width],
        share_mix[:, width : 2 * width],
        share_mix[:, 2 * width : 3 * width],
        share_mix[:, 3 * width :],
        share_out,
        share_up[:, :hidden_size],
        share_up[:, hidden_size:],
        share_down,
    )


def solution(mesh):
    rows = P(None, AXES, None)
    in_specs = (rows, rows, P(), P()) + (P("fsdp", None),) * 7 + (P(None, "fsdp"),)
    out_specs = (rows, rows) + (P(AXES, None),) * 7 + (P(None, AXES),)
    return jax.shard_map(local, mesh=mesh, in_specs=in_specs, out_specs=out_specs, check_vma=False)
```

```python
import functools
import math

import jax
import jax.numpy as jnp
from jax import lax
from jax.experimental import pallas as pl
from jax.experimental.pallas import tpu as pltpu
from jax.sharding import PartitionSpec as P

H = 8
DH = 128
EPSILON = 1e-06
AXES = ("fsdp", "head")
F32 = jnp.float32
BF16 = jnp.bfloat16
MESH = pl.DeviceIdType.MESH
ANY = pl.BlockSpec(memory_space=pl.ANY)
VMEM = pl.BlockSpec(memory_space=pltpu.VMEM)
SMEM = pl.BlockSpec(memory_space=pltpu.SMEM)
VMEM_BYTES = 63 * 1024 * 1024
TILE = 256


def norm_parts(values):
    inv_scale = lax.rsqrt(jnp.mean(values * values, axis=-1, keepdims=True) + EPSILON)
    return (values * inv_scale, inv_scale)


def norm_back(gradient, normed, inv_scale):
    return inv_scale * (gradient - normed * jnp.mean(gradient * normed, axis=-1, keepdims=True))


def rotate_pairs(values, cosine, sine_vals):
    half_size = values.shape[-1] // 2
    first_half = values[..., :half_size]
    second_half = values[..., half_size:]
    return jnp.concatenate(
        [
            first_half * cosine - second_half * sine_vals,
            first_half * sine_vals + second_half * cosine,
        ],
        axis=-1,
    )


def rotation_tables(positions, head_size):
    half_size = head_size // 2
    shifts = jnp.arange(half_size, dtype=jnp.int32) * 10 // half_size
    speeds = jnp.right_shift(jnp.full((half_size,), 651, jnp.int32), shifts) + 1
    phases = positions[:, None] * speeds[None, :] % 4096
    angles = phases.astype(F32) * (2.0 * math.pi / 4096.0)
    return (jnp.cos(angles)[:, None, :], jnp.sin(angles)[:, None, :])


def silu_slope(values):
    sigmoid_v = jax.nn.sigmoid(values)
    return sigmoid_v * (1.0 + values * (1.0 - sigmoid_v))


def dot(a, b):
    return jnp.dot(a, b, preferred_element_type=F32)


def dot_rows(a, b):
    return lax.dot_general(a, b, (((0,), (0,)), ((), ())), preferred_element_type=F32)


def dot_cols(a, b):
    return lax.dot_general(a, b, (((1,), (1,)), ((), ())), preferred_element_type=F32)


class Wires:
    def __init__(self):
        self.nf = lax.axis_size("fsdp")
        self.nh = lax.axis_size("head")
        self.fast = self.nf == 8 and self.nh == 4
        self.f = lax.axis_index("fsdp")
        self.h = lax.axis_index("head")

    def swap(self, values, fbits=0, hbits=0):
        pairs = []
        for f in range(self.nf):
            for h in range(self.nh):
                pairs.append((f * self.nh + h, (f ^ fbits) * self.nh + (h ^ hbits)))
        return lax.ppermute(values, AXES, pairs)

    def rel(self, values):
        if not self.fast:
            return values
        width = values.shape[1] // self.nf
        return jnp.concatenate(
            [
                lax.dynamic_slice_in_dim(values, (self.f ^ i) * width, width, 1)
                for i in range(self.nf)
            ],
            axis=1,
        )

    def gather(self, shard):
        if not self.fast:
            return lax.all_gather(shard, "fsdp", axis=0, tiled=True)
        half = shard.shape[1] // 2
        core, x, y = 1, 2, 4
        at_c = self.swap(shard, core)
        at_x = self.swap(shard, x)
        at_y = self.swap(shard, y)
        at_xy = jnp.concatenate(
            [self.swap(at_x[:, :half], y), self.swap(at_y[:, half:], x)], axis=1
        )
        at_cx = self.swap(at_x, core)
        at_cy = self.swap(at_y, core)
        at_cxy = self.swap(at_xy, core)
        return jnp.concatenate([shard, at_c, at_x, at_cx, at_y, at_cy, at_xy, at_cxy], axis=0)

    def reduce(self, grad):
        if not self.fast:
            return lax.psum_scatter(grad, AXES, scatter_dimension=0, tiled=True)
        core, x, y = 1, 2, 4
        rows, n = grad.shape[0] // 8, grad.shape[1]
        low = grad.astype(BF16).reshape(2, 2, 2, rows, n)
        merged = (low[:, :, 0].astype(F32) + self.swap(low[:, :, 1], core).astype(F32)).astype(BF16)
        half = n // 2
        a = merged[:, :, :, :half]
        a = (a[:, 0].astype(F32) + self.swap(a[:, 1], x).astype(F32)).astype(BF16)
        a = (a[0].astype(F32) + self.swap(a[1], y).astype(F32)).astype(BF16)
        b = merged[:, :, :, half:]
        b = (b[0].astype(F32) + self.swap(b[1], y).astype(F32)).astype(BF16)
        b = (b[0].astype(F32) + self.swap(b[1], x).astype(F32)).astype(BF16)
        return jnp.concatenate([self.along(a), self.along(b)], axis=1)

    def along(self, part):
        rows, n = part.shape
        part = part.reshape(2, 2, rows // 4, n)
        low, high = self.h % 2, self.h // 2
        keep = lax.dynamic_index_in_dim(part, low, 1, False)
        send = lax.dynamic_index_in_dim(part, 1 - low, 1, False)
        part = (keep.astype(F32) + self.swap(send, 0, 1).astype(F32)).astype(BF16)
        keep = lax.dynamic_index_in_dim(part, high, 0, False)
        send = lax.dynamic_index_in_dim(part, 1 - high, 0, False)
        return keep.astype(F32) + self.swap(send, 0, 2).astype(F32)

    def to_heads(self, states):
        mb, heads, d, _ = states.shape
        mine = heads // self.nh
        parts = jnp.moveaxis(states.reshape(mb, self.nh, mine, d, d), 1, 0)
        return self.scatter(parts)

    def scatter(self, parts):
        if not self.fast:
            return lax.all_to_all(parts, "head", split_axis=0, concat_axis=0, tiled=True)
        got = [lax.dynamic_index_in_dim(parts, self.h, 0, False)]
        for i in range(1, self.nh):
            got.append(self.swap(lax.dynamic_index_in_dim(parts, self.h ^ i, 0, False), 0, i))
        got = jnp.stack(got)
        order = self.h ^ jnp.arange(self.nh)
        return jnp.take(got, order, axis=0)

    def from_heads(self, parts):
        got = self.scatter(parts)
        nh, mb, mine, d, _ = got.shape
        return jnp.moveaxis(got, 0, 1).reshape(mb, nh * mine, d, d)

    def spread(self, total):
        if not self.fast:
            return lax.all_gather(total, "fsdp")
        core, x, y = 1, 2, 4
        at_c = self.swap(total, core)
        pair = jnp.stack([total, at_c])
        at_x = self.swap(pair, x)
        at_y = self.swap(pair, y)
        at_xy = self.swap(pair, x + y)
        got = jnp.concatenate([pair, at_x, at_y, at_xy])
        return jnp.take(got, self.f ^ jnp.arange(self.nf), axis=0)


def chain(wires, states, ends, decay, chunk, backward):
    nf, nh, f = wires.nf, wires.nh, wires.f
    mb, heads = states.shape[:2]
    mine = heads // nh
    rates = lax.dynamic_slice_in_dim(decay, wires.h * mine, mine)
    places = jnp.arange(nh)
    groups = jnp.arange(nf)
    at_group = lax.dynamic_slice_in_dim(ends, f * nh, nh, axis=1)
    before_group = jnp.where(
        f > 0, lax.dynamic_index_in_dim(ends, jnp.maximum(f * nh - 1, 0), 1, False), 0
    )
    before = jnp.concatenate([before_group[:, None], at_group[:, :-1]], axis=1)
    last = at_group[:, -1]
    group_last = ends.reshape(mb, nf, nh)[:, :, -1]
    group_before = jnp.concatenate([jnp.zeros_like(group_last[:, :1]), group_last[:, :-1]], axis=1)

    def factor(same, gap):
        gap = jnp.maximum(gap, 0)
        return jnp.where(
            same[..., None], jnp.exp(-rates * (chunk * gap).astype(F32)[..., None]), 0.0
        )

    own = wires.to_heads(states.astype(BF16)).astype(F32)
    if backward:
        to_total = factor(before == before_group[:, None], jnp.broadcast_to(places, (mb, nh)))
        group_same = (last[:, None] == group_before) & (groups > f)
        group_gap = jnp.broadcast_to((groups - 1 - f) * nh, (mb, nf))
        to_place = factor(at_group == last[:, None], jnp.broadcast_to(nh - 1 - places, (mb, nh)))
        same = (at_group[:, :, None] == before[:, None, :]) & (places[None, :] > places[:, None])
        gap = jnp.broadcast_to(places[None, :] - 1 - places[:, None], (mb, nh, nh))
    else:
        to_total = factor(at_group == last[:, None], jnp.broadcast_to(nh - 1 - places, (mb, nh)))
        group_same = (before_group[:, None] == group_last) & (groups < f)
        group_gap = jnp.broadcast_to((f - 1 - groups) * nh, (mb, nf))
        to_place = factor(before == before_group[:, None], jnp.broadcast_to(places, (mb, nh)))
        same = (before[:, :, None] == at_group[:, None, :]) & (places[None, :] < places[:, None])
        gap = jnp.broadcast_to(places[:, None] - 1 - places[None, :], (mb, nh, nh))
    total = sum(to_total[:, i, :, None, None] * own[i] for i in range(nh))
    totals = wires.spread(total.astype(BF16)).astype(F32)
    from_group = factor(group_same, group_gap)
    outer = sum(from_group[:, i, :, None, None] * totals[i] for i in range(nf))
    between = factor(same, gap)
    result = [
        to_place[:, i, :, None, None] * outer
        + sum(between[:, i, j, :, None, None] * own[j] for j in range(nh) if i != j)
        for i in range(nh)
    ]
    return wires.from_heads(jnp.stack(result).astype(BF16))


def masks(segs, before, last, decay):
    rows = segs.shape[1]
    offsets = jnp.arange(rows, dtype=F32)
    distance = offsets[:, None] - offsets[None, :]
    visible = (segs[:, :, None] == segs[:, None, :]) & (distance >= 0.0)
    within = jnp.where(
        visible[:, None],
        jnp.exp(-decay[:, None, None] * jnp.maximum(distance, 0.0))[None],
        0.0,
    )
    entering = jnp.where(
        (segs == before[:, None])[:, None, :],
        jnp.exp(-decay[:, None] * (offsets + 1.0))[None],
        0.0,
    )
    leaving = jnp.where(
        (segs == last[:, None])[:, None, :],
        jnp.exp(-decay[:, None] * (rows - 1.0 - offsets))[None],
        0.0,
    )
    return within, entering[..., None], leaving[..., None]


def local_any(
    tokens,
    cotangent,
    lengths,
    decay_rate,
    query_weight,
    key_weight,
    value_weight,
    gate_weight,
    out_weight,
    first_weight,
    second_weight,
    down_weight,
):
    wires = Wires()
    mb, chunk, width = tokens.shape
    rows = mb * chunk
    place = wires.f * wires.nh + wires.h
    count = wires.nf * wires.nh

    mix_weights = wires.gather(
        jnp.concatenate([query_weight, key_weight, value_weight, gate_weight], axis=1)
    )
    out_full = wires.gather(out_weight)
    gate_up = wires.gather(jnp.concatenate([first_weight, second_weight], axis=1))
    down_t = wires.gather(down_weight.T)
    hidden_size = down_t.shape[1]

    positions = place * chunk + jnp.arange(chunk, dtype=jnp.int32)
    cosine, sine_vals = rotation_tables(positions, DH)
    cosine, sine_vals = jnp.tile(cosine, (mb, 1, 1)), jnp.tile(sine_vals, (mb, 1, 1))
    seq_ends = jnp.cumsum(lengths, axis=1)
    segs = jnp.sum((seq_ends[:, None, :] <= positions[None, :, None]).astype(jnp.int32), axis=2)
    marks = (jnp.arange(count, dtype=jnp.int32) + 1) * chunk - 1
    ends = jnp.sum((seq_ends[:, None, :] <= marks[None, :, None]).astype(jnp.int32), axis=2)
    last = lax.dynamic_index_in_dim(ends, place, 1, False)
    before = jnp.where(
        place > 0, lax.dynamic_index_in_dim(ends, jnp.maximum(place - 1, 0), 1, False), 0
    )
    within, entering, leaving = masks(segs, before, last, decay_rate)

    def heads(values):
        return values.reshape(mb, chunk, H, DH).transpose(0, 2, 1, 3)

    def flat(values):
        return values.transpose(0, 2, 1, 3).reshape(rows, H * DH)

    def mm(spec, a, b):
        return jnp.einsum(spec, a.astype(BF16), b.astype(BF16), preferred_element_type=F32)

    inputs = tokens.reshape(rows, width).astype(F32)
    normed_in, scale_in = norm_parts(inputs)
    act_rel = wires.rel(normed_in.astype(BF16))
    mixed_pre = dot(act_rel, mix_weights)
    query_pre = mixed_pre[:, :width]
    key_pre = mixed_pre[:, width : 2 * width]
    value_low = mixed_pre[:, 2 * width : 3 * width].astype(BF16)
    gate_vals = mixed_pre[:, 3 * width :]

    def turned(values):
        return rotate_pairs(jax.nn.silu(values).reshape(rows, H, DH), cosine, sine_vals).astype(BF16)

    query_h = heads(turned(query_pre))
    key_h = heads(turned(key_pre))
    value_h = heads(value_low)
    local_state = mm("mhtd,mhte->mhde", key_h * leaving, value_h)
    state_in = chain(wires, local_state, ends, decay_rate, chunk, False)
    scores = (mm("mhsd,mhtd->mhst", query_h, key_h) * within).astype(BF16)
    attended = mm("mhst,mhte->mhse", scores, value_h)
    attended = attended + entering * mm("mhsd,mhde->mhse", query_h, state_in)
    attended = flat(attended.astype(BF16))

    normed_att, scale_att = norm_parts(attended.astype(F32))
    gated_rel = wires.rel((normed_att * gate_vals).astype(BF16))
    hidden = inputs + dot(gated_rel, out_full)
    normed_mid, scale_mid = norm_parts(hidden)
    mid_rel = wires.rel(normed_mid.astype(BF16))
    pre = dot(mid_rel, gate_up)
    first_pre, second_pre = pre[:, :hidden_size], pre[:, hidden_size:]
    product = (first_pre * second_pre).astype(BF16)
    mixed = (hidden + wires.rel(dot_cols(product, down_t))).astype(BF16)

    grad_low = cotangent.reshape(rows, width)
    grad_rel = wires.rel(grad_low)
    share_down = wires.reduce(dot_rows(grad_rel, product)).T
    grad_prod = dot(grad_rel, down_t)
    grad_pre = jnp.concatenate(
        [(grad_prod * second_pre).astype(BF16), (grad_prod * first_pre).astype(BF16)], axis=1
    )
    share_up = wires.reduce(dot_rows(mid_rel, grad_pre))
    grad_mid = wires.rel(dot_cols(grad_pre, gate_up))
    grad_hidden = grad_low.astype(F32) + norm_back(grad_mid, normed_mid, scale_mid)
    grad_hidden_low = grad_hidden.astype(BF16)
    share_out = wires.reduce(dot_rows(gated_rel, grad_hidden_low))
    grad_gated = wires.rel(dot_cols(grad_hidden_low, out_full))
    grad_gate_low = (grad_gated * normed_att).astype(BF16)
    grad_att = heads(norm_back(grad_gated * gate_vals, normed_att, scale_att).astype(BF16))

    grad_state = mm("mhsd,mhse->mhde", query_h * entering, grad_att)
    grad_end = chain(wires, grad_state, ends, decay_rate, chunk, True)
    grad_scores = (mm("mhse,mhte->mhst", grad_att, value_h) * within).astype(BF16)
    grad_q = mm("mhst,mhtd->mhsd", grad_scores, key_h)
    grad_q = grad_q + entering * mm("mhse,mhde->mhsd", grad_att, state_in)
    grad_k = mm("mhst,mhsd->mhtd", grad_scores, query_h)
    grad_k = grad_k + leaving * mm("mhte,mhde->mhtd", value_h, grad_end)
    grad_v = mm("mhst,mhse->mhte", scores, grad_att)
    grad_v = grad_v + leaving * mm("mhtd,mhde->mhte", key_h, grad_end)

    def turned_back(values, pre_values):
        back = flat(values.astype(BF16)).astype(F32).reshape(rows, H, DH)
        back = rotate_pairs(back, cosine, -sine_vals).reshape(rows, width)
        return (silu_slope(pre_values) * back).astype(BF16)

    grad_mix = jnp.concatenate(
        [
            turned_back(grad_q, query_pre),
            turned_back(grad_k, key_pre),
            flat(grad_v.astype(BF16)),
            grad_gate_low,
        ],
        axis=1,
    )
    share_mix = wires.reduce(dot_rows(act_rel, grad_mix))
    grad_act = wires.rel(dot_cols(grad_mix, mix_weights))
    grad_tokens = (grad_hidden + norm_back(grad_act, normed_in, scale_in)).astype(BF16)
    return (
        mixed.reshape(mb, chunk, width),
        grad_tokens.reshape(mb, chunk, width),
        share_mix[:, :width],
        share_mix[:, width : 2 * width],
        share_mix[:, 2 * width : 3 * width],
        share_mix[:, 3 * width :],
        share_out,
        share_up[:, :hidden_size],
        share_up[:, hidden_size:],
        share_down,
    )


def flip(index, bit):
    return index + bit - 2 * bit * ((index // bit) % 2)


def kdot(a, b, dims=((1,), (0,))):
    return lax.dot_general(a, b, (dims, ((), ())), preferred_element_type=F32)


def cols(start, size):
    return pl.ds(pl.multiple_of(start, 128), size)


class Place:
    def __init__(self):
        self.f = lax.axis_index("fsdp")
        self.z = lax.axis_index("head")
        self.fc, self.fx, self.fy = (flip(self.f, b) for b in (1, 2, 4))
        self.fxy = flip(self.fx, 4)
        self.zs = [flip(self.z, 1), flip(self.z, 2), flip(flip(self.z, 1), 2)]

    def at(self, f=None, z=None):
        return {"fsdp": self.f if f is None else f, "head": self.z if z is None else z}

    def greet(self):
        barrier = pltpu.get_barrier_semaphore()
        others = [self.at(f=f) for f in (self.fc, self.fx, self.fy, self.fxy)]
        others += [self.at(z=z) for z in self.zs]
        for other in others:
            pl.semaphore_signal(barrier, inc=1, device_id=other, device_id_type=MESH)
        pl.semaphore_wait(barrier, len(others))


class Scan:
    def __init__(self, place, table, base, states, inbox, totals, outbox, result, send, recv):
        self.p, self.table, self.base = place, table, base
        self.states, self.inbox, self.totals = states, inbox, totals
        self.outbox, self.result = outbox, result
        self.send, self.recv = send, recv

    def copy(self, src, dst, n, where):
        return pltpu.make_async_remote_copy(
            src_ref=src,
            dst_ref=dst,
            send_sem=self.send.at[n],
            recv_sem=self.recv.at[n],
            device_id=where,
            device_id_type=MESH,
        )

    def to_heads(self, i):
        z = self.p.zs[i]
        return self.copy(self.states.at[pl.ds(2 * z, 2)], self.inbox.at[self.p.z], i, self.p.at(z=z))

    def from_heads(self, i):
        z = self.p.zs[i]
        return self.copy(
            self.outbox.at[z], self.result.at[pl.ds(2 * self.p.z, 2)], 9 + i, self.p.at(z=z)
        )

    def total(self, n, origin, where):
        return self.copy(self.totals.at[origin], self.totals.at[origin], n, self.p.at(f=where))

    def start(self):
        p = self.p
        for i in range(3):
            self.to_heads(i).start()
        self.inbox[p.z] = self.states[pl.ds(2 * p.z, 2)]

    def factor(self, offset):
        return self.table[self.base + offset]

    def totals_out(self):
        p = self.p
        for i in range(3):
            self.to_heads(i).wait()
        for hh in range(2):
            for m in range(2):
                acc = self.factor((m * 4) * 2 + hh) * self.inbox[0, hh, m].astype(F32)
                for i in range(1, 4):
                    acc += self.factor((m * 4 + i) * 2 + hh) * self.inbox[i, hh, m].astype(F32)
                self.totals[p.f, hh, m] = acc.astype(BF16)
        for n, where in ((3, p.fx), (4, p.fy), (5, p.fxy)):
            self.total(n, p.f, where).start()
        self.total(12, p.f, p.fc).start()

    def forward(self):
        p = self.p
        for n, where in ((3, p.fx), (4, p.fy), (5, p.fxy)):
            self.total(n, p.f, where).wait()
            self.total(n + 3, where, p.fc).start()

    def results_out(self):
        p = self.p
        self.total(12, p.f, p.fc).wait()
        for n, where in ((3, p.fx), (4, p.fy), (5, p.fxy)):
            self.total(n + 3, where, p.fc).wait()
        for hh in range(2):
            for m in range(2):
                outer = self.factor(16 + (m * 8) * 2 + hh) * self.totals[0, hh, m].astype(F32)
                for g in range(1, 8):
                    outer += self.factor(16 + (m * 8 + g) * 2 + hh) * self.totals[
                        g, hh, m
                    ].astype(F32)
                for i in range(4):
                    acc = self.factor(48 + (m * 4 + i) * 2 + hh) * outer
                    for j in range(4):
                        if i != j:
                            acc += self.factor(64 + ((m * 4 + i) * 4 + j) * 2 + hh) * self.inbox[
                                j, hh, m
                            ].astype(F32)
                    self.outbox[i, hh, m] = acc.astype(BF16)
        for i in range(3):
            self.from_heads(i).start()
        self.result[pl.ds(2 * p.z, 2)] = self.outbox[p.z]

    def finish(self):
        for i in range(3):
            self.from_heads(i).wait()


def edge(seg, mark, rate, gap):
    return jnp.where(seg == mark, jnp.exp(-rate * gap), 0.0)


def decays(rate, rows):
    up = lax.broadcasted_iota(jnp.int32, (rows, rows), 0)
    across = lax.broadcasted_iota(jnp.int32, (rows, rows), 1)
    gap = (up - across).astype(F32)
    return jnp.where(gap >= 0.0, jnp.exp(-rate * jnp.maximum(gap, 0.0)), 0.0)


def forward_kernel(
    table, marks, x, cosine, sine, seg_col, seg_row,
    wq, wk, wv, wu, wo, w1, w2, wd,
    mix_o, wo_o, w1_o, w2_o, wd_o, q_o, k_o, v_o, u_o, qp_o, kp_o, ob_o, hid_o, p1_o, p2_o, s_o,
    state_o, mixed_o,
    fm, fo, f1, f2, fd, a1, q, k, v, u, qp, kp, att, ob, g, hid, p1, p2, s, mixed,
    states, inbox, totals, outbox, result,
    send, recv, own_sem, save_sem, scan_send, scan_recv,
):
    place = Place()
    f = place.f
    rows, width = x.shape
    chunk = rows // 2
    hidden_size = w1.shape[1]
    half_hidden = hidden_size // 2
    place.greet()

    pieces = []
    for i, w in enumerate((wq, wk, wv, wu)):
        pieces.append((w, fm, (0, 128), (0, width), (0, i * width)))
    pieces.append((wo, fo, (0, 128), (0, width), (0, 0)))
    for part in range(2):
        for w, full in ((w1, f1), (w2, f2)):
            pieces.append((w, full, (0, 128), (part * half_hidden, half_hidden), (0, part * half_hidden)))
    for part in range(2):
        pieces.append((wd, fd, (part * half_hidden, half_hidden), (0, 128), None))
    count = len(pieces)

    def own(n):
        w, _, (r, rs), (c, cs), _ = pieces[n]
        return w.at[pl.ds(r, rs), pl.ds(c, cs)]

    def block(n, origin, half=None):
        _, full, (r, rs), (c, cs), to = pieces[n]
        if to is None:
            start, size, at, wide = r, rs, origin * 128, 128
            if half is not None:
                start, size = r + half * (rs // 2), rs // 2
            return full.at[pl.ds(start, size), cols(at, wide)]
        start, size = origin * 128, 128
        if half is not None:
            start, size = start + half * 64, 64
        return full.at[pl.ds(pl.multiple_of(start, 64), size), pl.ds(to[1], cs)]

    def move(n, step, src, dst, where):
        return pltpu.make_async_remote_copy(
            src_ref=src,
            dst_ref=dst,
            send_sem=send.at[n * 8 + step],
            recv_sem=recv.at[n * 8 + step],
            device_id=place.at(f=where),
            device_id_type=MESH,
        )

    fc, fx, fy, fxy = place.fc, place.fx, place.fy, place.fxy

    def steps(n):
        return [
            (own(n), block(n, f), fc, block(n, fc)),
            (own(n), block(n, f), fx, block(n, fx)),
            (own(n), block(n, f), fy, block(n, fy)),
            (block(n, fx, 0), block(n, fx, 0), fy, block(n, fxy, 0)),
            (block(n, fy, 1), block(n, fy, 1), fx, block(n, fxy, 1)),
            (block(n, fx), block(n, fx), fc, block(n, flip(fx, 1))),
            (block(n, fy), block(n, fy), fc, block(n, flip(fy, 1))),
            (block(n, fxy), block(n, fxy), fc, block(n, flip(fxy, 1))),
        ]

    def go(n, step):
        src, dst, where, _ = steps(n)[step]
        move(n, step, src, dst, where).start()

    def got(n, step):
        _, _, where, dst = steps(n)[step]
        move(n, step, dst, dst, where).wait_recv()

    def own_copy(n):
        return pltpu.make_async_copy(own(n), block(n, f), own_sem.at[n])

    saves = []

    def save(src, dst):
        copy = pltpu.make_async_copy(src, dst, save_sem.at[len(saves)])
        copy.start()
        saves.append(copy)

    def save_piece(n):
        full_o = {id(fm): mix_o, id(fo): wo_o, id(f1): w1_o, id(f2): w2_o, id(fd): wd_o}
        _, full, (r, rs), (c, cs), to = pieces[n]
        out = full_o[id(full)]
        if to is None:
            save(full.at[pl.ds(r, rs)], out.at[pl.ds(r, rs)])
        else:
            save(full.at[:, pl.ds(to[1], cs)], out.at[:, pl.ds(to[1], cs)])

    def norm_in():
        @pl.loop(0, rows // 128)
        def _(t):
            at = pl.ds(pl.multiple_of(t * 128, 128), 128)
            value = x[at, :].astype(F32)
            scale = lax.rsqrt(jnp.mean(value * value, axis=-1, keepdims=True) + EPSILON)
            a1[at, :] = (value * scale).astype(BF16)

    def project(base, pre, low, turn):
        @pl.loop(0, width // TILE)
        def _(t):
            at = cols(t * TILE, TILE)
            acc = kdot(a1[...], fm[:, cols(base + t * TILE, TILE)])
            if not turn:
                low[:, at] = acc.astype(BF16)
                return
            pre[:, at] = acc.astype(BF16)
            acc = acc * lax.logistic(acc)
            turned = []
            for hh in range(TILE // DH):
                piece = acc[:, hh * DH : (hh + 1) * DH]
                turned.append(piece * cosine[...] + pltpu.roll(piece, DH // 2, 1) * sine[...])
            low[:, at] = jnp.concatenate(turned, axis=1).astype(BF16)

    offset = lax.broadcasted_iota(jnp.int32, (chunk, 1), 0).astype(F32)
    scan = Scan(
        place, table, 8, states, inbox, totals, outbox, result, scan_send, scan_recv
    )

    def local_states():
        @pl.loop(0, H)
        def _(h):
            at = cols(h * DH, DH)
            for m in range(2):
                r = slice(m * chunk, (m + 1) * chunk)
                leaving = edge(seg_col[r], marks[2 + m], table[h], chunk - 1.0 - offset)
                left = (k[r, at].astype(F32) * leaving).astype(BF16)
                states[h, m] = kdot(left, v[r, at], ((0,), (0,))).astype(BF16)

    def attend_local():
        @pl.loop(0, H)
        def _(h):
            at = cols(h * DH, DH)
            decay = decays(table[h], chunk)
            for m in range(2):
                r = slice(m * chunk, (m + 1) * chunk)
                within = jnp.where(seg_col[r] == seg_row[m : m + 1], decay, 0.0)
                scores = kdot(q[r, at], k[r, at], ((1,), (1,))) * within
                att[r, at] = kdot(scores.astype(BF16), v[r, at])

    def attend_rest():
        @pl.loop(0, H)
        def _(h):
            at = cols(h * DH, DH)
            for m in range(2):
                r = slice(m * chunk, (m + 1) * chunk)
                entering = edge(seg_col[r], marks[m], table[h], offset + 1.0)
                ob[r, at] = (att[r, at] + entering * kdot(q[r, at], result[h, m])).astype(BF16)

    def hidden():
        @pl.loop(0, rows // 128)
        def _(t):
            at = pl.ds(pl.multiple_of(t * 128, 128), 128)
            value = ob[at, :].astype(F32)
            scale = lax.rsqrt(jnp.mean(value * value, axis=-1, keepdims=True) + EPSILON)
            g[at, :] = (value * scale * u[at, :].astype(F32)).astype(BF16)

        @pl.loop(0, width // TILE)
        def _(t):
            at = cols(t * TILE, TILE)
            hid[:, at] = x[:, at].astype(F32) + kdot(g[...], fo[:, at])

        @pl.loop(0, rows // 128)
        def _(t):
            at = pl.ds(pl.multiple_of(t * 128, 128), 128)
            value = hid[at, :]
            scale = lax.rsqrt(jnp.mean(value * value, axis=-1, keepdims=True) + EPSILON)
            g[at, :] = (value * scale).astype(BF16)

    def up():
        @pl.loop(0, hidden_size // TILE)
        def _(t):
            at = cols(t * TILE, TILE)
            first = kdot(g[...], f1[:, at])
            second = kdot(g[...], f2[:, at])
            p1[:, at] = first.astype(BF16)
            p2[:, at] = second.astype(BF16)
            s[:, at] = (first * second).astype(BF16)

    def down():
        @pl.loop(0, width // TILE)
        def _(t):
            at = cols(t * TILE, TILE)
            mixed[:, at] = (hid[:, at] + kdot(s[...], fd[:, at])).astype(BF16)

    def work(n):
        if n == 0:
            project(0, qp, q, True)
            save(q, q_o)
            save(qp, qp_o)
        elif n == 1:
            project(width, kp, k, True)
            save(k, k_o)
            save(kp, kp_o)
        elif n == 2:
            project(2 * width, None, v, False)
            local_states()
            scan.start()
            save(v, v_o)
        elif n == 3:
            project(3 * width, None, u, False)
            save(u, u_o)
            scan.totals_out()
        elif n == 4:
            attend_local()
            scan.forward()
        elif n == 5:
            scan.results_out()
        elif n == 6:
            scan.finish()
            save(result, state_o)
            attend_rest()
            save(ob, ob_o)
            hidden()
            save(hid, hid_o)
        elif n == 8:
            up()
            save(p1, p1_o)
            save(p2, p2_o)
            save(s, s_o)
        elif n == 10:
            down()
            save(mixed, mixed_o)

    for n in range(2):
        for step in (1, 2, 0):
            go(n, step)
        own_copy(n).start()
    norm_in()
    for n in range(count + 2):
        if n < count:
            got(n, 1)
            go(n, 3)
            go(n, 5)
            got(n, 2)
            go(n, 4)
            go(n, 6)
            if n + 2 < count:
                for step in (1, 2, 0):
                    go(n + 2, step)
                own_copy(n + 2).start()
        if 0 <= n - 1 < count:
            got(n - 1, 3)
            got(n - 1, 4)
            go(n - 1, 7)
        if n - 2 >= 0:
            for step in (0, 5, 6, 7):
                got(n - 2, step)
            own_copy(n - 2).wait()
            save_piece(n - 2)
            work(n - 2)
    for n in range(count):
        for step in range(8):
            src, dst, where, _ = steps(n)[step]
            move(n, step, src, dst, where).wait_send()
    for copy in saves:
        copy.wait()


def run_forward(table, marks, x, cosine, sine, seg_col, seg_row, weights):
    rows, width = x.shape
    hidden_size = weights[5].shape[1]
    row = jax.ShapeDtypeStruct((rows, width), BF16)
    tall = jax.ShapeDtypeStruct((rows, hidden_size), BF16)
    outs = (
        [
            jax.ShapeDtypeStruct(shape, BF16)
            for shape in (
                (width, 4 * width), (width, width), (width, hidden_size), (width, hidden_size),
                (hidden_size, width),
            )
        ]
        + [row] * 7
        + [jax.ShapeDtypeStruct((rows, width), F32)]
        + [tall] * 3
        + [jax.ShapeDtypeStruct((H, 2, DH, DH), BF16), row]
    )
    rv = pltpu.VMEM((rows, width), BF16)
    tv = pltpu.VMEM((rows, hidden_size), BF16)
    scratch = (
        [pltpu.VMEM(o.shape, BF16) for o in outs[:5]]
        + [rv] * 7
        + [pltpu.VMEM((rows, width), F32), rv, rv, pltpu.VMEM((rows, width), F32)]
        + [tv] * 3
        + [rv]
        + scan_scratch()
        + [pltpu.SemaphoreType.DMA((88,))] * 2
        + [pltpu.SemaphoreType.DMA((11,)), pltpu.SemaphoreType.DMA((24,))]
        + [pltpu.SemaphoreType.DMA((13,))] * 2
    )
    return pl.pallas_call(
        forward_kernel,
        out_shape=outs,
        in_specs=[SMEM, SMEM] + [VMEM] * 5 + [ANY] * 8,
        out_specs=[ANY] * len(outs),
        scratch_shapes=scratch,
        compiler_params=pltpu.CompilerParams(
            collective_id=0, has_side_effects=True, vmem_limit_bytes=VMEM_BYTES
        ),
        name="forward",
    )(table, marks, x, cosine, sine, seg_col, seg_row, *weights)


def scan_scratch():
    return [
        pltpu.VMEM((H, 2, DH, DH), BF16),
        pltpu.VMEM((4, 2, 2, DH, DH), BF16),
        pltpu.VMEM((8, 2, 2, DH, DH), BF16),
        pltpu.VMEM((4, 2, 2, DH, DH), BF16),
        pltpu.VMEM((H, 2, DH, DH), BF16),
    ]


def factors(ends, rates, chunk, f, nf, nh, backward):
    mb = ends.shape[0]
    places = jnp.arange(nh)
    groups = jnp.arange(nf)
    at_group = lax.dynamic_slice_in_dim(ends, f * nh, nh, axis=1)
    before_group = jnp.where(
        f > 0, lax.dynamic_index_in_dim(ends, jnp.maximum(f * nh - 1, 0), 1, False), 0
    )
    before = jnp.concatenate([before_group[:, None], at_group[:, :-1]], axis=1)
    last = at_group[:, -1]
    group_last = ends.reshape(mb, nf, nh)[:, :, -1]
    group_before = jnp.concatenate([jnp.zeros_like(group_last[:, :1]), group_last[:, :-1]], axis=1)

    def factor(same, gap):
        gap = jnp.maximum(gap, 0)
        value = jnp.exp(-rates * (chunk * gap).astype(F32)[..., None])
        return jnp.where(same[..., None], value, 0.0).reshape(-1)

    rise = jnp.broadcast_to(places, (mb, nh))
    fall = jnp.broadcast_to(nh - 1 - places, (mb, nh))
    if backward:
        to_total = factor(before == before_group[:, None], rise)
        group_same = (last[:, None] == group_before) & (groups > f)
        group_gap = jnp.broadcast_to((groups - 1 - f) * nh, (mb, nf))
        to_place = factor(at_group == last[:, None], fall)
        same = (at_group[:, :, None] == before[:, None, :]) & (places[None, :] > places[:, None])
        gap = jnp.broadcast_to(places[None, :] - 1 - places[:, None], (mb, nh, nh))
    else:
        to_total = factor(at_group == last[:, None], fall)
        group_same = (before_group[:, None] == group_last) & (groups < f)
        group_gap = jnp.broadcast_to((f - 1 - groups) * nh, (mb, nf))
        to_place = factor(before == before_group[:, None], rise)
        same = (before[:, :, None] == at_group[:, None, :]) & (places[None, :] < places[:, None])
        gap = jnp.broadcast_to(places[:, None] - 1 - places[None, :], (mb, nh, nh))
    return jnp.concatenate([to_total, factor(group_same, group_gap), to_place, factor(same, gap)])


def local_fast(tokens, cotangent, lengths, decay_rate, *weights):
    wires = Wires()
    mb, chunk, width = tokens.shape
    rows = mb * chunk
    nf, nh = wires.nf, wires.nh
    place = wires.f * nh + wires.h
    positions = place * chunk + jnp.arange(chunk, dtype=jnp.int32)
    cosine, sine_vals = rotation_tables(positions, DH)
    cosine, sine_vals = cosine[:, 0], sine_vals[:, 0]
    cos_table = jnp.tile(cosine, (mb, 2))
    sin_table = jnp.tile(jnp.concatenate([-sine_vals, sine_vals], axis=1), (mb, 1))
    seq_ends = jnp.cumsum(lengths, axis=1)
    segs = jnp.sum((seq_ends[:, None, :] <= positions[None, :, None]).astype(jnp.int32), axis=2)
    chunk_ends = (jnp.arange(nf * nh, dtype=jnp.int32) + 1) * chunk - 1
    ends = jnp.sum((seq_ends[:, None, :] <= chunk_ends[None, :, None]).astype(jnp.int32), axis=2)
    last = lax.dynamic_index_in_dim(ends, place, 1, False)
    before = jnp.where(
        place > 0, lax.dynamic_index_in_dim(ends, jnp.maximum(place - 1, 0), 1, False), 0
    )
    marks = jnp.concatenate([before, last])
    mine = H // nh
    rates = lax.dynamic_slice_in_dim(decay_rate, wires.h * mine, mine)
    table = jnp.concatenate([decay_rate, factors(ends, rates, chunk, wires.f, nf, nh, False)])
    x = tokens.reshape(rows, width)
    seg_col = segs.reshape(rows, 1)
    outs = run_forward(table, marks, x, cos_table, sin_table, seg_col, segs, weights)
    (mix_weights, out_full, first_full, second_full, down_full) = outs[:5]
    (q, k, v, u, query_pre, key_pre, attended, hidden, p1, p2, product, state_in, mixed) = outs[5:]

    within, entering, leaving = masks(segs, before, last, decay_rate)
    cosine = jnp.tile(cosine[:, None], (mb, 1, 1))
    sine_vals = jnp.tile(sine_vals[:, None], (mb, 1, 1))

    def heads(values):
        return values.reshape(mb, chunk, H, DH).transpose(0, 2, 1, 3)

    def flat(values):
        return values.transpose(0, 2, 1, 3).reshape(rows, H * DH)

    def mm(spec, a, b):
        return jnp.einsum(spec, a.astype(BF16), b.astype(BF16), preferred_element_type=F32)

    query_h, key_h, value_h = heads(q), heads(k), heads(v)
    state_in = state_in.transpose(1, 0, 2, 3)
    gate_vals = u.astype(F32)
    query_pre, key_pre = query_pre.astype(F32), key_pre.astype(F32)
    first_pre, second_pre = p1.astype(F32), p2.astype(F32)
    normed_in, scale_in = norm_parts(x.astype(F32))
    act_rel = wires.rel(normed_in.astype(BF16))
    normed_att, scale_att = norm_parts(attended.astype(F32))
    gated_rel = wires.rel((normed_att * gate_vals).astype(BF16))
    normed_mid, scale_mid = norm_parts(hidden)
    mid_rel = wires.rel(normed_mid.astype(BF16))
    scores = (mm("mhsd,mhtd->mhst", query_h, key_h) * within).astype(BF16)

    grad_low = cotangent.reshape(rows, width)
    share_down = wires.reduce(dot_rows(wires.rel(grad_low), product)).T
    grad_prod = dot_cols(grad_low, down_full)
    grad_p1 = (grad_prod * second_pre).astype(BF16)
    grad_p2 = (grad_prod * first_pre).astype(BF16)
    share_first = wires.reduce(dot_rows(mid_rel, grad_p1))
    share_second = wires.reduce(dot_rows(mid_rel, grad_p2))
    grad_mid = dot_cols(grad_p1, first_full) + dot_cols(grad_p2, second_full)
    grad_hidden = grad_low.astype(F32) + norm_back(grad_mid, normed_mid, scale_mid)
    grad_hidden_low = grad_hidden.astype(BF16)
    share_out = wires.reduce(dot_rows(gated_rel, grad_hidden_low))
    grad_gated = dot_cols(grad_hidden_low, out_full)
    grad_gate_low = (grad_gated * normed_att).astype(BF16)
    grad_att = heads(norm_back(grad_gated * gate_vals, normed_att, scale_att).astype(BF16))
    grad_state = mm("mhsd,mhse->mhde", query_h * entering, grad_att)
    grad_end = chain(wires, grad_state, ends, decay_rate, chunk, True)
    grad_scores = (mm("mhse,mhte->mhst", grad_att, value_h) * within).astype(BF16)
    grad_q = mm("mhst,mhtd->mhsd", grad_scores, key_h)
    grad_q = grad_q + entering * mm("mhse,mhde->mhsd", grad_att, state_in)
    grad_k = mm("mhst,mhsd->mhtd", grad_scores, query_h)
    grad_k = grad_k + leaving * mm("mhte,mhde->mhtd", value_h, grad_end)
    grad_v = mm("mhst,mhse->mhte", scores, grad_att)
    grad_v = grad_v + leaving * mm("mhtd,mhde->mhte", key_h, grad_end)

    def turned_back(values, pre_values):
        back = flat(values.astype(BF16)).astype(F32).reshape(rows, H, DH)
        back = rotate_pairs(back, cosine, -sine_vals).reshape(rows, width)
        return (silu_slope(pre_values) * back).astype(BF16)

    grad_mix = jnp.concatenate(
        [
            turned_back(grad_q, query_pre),
            turned_back(grad_k, key_pre),
            flat(grad_v.astype(BF16)),
            grad_gate_low,
        ],
        axis=1,
    )
    share_mix = wires.reduce(dot_rows(act_rel, grad_mix))
    grad_act = dot_cols(grad_mix, mix_weights)
    grad_tokens = (grad_hidden + norm_back(grad_act, normed_in, scale_in)).astype(BF16)
    return (
        mixed.reshape(mb, chunk, width),
        grad_tokens.reshape(mb, chunk, width),
        share_mix[:, :width],
        share_mix[:, width : 2 * width],
        share_mix[:, 2 * width : 3 * width],
        share_mix[:, 3 * width :],
        share_out,
        share_first,
        share_second,
        share_down,
    )


def solution(mesh):
    rows = P(None, AXES, None)
    in_specs = (rows, rows, P(), P()) + (P("fsdp", None),) * 7 + (P(None, "fsdp"),)
    out_specs = (rows, rows) + (P(AXES, None),) * 7 + (P(None, AXES),)
    fast = mesh.shape["fsdp"] == 8 and mesh.shape["head"] == 4
    local = local_fast if fast else local_any
    return jax.shard_map(local, mesh=mesh, in_specs=in_specs, out_specs=out_specs, check_vma=False)
```

```python
import functools
import math

import jax
import jax.numpy as jnp
from jax import lax
from jax.experimental import pallas as pl
from jax.experimental.pallas import tpu as pltpu
from jax.sharding import PartitionSpec as P

H = 8
DH = 128
EPSILON = 1e-06
AXES = ("fsdp", "head")
F32 = jnp.float32
BF16 = jnp.bfloat16
MESH = pl.DeviceIdType.MESH
ANY = pl.BlockSpec(memory_space=pl.ANY)
VMEM = pl.BlockSpec(memory_space=pltpu.VMEM)
SMEM = pl.BlockSpec(memory_space=pltpu.SMEM)
VMEM_BYTES = 63 * 1024 * 1024
TILE = 256


def norm_parts(values):
    inv_scale = lax.rsqrt(jnp.mean(values * values, axis=-1, keepdims=True) + EPSILON)
    return (values * inv_scale, inv_scale)


def norm_back(gradient, normed, inv_scale):
    return inv_scale * (gradient - normed * jnp.mean(gradient * normed, axis=-1, keepdims=True))


def rotate_pairs(values, cosine, sine_vals):
    half_size = values.shape[-1] // 2
    first_half = values[..., :half_size]
    second_half = values[..., half_size:]
    return jnp.concatenate(
        [
            first_half * cosine - second_half * sine_vals,
            first_half * sine_vals + second_half * cosine,
        ],
        axis=-1,
    )


def rotation_tables(positions, head_size):
    half_size = head_size // 2
    shifts = jnp.arange(half_size, dtype=jnp.int32) * 10 // half_size
    speeds = jnp.right_shift(jnp.full((half_size,), 651, jnp.int32), shifts) + 1
    phases = positions[:, None] * speeds[None, :] % 4096
    angles = phases.astype(F32) * (2.0 * math.pi / 4096.0)
    return (jnp.cos(angles)[:, None, :], jnp.sin(angles)[:, None, :])


def silu_slope(values):
    sigmoid_v = jax.nn.sigmoid(values)
    return sigmoid_v * (1.0 + values * (1.0 - sigmoid_v))


def dot(a, b):
    return jnp.dot(a, b, preferred_element_type=F32)


def dot_rows(a, b):
    return lax.dot_general(a, b, (((0,), (0,)), ((), ())), preferred_element_type=F32)


def dot_cols(a, b):
    return lax.dot_general(a, b, (((1,), (1,)), ((), ())), preferred_element_type=F32)


class Wires:
    def __init__(self):
        self.nf = lax.axis_size("fsdp")
        self.nh = lax.axis_size("head")
        self.fast = self.nf == 8 and self.nh == 4
        self.f = lax.axis_index("fsdp")
        self.h = lax.axis_index("head")

    def swap(self, values, fbits=0, hbits=0):
        pairs = []
        for f in range(self.nf):
            for h in range(self.nh):
                pairs.append((f * self.nh + h, (f ^ fbits) * self.nh + (h ^ hbits)))
        return lax.ppermute(values, AXES, pairs)

    def rel(self, values):
        if not self.fast:
            return values
        width = values.shape[1] // self.nf
        return jnp.concatenate(
            [
                lax.dynamic_slice_in_dim(values, (self.f ^ i) * width, width, 1)
                for i in range(self.nf)
            ],
            axis=1,
        )

    def gather(self, shard):
        if not self.fast:
            return lax.all_gather(shard, "fsdp", axis=0, tiled=True)
        half = shard.shape[1] // 2
        core, x, y = 1, 2, 4
        at_c = self.swap(shard, core)
        at_x = self.swap(shard, x)
        at_y = self.swap(shard, y)
        at_xy = jnp.concatenate(
            [self.swap(at_x[:, :half], y), self.swap(at_y[:, half:], x)], axis=1
        )
        at_cx = self.swap(at_x, core)
        at_cy = self.swap(at_y, core)
        at_cxy = self.swap(at_xy, core)
        return jnp.concatenate([shard, at_c, at_x, at_cx, at_y, at_cy, at_xy, at_cxy], axis=0)

    def reduce(self, grad):
        if not self.fast:
            return lax.psum_scatter(grad, AXES, scatter_dimension=0, tiled=True)
        core, x, y = 1, 2, 4
        rows, n = grad.shape[0] // 8, grad.shape[1]
        low = grad.astype(BF16).reshape(2, 2, 2, rows, n)
        merged = (low[:, :, 0].astype(F32) + self.swap(low[:, :, 1], core).astype(F32)).astype(BF16)
        half = n // 2
        a = merged[:, :, :, :half]
        a = (a[:, 0].astype(F32) + self.swap(a[:, 1], x).astype(F32)).astype(BF16)
        a = (a[0].astype(F32) + self.swap(a[1], y).astype(F32)).astype(BF16)
        b = merged[:, :, :, half:]
        b = (b[0].astype(F32) + self.swap(b[1], y).astype(F32)).astype(BF16)
        b = (b[0].astype(F32) + self.swap(b[1], x).astype(F32)).astype(BF16)
        return jnp.concatenate([self.along(a), self.along(b)], axis=1)

    def along(self, part):
        rows, n = part.shape
        part = part.reshape(2, 2, rows // 4, n)
        low, high = self.h % 2, self.h // 2
        keep = lax.dynamic_index_in_dim(part, low, 1, False)
        send = lax.dynamic_index_in_dim(part, 1 - low, 1, False)
        part = (keep.astype(F32) + self.swap(send, 0, 1).astype(F32)).astype(BF16)
        keep = lax.dynamic_index_in_dim(part, high, 0, False)
        send = lax.dynamic_index_in_dim(part, 1 - high, 0, False)
        return keep.astype(F32) + self.swap(send, 0, 2).astype(F32)

    def to_heads(self, states):
        mb, heads, d, _ = states.shape
        mine = heads // self.nh
        parts = jnp.moveaxis(states.reshape(mb, self.nh, mine, d, d), 1, 0)
        return self.scatter(parts)

    def scatter(self, parts):
        if not self.fast:
            return lax.all_to_all(parts, "head", split_axis=0, concat_axis=0, tiled=True)
        got = [lax.dynamic_index_in_dim(parts, self.h, 0, False)]
        for i in range(1, self.nh):
            got.append(self.swap(lax.dynamic_index_in_dim(parts, self.h ^ i, 0, False), 0, i))
        got = jnp.stack(got)
        order = self.h ^ jnp.arange(self.nh)
        return jnp.take(got, order, axis=0)

    def from_heads(self, parts):
        got = self.scatter(parts)
        nh, mb, mine, d, _ = got.shape
        return jnp.moveaxis(got, 0, 1).reshape(mb, nh * mine, d, d)

    def spread(self, total):
        if not self.fast:
            return lax.all_gather(total, "fsdp")
        core, x, y = 1, 2, 4
        at_c = self.swap(total, core)
        pair = jnp.stack([total, at_c])
        at_x = self.swap(pair, x)
        at_y = self.swap(pair, y)
        at_xy = self.swap(pair, x + y)
        got = jnp.concatenate([pair, at_x, at_y, at_xy])
        return jnp.take(got, self.f ^ jnp.arange(self.nf), axis=0)


def chain(wires, states, ends, decay, chunk, backward):
    nf, nh, f = wires.nf, wires.nh, wires.f
    mb, heads = states.shape[:2]
    mine = heads // nh
    rates = lax.dynamic_slice_in_dim(decay, wires.h * mine, mine)
    places = jnp.arange(nh)
    groups = jnp.arange(nf)
    at_group = lax.dynamic_slice_in_dim(ends, f * nh, nh, axis=1)
    before_group = jnp.where(
        f > 0, lax.dynamic_index_in_dim(ends, jnp.maximum(f * nh - 1, 0), 1, False), 0
    )
    before = jnp.concatenate([before_group[:, None], at_group[:, :-1]], axis=1)
    last = at_group[:, -1]
    group_last = ends.reshape(mb, nf, nh)[:, :, -1]
    group_before = jnp.concatenate([jnp.zeros_like(group_last[:, :1]), group_last[:, :-1]], axis=1)

    def factor(same, gap):
        gap = jnp.maximum(gap, 0)
        return jnp.where(
            same[..., None], jnp.exp(-rates * (chunk * gap).astype(F32)[..., None]), 0.0
        )

    own = wires.to_heads(states.astype(BF16)).astype(F32)
    if backward:
        to_total = factor(before == before_group[:, None], jnp.broadcast_to(places, (mb, nh)))
        group_same = (last[:, None] == group_before) & (groups > f)
        group_gap = jnp.broadcast_to((groups - 1 - f) * nh, (mb, nf))
        to_place = factor(at_group == last[:, None], jnp.broadcast_to(nh - 1 - places, (mb, nh)))
        same = (at_group[:, :, None] == before[:, None, :]) & (places[None, :] > places[:, None])
        gap = jnp.broadcast_to(places[None, :] - 1 - places[:, None], (mb, nh, nh))
    else:
        to_total = factor(at_group == last[:, None], jnp.broadcast_to(nh - 1 - places, (mb, nh)))
        group_same = (before_group[:, None] == group_last) & (groups < f)
        group_gap = jnp.broadcast_to((f - 1 - groups) * nh, (mb, nf))
        to_place = factor(before == before_group[:, None], jnp.broadcast_to(places, (mb, nh)))
        same = (before[:, :, None] == at_group[:, None, :]) & (places[None, :] < places[:, None])
        gap = jnp.broadcast_to(places[:, None] - 1 - places[None, :], (mb, nh, nh))
    total = sum(to_total[:, i, :, None, None] * own[i] for i in range(nh))
    totals = wires.spread(total.astype(BF16)).astype(F32)
    from_group = factor(group_same, group_gap)
    outer = sum(from_group[:, i, :, None, None] * totals[i] for i in range(nf))
    between = factor(same, gap)
    result = [
        to_place[:, i, :, None, None] * outer
        + sum(between[:, i, j, :, None, None] * own[j] for j in range(nh) if i != j)
        for i in range(nh)
    ]
    return wires.from_heads(jnp.stack(result).astype(BF16))


def masks(segs, before, last, decay):
    rows = segs.shape[1]
    offsets = jnp.arange(rows, dtype=F32)
    distance = offsets[:, None] - offsets[None, :]
    visible = (segs[:, :, None] == segs[:, None, :]) & (distance >= 0.0)
    within = jnp.where(
        visible[:, None],
        jnp.exp(-decay[:, None, None] * jnp.maximum(distance, 0.0))[None],
        0.0,
    )
    entering = jnp.where(
        (segs == before[:, None])[:, None, :],
        jnp.exp(-decay[:, None] * (offsets + 1.0))[None],
        0.0,
    )
    leaving = jnp.where(
        (segs == last[:, None])[:, None, :],
        jnp.exp(-decay[:, None] * (rows - 1.0 - offsets))[None],
        0.0,
    )
    return within, entering[..., None], leaving[..., None]


def local_any(
    tokens,
    cotangent,
    lengths,
    decay_rate,
    query_weight,
    key_weight,
    value_weight,
    gate_weight,
    out_weight,
    first_weight,
    second_weight,
    down_weight,
):
    wires = Wires()
    mb, chunk, width = tokens.shape
    rows = mb * chunk
    place = wires.f * wires.nh + wires.h
    count = wires.nf * wires.nh

    mix_weights = wires.gather(
        jnp.concatenate([query_weight, key_weight, value_weight, gate_weight], axis=1)
    )
    out_full = wires.gather(out_weight)
    gate_up = wires.gather(jnp.concatenate([first_weight, second_weight], axis=1))
    down_t = wires.gather(down_weight.T)
    hidden_size = down_t.shape[1]

    positions = place * chunk + jnp.arange(chunk, dtype=jnp.int32)
    cosine, sine_vals = rotation_tables(positions, DH)
    cosine, sine_vals = jnp.tile(cosine, (mb, 1, 1)), jnp.tile(sine_vals, (mb, 1, 1))
    seq_ends = jnp.cumsum(lengths, axis=1)
    segs = jnp.sum((seq_ends[:, None, :] <= positions[None, :, None]).astype(jnp.int32), axis=2)
    marks = (jnp.arange(count, dtype=jnp.int32) + 1) * chunk - 1
    ends = jnp.sum((seq_ends[:, None, :] <= marks[None, :, None]).astype(jnp.int32), axis=2)
    last = lax.dynamic_index_in_dim(ends, place, 1, False)
    before = jnp.where(
        place > 0, lax.dynamic_index_in_dim(ends, jnp.maximum(place - 1, 0), 1, False), 0
    )
    within, entering, leaving = masks(segs, before, last, decay_rate)

    def heads(values):
        return values.reshape(mb, chunk, H, DH).transpose(0, 2, 1, 3)

    def flat(values):
        return values.transpose(0, 2, 1, 3).reshape(rows, H * DH)

    def mm(spec, a, b):
        return jnp.einsum(spec, a.astype(BF16), b.astype(BF16), preferred_element_type=F32)

    inputs = tokens.reshape(rows, width).astype(F32)
    normed_in, scale_in = norm_parts(inputs)
    act_rel = wires.rel(normed_in.astype(BF16))
    mixed_pre = dot(act_rel, mix_weights)
    query_pre = mixed_pre[:, :width]
    key_pre = mixed_pre[:, width : 2 * width]
    value_low = mixed_pre[:, 2 * width : 3 * width].astype(BF16)
    gate_vals = mixed_pre[:, 3 * width :]

    def turned(values):
        return rotate_pairs(jax.nn.silu(values).reshape(rows, H, DH), cosine, sine_vals).astype(BF16)

    query_h = heads(turned(query_pre))
    key_h = heads(turned(key_pre))
    value_h = heads(value_low)
    local_state = mm("mhtd,mhte->mhde", key_h * leaving, value_h)
    state_in = chain(wires, local_state, ends, decay_rate, chunk, False)
    scores = (mm("mhsd,mhtd->mhst", query_h, key_h) * within).astype(BF16)
    attended = mm("mhst,mhte->mhse", scores, value_h)
    attended = attended + entering * mm("mhsd,mhde->mhse", query_h, state_in)
    attended = flat(attended.astype(BF16))

    normed_att, scale_att = norm_parts(attended.astype(F32))
    gated_rel = wires.rel((normed_att * gate_vals).astype(BF16))
    hidden = inputs + dot(gated_rel, out_full)
    normed_mid, scale_mid = norm_parts(hidden)
    mid_rel = wires.rel(normed_mid.astype(BF16))
    pre = dot(mid_rel, gate_up)
    first_pre, second_pre = pre[:, :hidden_size], pre[:, hidden_size:]
    product = (first_pre * second_pre).astype(BF16)
    mixed = (hidden + wires.rel(dot_cols(product, down_t))).astype(BF16)

    grad_low = cotangent.reshape(rows, width)
    grad_rel = wires.rel(grad_low)
    share_down = wires.reduce(dot_rows(grad_rel, product)).T
    grad_prod = dot(grad_rel, down_t)
    grad_pre = jnp.concatenate(
        [(grad_prod * second_pre).astype(BF16), (grad_prod * first_pre).astype(BF16)], axis=1
    )
    share_up = wires.reduce(dot_rows(mid_rel, grad_pre))
    grad_mid = wires.rel(dot_cols(grad_pre, gate_up))
    grad_hidden = grad_low.astype(F32) + norm_back(grad_mid, normed_mid, scale_mid)
    grad_hidden_low = grad_hidden.astype(BF16)
    share_out = wires.reduce(dot_rows(gated_rel, grad_hidden_low))
    grad_gated = wires.rel(dot_cols(grad_hidden_low, out_full))
    grad_gate_low = (grad_gated * normed_att).astype(BF16)
    grad_att = heads(norm_back(grad_gated * gate_vals, normed_att, scale_att).astype(BF16))

    grad_state = mm("mhsd,mhse->mhde", query_h * entering, grad_att)
    grad_end = chain(wires, grad_state, ends, decay_rate, chunk, True)
    grad_scores = (mm("mhse,mhte->mhst", grad_att, value_h) * within).astype(BF16)
    grad_q = mm("mhst,mhtd->mhsd", grad_scores, key_h)
    grad_q = grad_q + entering * mm("mhse,mhde->mhsd", grad_att, state_in)
    grad_k = mm("mhst,mhsd->mhtd", grad_scores, query_h)
    grad_k = grad_k + leaving * mm("mhte,mhde->mhtd", value_h, grad_end)
    grad_v = mm("mhst,mhse->mhte", scores, grad_att)
    grad_v = grad_v + leaving * mm("mhtd,mhde->mhte", key_h, grad_end)

    def turned_back(values, pre_values):
        back = flat(values.astype(BF16)).astype(F32).reshape(rows, H, DH)
        back = rotate_pairs(back, cosine, -sine_vals).reshape(rows, width)
        return (silu_slope(pre_values) * back).astype(BF16)

    grad_mix = jnp.concatenate(
        [
            turned_back(grad_q, query_pre),
            turned_back(grad_k, key_pre),
            flat(grad_v.astype(BF16)),
            grad_gate_low,
        ],
        axis=1,
    )
    share_mix = wires.reduce(dot_rows(act_rel, grad_mix))
    grad_act = wires.rel(dot_cols(grad_mix, mix_weights))
    grad_tokens = (grad_hidden + norm_back(grad_act, normed_in, scale_in)).astype(BF16)
    return (
        mixed.reshape(mb, chunk, width),
        grad_tokens.reshape(mb, chunk, width),
        share_mix[:, :width],
        share_mix[:, width : 2 * width],
        share_mix[:, 2 * width : 3 * width],
        share_mix[:, 3 * width :],
        share_out,
        share_up[:, :hidden_size],
        share_up[:, hidden_size:],
        share_down,
    )


def flip(index, bit):
    return index + bit - 2 * bit * ((index // bit) % 2)


def kdot(a, b, dims=((1,), (0,))):
    return lax.dot_general(a, b, (dims, ((), ())), preferred_element_type=F32)


def cols(start, size):
    return pl.ds(pl.multiple_of(start, 128), size)


class Place:
    def __init__(self):
        self.f = lax.axis_index("fsdp")
        self.z = lax.axis_index("head")
        self.fc, self.fx, self.fy = (flip(self.f, b) for b in (1, 2, 4))
        self.fxy = flip(self.fx, 4)
        self.zs = [flip(self.z, 1), flip(self.z, 2), flip(flip(self.z, 1), 2)]

    def at(self, f=None, z=None):
        return {"fsdp": self.f if f is None else f, "head": self.z if z is None else z}

    def greet(self):
        barrier = pltpu.get_barrier_semaphore()
        others = [self.at(f=f) for f in (self.fc, self.fx, self.fy, self.fxy)]
        others += [self.at(z=z) for z in self.zs]
        for other in others:
            pl.semaphore_signal(barrier, inc=1, device_id=other, device_id_type=MESH)
        pl.semaphore_wait(barrier, len(others))


class Scan:
    def __init__(self, place, table, base, states, inbox, totals, outbox, result, send, recv):
        self.p, self.table, self.base = place, table, base
        self.states, self.inbox, self.totals = states, inbox, totals
        self.outbox, self.result = outbox, result
        self.send, self.recv = send, recv

    def copy(self, src, dst, n, where):
        return pltpu.make_async_remote_copy(
            src_ref=src,
            dst_ref=dst,
            send_sem=self.send.at[n],
            recv_sem=self.recv.at[n],
            device_id=where,
            device_id_type=MESH,
        )

    def to_heads(self, i):
        z = self.p.zs[i]
        return self.copy(self.states.at[pl.ds(2 * z, 2)], self.inbox.at[self.p.z], i, self.p.at(z=z))

    def from_heads(self, i):
        z = self.p.zs[i]
        return self.copy(
            self.outbox.at[z], self.result.at[pl.ds(2 * self.p.z, 2)], 9 + i, self.p.at(z=z)
        )

    def total(self, n, origin, where):
        return self.copy(self.totals.at[origin], self.totals.at[origin], n, self.p.at(f=where))

    def start(self):
        p = self.p
        for i in range(3):
            self.to_heads(i).start()
        self.inbox[p.z] = self.states[pl.ds(2 * p.z, 2)]

    def factor(self, offset):
        return self.table[self.base + offset]

    def totals_out(self):
        p = self.p
        for i in range(3):
            self.to_heads(i).wait()
        for hh in range(2):
            for m in range(2):
                acc = self.factor((m * 4) * 2 + hh) * self.inbox[0, hh, m].astype(F32)
                for i in range(1, 4):
                    acc += self.factor((m * 4 + i) * 2 + hh) * self.inbox[i, hh, m].astype(F32)
                self.totals[p.f, hh, m] = acc.astype(BF16)
        for n, where in ((3, p.fx), (4, p.fy), (5, p.fxy)):
            self.total(n, p.f, where).start()
        self.total(12, p.f, p.fc).start()

    def forward(self):
        p = self.p
        for n, where in ((3, p.fx), (4, p.fy), (5, p.fxy)):
            self.total(n, p.f, where).wait()
            self.total(n + 3, where, p.fc).start()

    def results_out(self):
        p = self.p
        self.total(12, p.f, p.fc).wait()
        for n, where in ((3, p.fx), (4, p.fy), (5, p.fxy)):
            self.total(n + 3, where, p.fc).wait()
        for hh in range(2):
            for m in range(2):
                outer = self.factor(16 + (m * 8) * 2 + hh) * self.totals[0, hh, m].astype(F32)
                for g in range(1, 8):
                    outer += self.factor(16 + (m * 8 + g) * 2 + hh) * self.totals[
                        g, hh, m
                    ].astype(F32)
                for i in range(4):
                    acc = self.factor(48 + (m * 4 + i) * 2 + hh) * outer
                    for j in range(4):
                        if i != j:
                            acc += self.factor(64 + ((m * 4 + i) * 4 + j) * 2 + hh) * self.inbox[
                                j, hh, m
                            ].astype(F32)
                    self.outbox[i, hh, m] = acc.astype(BF16)
        for i in range(3):
            self.from_heads(i).start()
        self.result[pl.ds(2 * p.z, 2)] = self.outbox[p.z]

    def finish(self):
        for i in range(3):
            self.from_heads(i).wait()


def edge(seg, mark, rate, gap):
    return jnp.where(seg == mark, jnp.exp(-rate * gap), 0.0)


def decays(rate, rows):
    up = lax.broadcasted_iota(jnp.int32, (rows, rows), 0)
    across = lax.broadcasted_iota(jnp.int32, (rows, rows), 1)
    gap = (up - across).astype(F32)
    return jnp.where(gap >= 0.0, jnp.exp(-rate * jnp.maximum(gap, 0.0)), 0.0)


def forward_kernel(
    table, marks, x, dy, cosine, sine, seg_col, seg_row,
    wq, wk, wv, wu, wo, w1, w2, wd,
    mix_o, wo_o, w1_o, w2_o, wd_o, q_o, k_o, v_o, u_o, qp_o, kp_o, ob_o, hid_o, p1_o, p2_o, s_o,
    state_o, mixed_o, a1t_o, a2t_o, gt_o, dyt_o,
    fm, fo, f1, f2, fd, a1, q, k, v, u, qp, kp, att, ob, g, hid, p1, p2, s, mixed,
    a1t, a2t, gt, dyt, states, inbox, totals, outbox, result,
    send, recv, own_sem, save_sem, scan_send, scan_recv,
):
    place = Place()
    f = place.f
    rows, width = x.shape
    chunk = rows // 2
    hidden_size = w1.shape[1]
    half_hidden = hidden_size // 2
    place.greet()

    pieces = []
    for i, w in enumerate((wq, wk, wv, wu)):
        pieces.append((w, fm, (0, 128), (0, width), (0, i * width)))
    pieces.append((wo, fo, (0, 128), (0, width), (0, 0)))
    for part in range(2):
        for w, full in ((w1, f1), (w2, f2)):
            pieces.append((w, full, (0, 128), (part * half_hidden, half_hidden), (0, part * half_hidden)))
    for part in range(2):
        pieces.append((wd, fd, (part * half_hidden, half_hidden), (0, 128), None))
    count = len(pieces)

    def own(n):
        w, _, (r, rs), (c, cs), _ = pieces[n]
        return w.at[pl.ds(r, rs), pl.ds(c, cs)]

    def block(n, origin, half=None):
        _, full, (r, rs), (c, cs), to = pieces[n]
        if to is None:
            start, size, at, wide = r, rs, origin * 128, 128
            if half is not None:
                start, size = r + half * (rs // 2), rs // 2
            return full.at[pl.ds(start, size), cols(at, wide)]
        start, size = origin * 128, 128
        if half is not None:
            start, size = start + half * 64, 64
        return full.at[pl.ds(pl.multiple_of(start, 64), size), pl.ds(to[1], cs)]

    def move(n, step, src, dst, where):
        return pltpu.make_async_remote_copy(
            src_ref=src,
            dst_ref=dst,
            send_sem=send.at[n * 8 + step],
            recv_sem=recv.at[n * 8 + step],
            device_id=place.at(f=where),
            device_id_type=MESH,
        )

    fc, fx, fy, fxy = place.fc, place.fx, place.fy, place.fxy

    def steps(n):
        return [
            (own(n), block(n, f), fc, block(n, fc)),
            (own(n), block(n, f), fx, block(n, fx)),
            (own(n), block(n, f), fy, block(n, fy)),
            (block(n, fx, 0), block(n, fx, 0), fy, block(n, fxy, 0)),
            (block(n, fy, 1), block(n, fy, 1), fx, block(n, fxy, 1)),
            (block(n, fx), block(n, fx), fc, block(n, flip(fx, 1))),
            (block(n, fy), block(n, fy), fc, block(n, flip(fy, 1))),
            (block(n, fxy), block(n, fxy), fc, block(n, flip(fxy, 1))),
        ]

    def go(n, step):
        src, dst, where, _ = steps(n)[step]
        move(n, step, src, dst, where).start()

    def got(n, step):
        _, _, where, dst = steps(n)[step]
        move(n, step, dst, dst, where).wait_recv()

    def own_copy(n):
        return pltpu.make_async_copy(own(n), block(n, f), own_sem.at[n])

    saves = []

    def save(src, dst):
        copy = pltpu.make_async_copy(src, dst, save_sem.at[len(saves)])
        copy.start()
        saves.append(copy)

    def save_piece(n):
        full_o = {id(fm): mix_o, id(fo): wo_o, id(f1): w1_o, id(f2): w2_o, id(fd): wd_o}
        _, full, (r, rs), (c, cs), to = pieces[n]
        out = full_o[id(full)]
        if to is None:
            save(full.at[pl.ds(r, rs)], out.at[pl.ds(r, rs)])
        else:
            save(full.at[:, pl.ds(to[1], cs)], out.at[:, pl.ds(to[1], cs)])

    def norm_in():
        @pl.loop(0, rows // 128)
        def _(t):
            at = pl.ds(pl.multiple_of(t * 128, 128), 128)
            value = x[at, :].astype(F32)
            scale = lax.rsqrt(jnp.mean(value * value, axis=-1, keepdims=True) + EPSILON)
            a1[at, :] = (value * scale).astype(BF16)

    def turn_over(src, dst):
        @pl.loop(0, width // 128)
        def _(b):
            other_c = (b + f) % 2
            other_x = (b // 2 + f // 2) % 2
            other_y = (b // 4 + f // 4) % 2
            slot = other_c * 4 + other_y * 2 + other_x
            value = src[:, cols(b * 128, 128)].astype(F32)
            dst[pl.ds(pl.multiple_of(slot * 128, 128), 128), :] = value.T.astype(BF16)

    def project(base, pre, low, turn):
        @pl.loop(0, width // TILE)
        def _(t):
            at = cols(t * TILE, TILE)
            acc = kdot(a1[...], fm[:, cols(base + t * TILE, TILE)])
            if not turn:
                low[:, at] = acc.astype(BF16)
                return
            pre[:, at] = acc.astype(BF16)
            acc = acc * lax.logistic(acc)
            turned = []
            for hh in range(TILE // DH):
                piece = acc[:, hh * DH : (hh + 1) * DH]
                turned.append(piece * cosine[...] + pltpu.roll(piece, DH // 2, 1) * sine[...])
            low[:, at] = jnp.concatenate(turned, axis=1).astype(BF16)

    offset = lax.broadcasted_iota(jnp.int32, (chunk, 1), 0).astype(F32)
    scan = Scan(
        place, table, 8, states, inbox, totals, outbox, result, scan_send, scan_recv
    )

    def local_states():
        @pl.loop(0, H)
        def _(h):
            at = cols(h * DH, DH)
            for m in range(2):
                r = slice(m * chunk, (m + 1) * chunk)
                leaving = edge(seg_col[r], marks[2 + m], table[h], chunk - 1.0 - offset)
                left = (k[r, at].astype(F32) * leaving).astype(BF16)
                states[h, m] = kdot(left, v[r, at], ((0,), (0,))).astype(BF16)

    def attend_local():
        @pl.loop(0, H)
        def _(h):
            at = cols(h * DH, DH)
            decay = decays(table[h], chunk)
            for m in range(2):
                r = slice(m * chunk, (m + 1) * chunk)
                within = jnp.where(seg_col[r] == seg_row[m : m + 1], decay, 0.0)
                scores = kdot(q[r, at], k[r, at], ((1,), (1,))) * within
                att[r, at] = kdot(scores.astype(BF16), v[r, at])

    def attend_rest():
        @pl.loop(0, H)
        def _(h):
            at = cols(h * DH, DH)
            for m in range(2):
                r = slice(m * chunk, (m + 1) * chunk)
                entering = edge(seg_col[r], marks[m], table[h], offset + 1.0)
                ob[r, at] = (att[r, at] + entering * kdot(q[r, at], result[h, m])).astype(BF16)

    def hidden():
        @pl.loop(0, rows // 128)
        def _(t):
            at = pl.ds(pl.multiple_of(t * 128, 128), 128)
            value = ob[at, :].astype(F32)
            scale = lax.rsqrt(jnp.mean(value * value, axis=-1, keepdims=True) + EPSILON)
            g[at, :] = (value * scale * u[at, :].astype(F32)).astype(BF16)

        turn_over(g, gt)
        save(gt, gt_o)

        @pl.loop(0, width // TILE)
        def _(t):
            at = cols(t * TILE, TILE)
            hid[:, at] = x[:, at].astype(F32) + kdot(g[...], fo[:, at])

        @pl.loop(0, rows // 128)
        def _(t):
            at = pl.ds(pl.multiple_of(t * 128, 128), 128)
            value = hid[at, :]
            scale = lax.rsqrt(jnp.mean(value * value, axis=-1, keepdims=True) + EPSILON)
            g[at, :] = (value * scale).astype(BF16)

    def up():
        @pl.loop(0, hidden_size // TILE)
        def _(t):
            at = cols(t * TILE, TILE)
            first = kdot(g[...], f1[:, at])
            second = kdot(g[...], f2[:, at])
            p1[:, at] = first.astype(BF16)
            p2[:, at] = second.astype(BF16)
            s[:, at] = (first * second).astype(BF16)

    def down():
        @pl.loop(0, width // TILE)
        def _(t):
            at = cols(t * TILE, TILE)
            mixed[:, at] = (hid[:, at] + kdot(s[...], fd[:, at])).astype(BF16)

    def work(n):
        if n == 0:
            project(0, qp, q, True)
            save(q, q_o)
            save(qp, qp_o)
        elif n == 1:
            project(width, kp, k, True)
            save(k, k_o)
            save(kp, kp_o)
        elif n == 2:
            project(2 * width, None, v, False)
            local_states()
            scan.start()
            save(v, v_o)
        elif n == 3:
            project(3 * width, None, u, False)
            save(u, u_o)
            scan.totals_out()
            turn_over(a1, a1t)
            save(a1t, a1t_o)
        elif n == 4:
            attend_local()
            scan.forward()
        elif n == 5:
            scan.results_out()
            turn_over(dy, dyt)
            save(dyt, dyt_o)
        elif n == 6:
            scan.finish()
            save(result, state_o)
            attend_rest()
            save(ob, ob_o)
            hidden()
            save(hid, hid_o)
            turn_over(g, a2t)
            save(a2t, a2t_o)
        elif n == 8:
            up()
            save(p1, p1_o)
            save(p2, p2_o)
            save(s, s_o)
        elif n == 10:
            down()
            save(mixed, mixed_o)

    for n in range(2):
        for step in (1, 2, 0):
            go(n, step)
        own_copy(n).start()
    norm_in()
    for n in range(count + 2):
        if n < count:
            got(n, 1)
            go(n, 3)
            go(n, 5)
            got(n, 2)
            go(n, 4)
            go(n, 6)
            if n + 2 < count:
                for step in (1, 2, 0):
                    go(n + 2, step)
                own_copy(n + 2).start()
        if 0 <= n - 1 < count:
            got(n - 1, 3)
            got(n - 1, 4)
            go(n - 1, 7)
        if n - 2 >= 0:
            for step in (0, 5, 6, 7):
                got(n - 2, step)
            own_copy(n - 2).wait()
            save_piece(n - 2)
            work(n - 2)
    for n in range(count):
        for step in range(8):
            src, dst, where, _ = steps(n)[step]
            move(n, step, src, dst, where).wait_send()
    for copy in saves:
        copy.wait()


def run_forward(table, marks, x, dy, cosine, sine, seg_col, seg_row, weights):
    rows, width = x.shape
    hidden_size = weights[5].shape[1]
    row = jax.ShapeDtypeStruct((rows, width), BF16)
    tall = jax.ShapeDtypeStruct((rows, hidden_size), BF16)
    outs = (
        [
            jax.ShapeDtypeStruct(shape, BF16)
            for shape in (
                (width, 4 * width), (width, width), (width, hidden_size), (width, hidden_size),
                (hidden_size, width),
            )
        ]
        + [row] * 7
        + [jax.ShapeDtypeStruct((rows, width), F32)]
        + [tall] * 3
        + [jax.ShapeDtypeStruct((H, 2, DH, DH), BF16), row]
        + [jax.ShapeDtypeStruct((width, rows), BF16)] * 4
    )
    rv = pltpu.VMEM((rows, width), BF16)
    tv = pltpu.VMEM((rows, hidden_size), BF16)
    scratch = (
        [pltpu.VMEM(o.shape, BF16) for o in outs[:5]]
        + [rv] * 7
        + [pltpu.VMEM((rows, width), F32), rv, rv, pltpu.VMEM((rows, width), F32)]
        + [tv] * 3
        + [rv]
        + [pltpu.VMEM((width, rows), BF16)] * 4
        + scan_scratch()
        + [pltpu.SemaphoreType.DMA((88,))] * 2
        + [pltpu.SemaphoreType.DMA((11,)), pltpu.SemaphoreType.DMA((28,))]
        + [pltpu.SemaphoreType.DMA((13,))] * 2
    )
    return pl.pallas_call(
        forward_kernel,
        out_shape=outs,
        in_specs=[SMEM, SMEM] + [VMEM] * 6 + [ANY] * 8,
        out_specs=[ANY] * len(outs),
        scratch_shapes=scratch,
        compiler_params=pltpu.CompilerParams(
            collective_id=0, has_side_effects=True, vmem_limit_bytes=VMEM_BYTES
        ),
        name="forward",
    )(table, marks, x, dy, cosine, sine, seg_col, seg_row, *weights)


def scan_scratch():
    return [
        pltpu.VMEM((H, 2, DH, DH), BF16),
        pltpu.VMEM((4, 2, 2, DH, DH), BF16),
        pltpu.VMEM((8, 2, 2, DH, DH), BF16),
        pltpu.VMEM((4, 2, 2, DH, DH), BF16),
        pltpu.VMEM((H, 2, DH, DH), BF16),
    ]


def backward_kernel(
    table, marks, cosine, sine, seg_col, seg_row,
    x_i, dy_i, wm_i, wo_i, w1_i, w2_i, wd_i, q_i, k_i, v_i, u_i, qp_i, kp_i, ob_i, hid_i,
    p1_i, p2_i, s_i, state_i, a1t_i, a2t_i, gt_i, dyt_i,
    grad_x_o, gq_o, gk_o, gv_o, gu_o, go_o, g1_o, g2_o, gd_o,
    wd, w1, w2, s, p1, p2, dy, hid, dh, dz, ob, u, q, k, v, dqp, dkp, dv, state_in,
    a1t, a2t, gt, dyt, states, inbox, totals, outbox, result,
    give, take, merged, take_a, take_b, half_a, half_b, take2, mine, take3, pair, take4, final,
    send, recv, free, load_sem, out_sem, scan_send, scan_recv,
):
    place = Place()
    rows, width = dy.shape
    chunk = rows // 2
    hidden_size = s.shape[1]
    place.greet()

    loads = {}

    def load(name, src, dst):
        copy = pltpu.make_async_copy(src, dst, load_sem.at[len(loads)])
        copy.start()
        loads[name] = copy

    def ready(*names):
        for name in names:
            loads[name].wait()

    for name, src, dst in (
        ("dyt", dyt_i, dyt), ("s", s_i, s), ("dy", dy_i, dy), ("wd", wd_i, wd), ("p1", p1_i, p1),
        ("p2", p2_i, p2), ("a2t", a2t_i, a2t), ("w1", w1_i, w1), ("w2", w2_i, w2),
        ("hid", hid_i, hid), ("ob", ob_i, ob), ("u", u_i, u), ("q", q_i, q), ("gt", gt_i, gt),
        ("k", k_i, k), ("v", v_i, v), ("state", state_i, state_in), ("a1t", a1t_i, a1t),
    ):
        load(name, src, dst)

    pieces = []
    for left, right, out in ((dyt, s, gd_o), (a2t, p1, g1_o), (a2t, p2, g2_o)):
        start = 0
        while start < hidden_size:
            size = min(1024, hidden_size - start)
            pieces.append((left, right, out, start, size))
            start += size
    for left, right, out in (
        (gt, dz, go_o), (a1t, u, gu_o), (a1t, dqp, gq_o), (a1t, dkp, gk_o), (a1t, dv, gv_o),
    ):
        pieces.append((left, right, out, 0, width))
    count = len(pieces)
    low, high = place.z % 2, place.z // 2
    f = place.f
    partner = [
        place.at(f=place.fc),
        place.at(f=place.fx),
        place.at(f=place.fy),
        place.at(f=place.fy),
        place.at(f=place.fx),
        place.at(z=place.zs[0]),
        place.at(z=place.zs[1]),
    ]

    def move(n, t):
        _, _, _, _, size = pieces[n]
        slot, half = n % 2, size // 2
        a, b, whole = pl.ds(0, half), pl.ds(half, half), pl.ds(0, size)
        src, dst = [
            (give.at[slot, :, whole], take.at[slot, :, whole]),
            (merged.at[slot, :, 1, :, a], take_a.at[slot, :, :, a]),
            (merged.at[slot, 1, :, :, b], take_b.at[slot, :, :, a]),
            (half_a.at[slot, 1, :, a], take2.at[slot, 0, :, a]),
            (half_b.at[slot, 1, :, a], take2.at[slot, 1, :, a]),
            (mine.at[slot, :, 1 - low, :, whole], take3.at[slot, :, :, whole]),
            (pair.at[slot, 1 - high, :, whole], take4.at[slot, :, whole]),
        ][t]
        return pltpu.make_async_remote_copy(
            src_ref=src,
            dst_ref=dst,
            send_sem=send.at[2 * t + slot],
            recv_sem=recv.at[2 * t + slot],
            device_id=partner[t],
            device_id_type=MESH,
        )

    def go(n, t):
        if n >= 2:
            pl.semaphore_wait(free.at[t], 1)
        move(n, t).start()

    def reuse(n, t):
        if n >= 2:
            move(n - 2, t).wait_send()

    def got(n, t):
        move(n, t).wait_recv()

    def used(n, t):
        if n + 2 < count:
            pl.semaphore_signal(free.at[t], 1, device_id=partner[t], device_id_type=MESH)

    def tiles(size):
        return size // TILE

    def give_half(n):
        left, right, _, start, size = pieces[n]
        slot = n % 2
        reuse(n, 0)

        @pl.loop(0, tiles(size))
        def _(t):
            value = kdot(left[rows : 2 * rows, :], right[:, cols(start + t * TILE, TILE)])
            give[slot, :, cols(t * TILE, TILE)] = value.astype(BF16)

        go(n, 0)

    def merge(n):
        left, right, _, start, size = pieces[n]
        slot = n % 2
        got(n, 0)
        reuse(n, 1)
        reuse(n, 2)

        @pl.loop(0, tiles(size))
        def _(t):
            at = cols(t * TILE, TILE)
            value = kdot(left[0:rows, :], right[:, cols(start + t * TILE, TILE)])
            value = (value + take[slot, :, at].astype(F32)).astype(BF16)
            for y in range(2):
                for x in range(2):
                    r = (2 * y + x) * 128
                    merged[slot, y, x, :, at] = value[r : r + 128]

        used(n, 0)
        go(n, 1)
        go(n, 2)

    def add(a, b):
        return a.astype(F32) + b.astype(F32)

    def halve(n):
        size = pieces[n][4]
        slot, half = n % 2, size // 2
        got(n, 1)
        reuse(n, 3)
        for i in (1, 0):
            half_a[slot, i, :, :half] = add(
                merged[slot, i, 0, :, :half], take_a[slot, i, :, :half]
            ).astype(BF16)
        used(n, 1)
        go(n, 3)
        got(n, 2)
        reuse(n, 4)
        for i in (1, 0):
            half_b[slot, i, :, :half] = add(
                merged[slot, 0, i, :, half:size], take_b[slot, i, :, :half]
            ).astype(BF16)
        used(n, 2)
        go(n, 4)

    def quarter(n):
        size = pieces[n][4]
        slot, half = n % 2, size // 2
        reuse(n, 5)
        for t, kept, at in ((3, half_a, slice(0, half)), (4, half_b, slice(half, size))):
            got(n, t)
            value = add(kept[slot, 0, :, :half], take2[slot, t - 3, :, :half]).astype(BF16)
            used(n, t)
            for i in range(4):
                mine[slot, i // 2, i % 2, :, at] = value[32 * i : 32 * i + 32]
        go(n, 5)

    def along(n):
        size = pieces[n][4]
        slot = n % 2
        got(n, 5)
        reuse(n, 6)
        for i in range(2):
            pair[slot, i, :, :size] = add(
                mine[slot, i, low, :, :size], take3[slot, i, :, :size]
            ).astype(BF16)
        used(n, 5)
        go(n, 6)

    def final_copy(n):
        _, _, out, start, size = pieces[n]
        slot = n % 2
        return pltpu.make_async_copy(
            final.at[slot, :, pl.ds(0, size)], out.at[:, pl.ds(start, size)], out_sem.at[slot]
        )

    def end(n):
        size = pieces[n][4]
        slot = n % 2
        got(n, 6)
        if n >= 2:
            final_copy(n - 2).wait()
        final[slot, :, :size] = add(pair[slot, high, :, :size], take4[slot, :, :size])
        used(n, 6)
        final_copy(n).start()

    offset = lax.broadcasted_iota(jnp.int32, (chunk, 1), 0).astype(F32)
    scan = Scan(place, table, 8, states, inbox, totals, outbox, result, scan_send, scan_recv)

    def row_tiles(body):
        @pl.loop(0, rows // 128)
        def _(t):
            body(pl.ds(pl.multiple_of(t * 128, 128), 128))

    def inner():
        ready("dy", "wd", "p1", "p2")

        @pl.loop(0, hidden_size // TILE)
        def _(t):
            at = cols(t * TILE, TILE)
            ds = kdot(dy[...], wd[pl.ds(pl.multiple_of(t * TILE, TILE), TILE), :], ((1,), (1,)))
            first = p1[:, at].astype(F32)
            p1[:, at] = (ds * p2[:, at].astype(F32)).astype(BF16)
            p2[:, at] = (ds * first).astype(BF16)

        load("wo", wo_i, wd.at[pl.ds(0, width)])

    def middle():
        ready("w1", "w2", "hid")

        @pl.loop(0, width // TILE)
        def _(t):
            r = pl.ds(pl.multiple_of(t * TILE, TILE), TILE)
            dh[:, cols(t * TILE, TILE)] = kdot(p1[...], w1[r, :], ((1,), (1,))) + kdot(
                p2[...], w2[r, :], ((1,), (1,))
            )

        load("wq", wm_i.at[:, pl.ds(0, 2 * width)], w1.at[:, pl.ds(0, 2 * width)])
        load("wv", wm_i.at[:, pl.ds(2 * width, 2 * width)], w2.at[:, pl.ds(0, 2 * width)])

        def body(at):
            value = hid[at, :]
            scale = lax.rsqrt(jnp.mean(value * value, axis=-1, keepdims=True) + EPSILON)
            normed = value * scale
            grad = dh[at, :]
            mean = jnp.mean(grad * normed, axis=-1, keepdims=True)
            grad = dy[at, :].astype(F32) + scale * (grad - normed * mean)
            dh[at, :] = grad
            dz[at, :] = grad.astype(BF16)

        row_tiles(body)
        load("x", x_i, dy)

    def outer():
        ready("wo", "ob", "u", "q")

        @pl.loop(0, width // TILE)
        def _(t):
            r = pl.ds(pl.multiple_of(t * TILE, TILE), TILE)
            hid[:, cols(t * TILE, TILE)] = kdot(dz[...], wd[r, :], ((1,), (1,)))

        def body(at):
            value = ob[at, :].astype(F32)
            scale = lax.rsqrt(jnp.mean(value * value, axis=-1, keepdims=True) + EPSILON)
            normed = value * scale
            grad = hid[at, :]
            dm = grad * u[at, :].astype(F32)
            u[at, :] = (grad * normed).astype(BF16)
            mean = jnp.mean(dm * normed, axis=-1, keepdims=True)
            ob[at, :] = (scale * (dm - normed * mean)).astype(BF16)

        row_tiles(body)

        @pl.loop(0, H)
        def _(h):
            at = cols(h * DH, DH)
            for m in range(2):
                r = slice(m * chunk, (m + 1) * chunk)
                entering = edge(seg_col[r], marks[m], table[h], offset + 1.0)
                left = (q[r, at].astype(F32) * entering).astype(BF16)
                states[h, m] = kdot(left, ob[r, at], ((0,), (0,))).astype(BF16)

        scan.start()

    def turn_back(grad, pre):
        grad = grad.astype(BF16).astype(F32)
        pre = pre.astype(F32)
        return grad, pre

    def attend(first, last):
        @pl.loop(first, last)
        def _(h):
            at = cols(h * DH, DH)
            decay = decays(table[h], chunk)
            for m in range(2):
                r = slice(m * chunk, (m + 1) * chunk)
                within = jnp.where(seg_col[r] == seg_row[m : m + 1], decay, 0.0)
                entering = edge(seg_col[r], marks[m], table[h], offset + 1.0)
                leaving = edge(seg_col[r], marks[2 + m], table[h], chunk - 1.0 - offset)
                qh, kh, vh, oh = q[r, at], k[r, at], v[r, at], ob[r, at]
                scores = (kdot(qh, kh, ((1,), (1,))) * within).astype(BF16)
                grads = (kdot(oh, vh, ((1,), (1,))) * within).astype(BF16)
                dq = kdot(grads, kh) + entering * kdot(oh, state_in[h, m], ((1,), (1,)))
                dk = kdot(grads, qh, ((0,), (0,)))
                dk = dk + leaving * kdot(vh, result[h, m], ((1,), (1,)))
                grad_v = kdot(scores, oh, ((0,), (0,))) + leaving * kdot(kh, result[h, m])
                dv[r, at] = grad_v.astype(BF16)
                for grad, base, low_out in ((dq, 0, dqp), (dk, width, dkp)):
                    grad = grad.astype(BF16).astype(F32)
                    back = grad * cosine[r, :] - pltpu.roll(grad, DH // 2, 1) * sine[r, :]
                    pre = s[r, cols(base + h * DH, DH)].astype(F32)
                    sig = lax.logistic(pre)
                    slope = sig * (1.0 + pre * (1.0 - sig))
                    low_out[r, at] = (slope * back).astype(BF16)

    def inputs():
        ready("wq", "wv", "x")

        @pl.loop(0, width // TILE)
        def _(t):
            r = pl.ds(pl.multiple_of(t * TILE, TILE), TILE)
            acc = kdot(dqp[...], w1[r, 0:width], ((1,), (1,)))
            acc += kdot(dkp[...], w1[r, width : 2 * width], ((1,), (1,)))
            acc += kdot(dv[...], w2[r, 0:width], ((1,), (1,)))
            acc += kdot(u[...], w2[r, width : 2 * width], ((1,), (1,)))
            hid[:, cols(t * TILE, TILE)] = acc

        def body(at):
            value = dy[at, :].astype(F32)
            scale = lax.rsqrt(jnp.mean(value * value, axis=-1, keepdims=True) + EPSILON)
            normed = value * scale
            grad = hid[at, :]
            mean = jnp.mean(grad * normed, axis=-1, keepdims=True)
            dz[at, :] = (dh[at, :] + scale * (grad - normed * mean)).astype(BF16)

        row_tiles(body)
        load("grad_x", dz, grad_x_o)

    def work(n):
        if n == 1:
            inner()
        elif n == 2:
            ready("a2t")
            middle()
        elif n == 3:
            load("qp", qp_i, s.at[:, pl.ds(0, width)])
            load("kp", kp_i, s.at[:, pl.ds(width, width)])
            outer()
        elif n == 4:
            scan.totals_out()
        elif n == 5:
            scan.forward()
        elif n == 6:
            scan.results_out()
            ready("gt", "k", "v", "state", "a1t", "qp", "kp")
        elif n == 7:
            scan.finish()
            attend(0, H // 2)
        elif n == 8:
            attend(H // 2, H)
        elif n == 11:
            inputs()

    ready("dyt", "s")
    for n in range(count + 5):
        if n < count:
            give_half(n)
        if 0 <= n - 1 < count:
            merge(n - 1)
        if 0 <= n - 2 < count:
            halve(n - 2)
        if 0 <= n - 3 < count:
            quarter(n - 3)
        if 0 <= n - 4 < count:
            along(n - 4)
        if 0 <= n - 5 < count:
            end(n - 5)
        work(n)
    for n in (count - 2, count - 1):
        for t in range(7):
            move(n, t).wait_send()
        final_copy(n).wait()
    ready("grad_x")


def run_backward(table, marks, cosine, sine, seg_col, seg_row, x, dy, kept):
    rows, width = x.shape
    hidden_size = kept[2].shape[1]
    part = width // 32
    row = jax.ShapeDtypeStruct((rows, width), BF16)
    outs = (
        [row]
        + [jax.ShapeDtypeStruct((part, width), F32)] * 5
        + [jax.ShapeDtypeStruct((part, hidden_size), F32)] * 3
    )
    rv = pltpu.VMEM((rows, width), BF16)
    fv = pltpu.VMEM((rows, width), F32)
    tv = pltpu.VMEM((rows, hidden_size), BF16)
    wv = pltpu.VMEM((width, hidden_size), BF16)
    n = 1024
    scratch = (
        [pltpu.VMEM((hidden_size, width), BF16), wv, wv, tv, tv, tv, rv, fv, fv]
        + [rv] * 9
        + [pltpu.VMEM((H, 2, DH, DH), BF16)]
        + [pltpu.VMEM((width, rows), BF16)] * 4
        + scan_scratch()
        + [
            pltpu.VMEM((2, 512, n), BF16),
            pltpu.VMEM((2, 512, n), BF16),
            pltpu.VMEM((2, 2, 2, 128, n), BF16),
            pltpu.VMEM((2, 2, 128, n // 2), BF16),
            pltpu.VMEM((2, 2, 128, n // 2), BF16),
            pltpu.VMEM((2, 2, 128, n // 2), BF16),
            pltpu.VMEM((2, 2, 128, n // 2), BF16),
            pltpu.VMEM((2, 2, 128, n // 2), BF16),
            pltpu.VMEM((2, 2, 2, 32, n), BF16),
            pltpu.VMEM((2, 2, 32, n), BF16),
            pltpu.VMEM((2, 2, 32, n), BF16),
            pltpu.VMEM((2, 32, n), BF16),
            pltpu.VMEM((2, 32, n), F32),
        ]
        + [pltpu.SemaphoreType.DMA((14,))] * 2
        + [pltpu.SemaphoreType.REGULAR((7,)), pltpu.SemaphoreType.DMA((26,))]
        + [pltpu.SemaphoreType.DMA((2,))]
        + [pltpu.SemaphoreType.DMA((13,))] * 2
    )
    return pl.pallas_call(
        backward_kernel,
        out_shape=outs,
        in_specs=[SMEM, SMEM] + [VMEM] * 4 + [ANY] * (2 + len(kept)),
        out_specs=[ANY] * len(outs),
        scratch_shapes=scratch,
        compiler_params=pltpu.CompilerParams(
            collective_id=1, has_side_effects=True, vmem_limit_bytes=VMEM_BYTES
        ),
        name="backward",
    )(table, marks, cosine, sine, seg_col, seg_row, x, dy, *kept)


def factors(ends, rates, chunk, f, nf, nh, backward):
    mb = ends.shape[0]
    places = jnp.arange(nh)
    groups = jnp.arange(nf)
    at_group = lax.dynamic_slice_in_dim(ends, f * nh, nh, axis=1)
    before_group = jnp.where(
        f > 0, lax.dynamic_index_in_dim(ends, jnp.maximum(f * nh - 1, 0), 1, False), 0
    )
    before = jnp.concatenate([before_group[:, None], at_group[:, :-1]], axis=1)
    last = at_group[:, -1]
    group_last = ends.reshape(mb, nf, nh)[:, :, -1]
    group_before = jnp.concatenate([jnp.zeros_like(group_last[:, :1]), group_last[:, :-1]], axis=1)

    def factor(same, gap):
        gap = jnp.maximum(gap, 0)
        value = jnp.exp(-rates * (chunk * gap).astype(F32)[..., None])
        return jnp.where(same[..., None], value, 0.0).reshape(-1)

    rise = jnp.broadcast_to(places, (mb, nh))
    fall = jnp.broadcast_to(nh - 1 - places, (mb, nh))
    if backward:
        to_total = factor(before == before_group[:, None], rise)
        group_same = (last[:, None] == group_before) & (groups > f)
        group_gap = jnp.broadcast_to((groups - 1 - f) * nh, (mb, nf))
        to_place = factor(at_group == last[:, None], fall)
        same = (at_group[:, :, None] == before[:, None, :]) & (places[None, :] > places[:, None])
        gap = jnp.broadcast_to(places[None, :] - 1 - places[:, None], (mb, nh, nh))
    else:
        to_total = factor(at_group == last[:, None], fall)
        group_same = (before_group[:, None] == group_last) & (groups < f)
        group_gap = jnp.broadcast_to((f - 1 - groups) * nh, (mb, nf))
        to_place = factor(before == before_group[:, None], rise)
        same = (before[:, :, None] == at_group[:, None, :]) & (places[None, :] < places[:, None])
        gap = jnp.broadcast_to(places[:, None] - 1 - places[None, :], (mb, nh, nh))
    return jnp.concatenate([to_total, factor(group_same, group_gap), to_place, factor(same, gap)])


def local_fast(tokens, cotangent, lengths, decay_rate, *weights):
    wires = Wires()
    mb, chunk, width = tokens.shape
    rows = mb * chunk
    nf, nh = wires.nf, wires.nh
    place = wires.f * nh + wires.h
    positions = place * chunk + jnp.arange(chunk, dtype=jnp.int32)
    cosine, sine_vals = rotation_tables(positions, DH)
    cosine, sine_vals = cosine[:, 0], sine_vals[:, 0]
    cos_table = jnp.tile(cosine, (mb, 2))
    sin_table = jnp.tile(jnp.concatenate([-sine_vals, sine_vals], axis=1), (mb, 1))
    seq_ends = jnp.cumsum(lengths, axis=1)
    segs = jnp.sum((seq_ends[:, None, :] <= positions[None, :, None]).astype(jnp.int32), axis=2)
    chunk_ends = (jnp.arange(nf * nh, dtype=jnp.int32) + 1) * chunk - 1
    ends = jnp.sum((seq_ends[:, None, :] <= chunk_ends[None, :, None]).astype(jnp.int32), axis=2)
    last = lax.dynamic_index_in_dim(ends, place, 1, False)
    before = jnp.where(
        place > 0, lax.dynamic_index_in_dim(ends, jnp.maximum(place - 1, 0), 1, False), 0
    )
    marks = jnp.concatenate([before, last])
    mine = H // nh
    rates = lax.dynamic_slice_in_dim(decay_rate, wires.h * mine, mine)
    table = jnp.concatenate([decay_rate, factors(ends, rates, chunk, wires.f, nf, nh, False)])
    back_table = jnp.concatenate([decay_rate, factors(ends, rates, chunk, wires.f, nf, nh, True)])
    x = tokens.reshape(rows, width)
    dy = cotangent.reshape(rows, width)
    seg_col = segs.reshape(rows, 1)
    around = (marks, cos_table, sin_table, seg_col, segs)
    outs = run_forward(table, marks, x, dy, *around[1:], weights)
    mixed = outs[17]
    kept = outs[:17] + outs[18:]
    grads = run_backward(back_table, *around, x, dy, kept)
    return (
        mixed.reshape(mb, chunk, width),
        grads[0].reshape(mb, chunk, width),
        *grads[1:8],
        grads[8].T,
    )


def solution(mesh):
    rows = P(None, AXES, None)
    in_specs = (rows, rows, P(), P()) + (P("fsdp", None),) * 7 + (P(None, "fsdp"),)
    out_specs = (rows, rows) + (P(AXES, None),) * 7 + (P(None, AXES),)
    fast = mesh.shape["fsdp"] == 8 and mesh.shape["head"] == 4
    local = local_fast if fast else local_any
    return jax.shard_map(local, mesh=mesh, in_specs=in_specs, out_specs=out_specs, check_vma=False)
```

```python
import functools
import math

import jax
import jax.numpy as jnp
from jax import lax
from jax.experimental import pallas as pl
from jax.experimental.pallas import tpu as pltpu
from jax.sharding import PartitionSpec as P

H = 8
DH = 128
EPSILON = 1e-06
AXES = ("fsdp", "head")
F32 = jnp.float32
BF16 = jnp.bfloat16
MESH = pl.DeviceIdType.MESH
ANY = pl.BlockSpec(memory_space=pl.ANY)
VMEM = pl.BlockSpec(memory_space=pltpu.VMEM)
SMEM = pl.BlockSpec(memory_space=pltpu.SMEM)
VMEM_BYTES = 63 * 1024 * 1024
TILE = 256


def norm_parts(values):
    inv_scale = lax.rsqrt(jnp.mean(values * values, axis=-1, keepdims=True) + EPSILON)
    return (values * inv_scale, inv_scale)


def norm_back(gradient, normed, inv_scale):
    return inv_scale * (gradient - normed * jnp.mean(gradient * normed, axis=-1, keepdims=True))


def rotate_pairs(values, cosine, sine_vals):
    half_size = values.shape[-1] // 2
    first_half = values[..., :half_size]
    second_half = values[..., half_size:]
    return jnp.concatenate(
        [
            first_half * cosine - second_half * sine_vals,
            first_half * sine_vals + second_half * cosine,
        ],
        axis=-1,
    )


def rotation_tables(positions, head_size):
    half_size = head_size // 2
    shifts = jnp.arange(half_size, dtype=jnp.int32) * 10 // half_size
    speeds = jnp.right_shift(jnp.full((half_size,), 651, jnp.int32), shifts) + 1
    phases = positions[:, None] * speeds[None, :] % 4096
    angles = phases.astype(F32) * (2.0 * math.pi / 4096.0)
    return (jnp.cos(angles)[:, None, :], jnp.sin(angles)[:, None, :])


def silu_slope(values):
    sigmoid_v = jax.nn.sigmoid(values)
    return sigmoid_v * (1.0 + values * (1.0 - sigmoid_v))


def dot(a, b):
    return jnp.dot(a, b, preferred_element_type=F32)


def dot_rows(a, b):
    return lax.dot_general(a, b, (((0,), (0,)), ((), ())), preferred_element_type=F32)


def dot_cols(a, b):
    return lax.dot_general(a, b, (((1,), (1,)), ((), ())), preferred_element_type=F32)


class Wires:
    def __init__(self):
        self.nf = lax.axis_size("fsdp")
        self.nh = lax.axis_size("head")
        self.fast = self.nf == 8 and self.nh == 4
        self.f = lax.axis_index("fsdp")
        self.h = lax.axis_index("head")

    def swap(self, values, fbits=0, hbits=0):
        pairs = []
        for f in range(self.nf):
            for h in range(self.nh):
                pairs.append((f * self.nh + h, (f ^ fbits) * self.nh + (h ^ hbits)))
        return lax.ppermute(values, AXES, pairs)

    def rel(self, values):
        if not self.fast:
            return values
        width = values.shape[1] // self.nf
        return jnp.concatenate(
            [
                lax.dynamic_slice_in_dim(values, (self.f ^ i) * width, width, 1)
                for i in range(self.nf)
            ],
            axis=1,
        )

    def gather(self, shard):
        if not self.fast:
            return lax.all_gather(shard, "fsdp", axis=0, tiled=True)
        half = shard.shape[1] // 2
        core, x, y = 1, 2, 4
        at_c = self.swap(shard, core)
        at_x = self.swap(shard, x)
        at_y = self.swap(shard, y)
        at_xy = jnp.concatenate(
            [self.swap(at_x[:, :half], y), self.swap(at_y[:, half:], x)], axis=1
        )
        at_cx = self.swap(at_x, core)
        at_cy = self.swap(at_y, core)
        at_cxy = self.swap(at_xy, core)
        return jnp.concatenate([shard, at_c, at_x, at_cx, at_y, at_cy, at_xy, at_cxy], axis=0)

    def reduce(self, grad):
        if not self.fast:
            return lax.psum_scatter(grad, AXES, scatter_dimension=0, tiled=True)
        core, x, y = 1, 2, 4
        rows, n = grad.shape[0] // 8, grad.shape[1]
        low = grad.astype(BF16).reshape(2, 2, 2, rows, n)
        merged = (low[:, :, 0].astype(F32) + self.swap(low[:, :, 1], core).astype(F32)).astype(BF16)
        half = n // 2
        a = merged[:, :, :, :half]
        a = (a[:, 0].astype(F32) + self.swap(a[:, 1], x).astype(F32)).astype(BF16)
        a = (a[0].astype(F32) + self.swap(a[1], y).astype(F32)).astype(BF16)
        b = merged[:, :, :, half:]
        b = (b[0].astype(F32) + self.swap(b[1], y).astype(F32)).astype(BF16)
        b = (b[0].astype(F32) + self.swap(b[1], x).astype(F32)).astype(BF16)
        return jnp.concatenate([self.along(a), self.along(b)], axis=1)

    def along(self, part):
        rows, n = part.shape
        part = part.reshape(2, 2, rows // 4, n)
        low, high = self.h % 2, self.h // 2
        keep = lax.dynamic_index_in_dim(part, low, 1, False)
        send = lax.dynamic_index_in_dim(part, 1 - low, 1, False)
        part = (keep.astype(F32) + self.swap(send, 0, 1).astype(F32)).astype(BF16)
        keep = lax.dynamic_index_in_dim(part, high, 0, False)
        send = lax.dynamic_index_in_dim(part, 1 - high, 0, False)
        return keep.astype(F32) + self.swap(send, 0, 2).astype(F32)

    def to_heads(self, states):
        mb, heads, d, _ = states.shape
        mine = heads // self.nh
        parts = jnp.moveaxis(states.reshape(mb, self.nh, mine, d, d), 1, 0)
        return self.scatter(parts)

    def scatter(self, parts):
        if not self.fast:
            return lax.all_to_all(parts, "head", split_axis=0, concat_axis=0, tiled=True)
        got = [lax.dynamic_index_in_dim(parts, self.h, 0, False)]
        for i in range(1, self.nh):
            got.append(self.swap(lax.dynamic_index_in_dim(parts, self.h ^ i, 0, False), 0, i))
        got = jnp.stack(got)
        order = self.h ^ jnp.arange(self.nh)
        return jnp.take(got, order, axis=0)

    def from_heads(self, parts):
        got = self.scatter(parts)
        nh, mb, mine, d, _ = got.shape
        return jnp.moveaxis(got, 0, 1).reshape(mb, nh * mine, d, d)

    def spread(self, total):
        if not self.fast:
            return lax.all_gather(total, "fsdp")
        core, x, y = 1, 2, 4
        at_c = self.swap(total, core)
        pair = jnp.stack([total, at_c])
        at_x = self.swap(pair, x)
        at_y = self.swap(pair, y)
        at_xy = self.swap(pair, x + y)
        got = jnp.concatenate([pair, at_x, at_y, at_xy])
        return jnp.take(got, self.f ^ jnp.arange(self.nf), axis=0)


def chain(wires, states, ends, decay, chunk, backward):
    nf, nh, f = wires.nf, wires.nh, wires.f
    mb, heads = states.shape[:2]
    mine = heads // nh
    rates = lax.dynamic_slice_in_dim(decay, wires.h * mine, mine)
    places = jnp.arange(nh)
    groups = jnp.arange(nf)
    at_group = lax.dynamic_slice_in_dim(ends, f * nh, nh, axis=1)
    before_group = jnp.where(
        f > 0, lax.dynamic_index_in_dim(ends, jnp.maximum(f * nh - 1, 0), 1, False), 0
    )
    before = jnp.concatenate([before_group[:, None], at_group[:, :-1]], axis=1)
    last = at_group[:, -1]
    group_last = ends.reshape(mb, nf, nh)[:, :, -1]
    group_before = jnp.concatenate([jnp.zeros_like(group_last[:, :1]), group_last[:, :-1]], axis=1)

    def factor(same, gap):
        gap = jnp.maximum(gap, 0)
        return jnp.where(
            same[..., None], jnp.exp(-rates * (chunk * gap).astype(F32)[..., None]), 0.0
        )

    own = wires.to_heads(states.astype(BF16)).astype(F32)
    if backward:
        to_total = factor(before == before_group[:, None], jnp.broadcast_to(places, (mb, nh)))
        group_same = (last[:, None] == group_before) & (groups > f)
        group_gap = jnp.broadcast_to((groups - 1 - f) * nh, (mb, nf))
        to_place = factor(at_group == last[:, None], jnp.broadcast_to(nh - 1 - places, (mb, nh)))
        same = (at_group[:, :, None] == before[:, None, :]) & (places[None, :] > places[:, None])
        gap = jnp.broadcast_to(places[None, :] - 1 - places[:, None], (mb, nh, nh))
    else:
        to_total = factor(at_group == last[:, None], jnp.broadcast_to(nh - 1 - places, (mb, nh)))
        group_same = (before_group[:, None] == group_last) & (groups < f)
        group_gap = jnp.broadcast_to((f - 1 - groups) * nh, (mb, nf))
        to_place = factor(before == before_group[:, None], jnp.broadcast_to(places, (mb, nh)))
        same = (before[:, :, None] == at_group[:, None, :]) & (places[None, :] < places[:, None])
        gap = jnp.broadcast_to(places[:, None] - 1 - places[None, :], (mb, nh, nh))
    total = sum(to_total[:, i, :, None, None] * own[i] for i in range(nh))
    totals = wires.spread(total.astype(BF16)).astype(F32)
    from_group = factor(group_same, group_gap)
    outer = sum(from_group[:, i, :, None, None] * totals[i] for i in range(nf))
    between = factor(same, gap)
    result = [
        to_place[:, i, :, None, None] * outer
        + sum(between[:, i, j, :, None, None] * own[j] for j in range(nh) if i != j)
        for i in range(nh)
    ]
    return wires.from_heads(jnp.stack(result).astype(BF16))


def masks(segs, before, last, decay):
    rows = segs.shape[1]
    offsets = jnp.arange(rows, dtype=F32)
    distance = offsets[:, None] - offsets[None, :]
    visible = (segs[:, :, None] == segs[:, None, :]) & (distance >= 0.0)
    within = jnp.where(
        visible[:, None],
        jnp.exp(-decay[:, None, None] * jnp.maximum(distance, 0.0))[None],
        0.0,
    )
    entering = jnp.where(
        (segs == before[:, None])[:, None, :],
        jnp.exp(-decay[:, None] * (offsets + 1.0))[None],
        0.0,
    )
    leaving = jnp.where(
        (segs == last[:, None])[:, None, :],
        jnp.exp(-decay[:, None] * (rows - 1.0 - offsets))[None],
        0.0,
    )
    return within, entering[..., None], leaving[..., None]


def local_any(
    tokens,
    cotangent,
    lengths,
    decay_rate,
    query_weight,
    key_weight,
    value_weight,
    gate_weight,
    out_weight,
    first_weight,
    second_weight,
    down_weight,
):
    wires = Wires()
    mb, chunk, width = tokens.shape
    rows = mb * chunk
    place = wires.f * wires.nh + wires.h
    count = wires.nf * wires.nh

    mix_weights = wires.gather(
        jnp.concatenate([query_weight, key_weight, value_weight, gate_weight], axis=1)
    )
    out_full = wires.gather(out_weight)
    gate_up = wires.gather(jnp.concatenate([first_weight, second_weight], axis=1))
    down_t = wires.gather(down_weight.T)
    hidden_size = down_t.shape[1]

    positions = place * chunk + jnp.arange(chunk, dtype=jnp.int32)
    cosine, sine_vals = rotation_tables(positions, DH)
    cosine, sine_vals = jnp.tile(cosine, (mb, 1, 1)), jnp.tile(sine_vals, (mb, 1, 1))
    seq_ends = jnp.cumsum(lengths, axis=1)
    segs = jnp.sum((seq_ends[:, None, :] <= positions[None, :, None]).astype(jnp.int32), axis=2)
    marks = (jnp.arange(count, dtype=jnp.int32) + 1) * chunk - 1
    ends = jnp.sum((seq_ends[:, None, :] <= marks[None, :, None]).astype(jnp.int32), axis=2)
    last = lax.dynamic_index_in_dim(ends, place, 1, False)
    before = jnp.where(
        place > 0, lax.dynamic_index_in_dim(ends, jnp.maximum(place - 1, 0), 1, False), 0
    )
    within, entering, leaving = masks(segs, before, last, decay_rate)

    def heads(values):
        return values.reshape(mb, chunk, H, DH).transpose(0, 2, 1, 3)

    def flat(values):
        return values.transpose(0, 2, 1, 3).reshape(rows, H * DH)

    def mm(spec, a, b):
        return jnp.einsum(spec, a.astype(BF16), b.astype(BF16), preferred_element_type=F32)

    inputs = tokens.reshape(rows, width).astype(F32)
    normed_in, scale_in = norm_parts(inputs)
    act_rel = wires.rel(normed_in.astype(BF16))
    mixed_pre = dot(act_rel, mix_weights)
    query_pre = mixed_pre[:, :width]
    key_pre = mixed_pre[:, width : 2 * width]
    value_low = mixed_pre[:, 2 * width : 3 * width].astype(BF16)
    gate_vals = mixed_pre[:, 3 * width :]

    def turned(values):
        return rotate_pairs(jax.nn.silu(values).reshape(rows, H, DH), cosine, sine_vals).astype(BF16)

    query_h = heads(turned(query_pre))
    key_h = heads(turned(key_pre))
    value_h = heads(value_low)
    local_state = mm("mhtd,mhte->mhde", key_h * leaving, value_h)
    state_in = chain(wires, local_state, ends, decay_rate, chunk, False)
    scores = (mm("mhsd,mhtd->mhst", query_h, key_h) * within).astype(BF16)
    attended = mm("mhst,mhte->mhse", scores, value_h)
    attended = attended + entering * mm("mhsd,mhde->mhse", query_h, state_in)
    attended = flat(attended.astype(BF16))

    normed_att, scale_att = norm_parts(attended.astype(F32))
    gated_rel = wires.rel((normed_att * gate_vals).astype(BF16))
    hidden = inputs + dot(gated_rel, out_full)
    normed_mid, scale_mid = norm_parts(hidden)
    mid_rel = wires.rel(normed_mid.astype(BF16))
    pre = dot(mid_rel, gate_up)
    first_pre, second_pre = pre[:, :hidden_size], pre[:, hidden_size:]
    product = (first_pre * second_pre).astype(BF16)
    mixed = (hidden + wires.rel(dot_cols(product, down_t))).astype(BF16)

    grad_low = cotangent.reshape(rows, width)
    grad_rel = wires.rel(grad_low)
    share_down = wires.reduce(dot_rows(grad_rel, product)).T
    grad_prod = dot(grad_rel, down_t)
    grad_pre = jnp.concatenate(
        [(grad_prod * second_pre).astype(BF16), (grad_prod * first_pre).astype(BF16)], axis=1
    )
    share_up = wires.reduce(dot_rows(mid_rel, grad_pre))
    grad_mid = wires.rel(dot_cols(grad_pre, gate_up))
    grad_hidden = grad_low.astype(F32) + norm_back(grad_mid, normed_mid, scale_mid)
    grad_hidden_low = grad_hidden.astype(BF16)
    share_out = wires.reduce(dot_rows(gated_rel, grad_hidden_low))
    grad_gated = wires.rel(dot_cols(grad_hidden_low, out_full))
    grad_gate_low = (grad_gated * normed_att).astype(BF16)
    grad_att = heads(norm_back(grad_gated * gate_vals, normed_att, scale_att).astype(BF16))

    grad_state = mm("mhsd,mhse->mhde", query_h * entering, grad_att)
    grad_end = chain(wires, grad_state, ends, decay_rate, chunk, True)
    grad_scores = (mm("mhse,mhte->mhst", grad_att, value_h) * within).astype(BF16)
    grad_q = mm("mhst,mhtd->mhsd", grad_scores, key_h)
    grad_q = grad_q + entering * mm("mhse,mhde->mhsd", grad_att, state_in)
    grad_k = mm("mhst,mhsd->mhtd", grad_scores, query_h)
    grad_k = grad_k + leaving * mm("mhte,mhde->mhtd", value_h, grad_end)
    grad_v = mm("mhst,mhse->mhte", scores, grad_att)
    grad_v = grad_v + leaving * mm("mhtd,mhde->mhte", key_h, grad_end)

    def turned_back(values, pre_values):
        back = flat(values.astype(BF16)).astype(F32).reshape(rows, H, DH)
        back = rotate_pairs(back, cosine, -sine_vals).reshape(rows, width)
        return (silu_slope(pre_values) * back).astype(BF16)

    grad_mix = jnp.concatenate(
        [
            turned_back(grad_q, query_pre),
            turned_back(grad_k, key_pre),
            flat(grad_v.astype(BF16)),
            grad_gate_low,
        ],
        axis=1,
    )
    share_mix = wires.reduce(dot_rows(act_rel, grad_mix))
    grad_act = wires.rel(dot_cols(grad_mix, mix_weights))
    grad_tokens = (grad_hidden + norm_back(grad_act, normed_in, scale_in)).astype(BF16)
    return (
        mixed.reshape(mb, chunk, width),
        grad_tokens.reshape(mb, chunk, width),
        share_mix[:, :width],
        share_mix[:, width : 2 * width],
        share_mix[:, 2 * width : 3 * width],
        share_mix[:, 3 * width :],
        share_out,
        share_up[:, :hidden_size],
        share_up[:, hidden_size:],
        share_down,
    )


def flip(index, bit):
    return index + bit - 2 * bit * ((index // bit) % 2)


def kdot(a, b, dims=((1,), (0,))):
    return lax.dot_general(a, b, (dims, ((), ())), preferred_element_type=F32)


def cols(start, size):
    return pl.ds(pl.multiple_of(start, 128), size)


class Place:
    def __init__(self):
        self.f = lax.axis_index("fsdp")
        self.z = lax.axis_index("head")
        self.fc, self.fx, self.fy = (flip(self.f, b) for b in (1, 2, 4))
        self.fxy = flip(self.fx, 4)
        self.zs = [flip(self.z, 1), flip(self.z, 2), flip(flip(self.z, 1), 2)]

    def at(self, f=None, z=None):
        return {"fsdp": self.f if f is None else f, "head": self.z if z is None else z}

    def greet(self):
        barrier = pltpu.get_barrier_semaphore()
        others = [self.at(f=f) for f in (self.fc, self.fx, self.fy, self.fxy)]
        others += [self.at(z=z) for z in self.zs]
        for other in others:
            pl.semaphore_signal(barrier, inc=1, device_id=other, device_id_type=MESH)
        pl.semaphore_wait(barrier, len(others))


class Weigh:
    def __init__(self, place, lengths, decay, chunk, backward):
        self.p, self.decay, self.chunk, self.backward = place, decay, chunk, backward
        self.sums = []
        for m in range(2):
            total, row = 0, []
            for j in range(lengths.shape[1]):
                total = total + lengths[m, j]
                row.append(total)
            self.sums.append(row)
        first = 4 * place.f
        self.ends = [[self.end(m, first + i) for i in range(-1, 4)] for m in range(2)]
        self.groups = [[self.end(m, 4 * g + 3) for g in range(8)] for m in range(2)]
        own = first + place.z
        self.before = [self.end(m, own - 1) for m in range(2)]
        self.last = [self.end(m, own) for m in range(2)]

    def end(self, m, i):
        position = (i + 1) * self.chunk - 1
        return sum(jnp.where(total <= position, 1, 0) for total in self.sums[m])

    def tables(self, cosine, sine, seg_col, seg_row):
        chunk = self.chunk
        base = (4 * self.p.f + self.p.z) * chunk
        shape = (chunk, DH)
        lane = lax.broadcasted_iota(jnp.int32, shape, 1)
        row = lax.broadcasted_iota(jnp.int32, shape, 0) + base
        half = DH // 2
        turn = lane % half
        speed = jnp.right_shift(jnp.full(shape, 651, jnp.int32), turn * 10 // half) + 1
        angle = ((row * speed) % 4096).astype(F32) * (2.0 * math.pi / 4096.0)
        cos, sin = jnp.cos(angle), jnp.sin(angle)
        sin = jnp.where(lane < half, -sin, sin)
        down = lax.broadcasted_iota(jnp.int32, (chunk, 1), 0) + base
        across = lax.broadcasted_iota(jnp.int32, (1, chunk), 1) + base
        for m in range(2):
            at = slice(m * chunk, (m + 1) * chunk)
            cosine[at, :] = cos
            sine[at, :] = sin
            seg_col[at, :] = sum(jnp.where(total <= down, 1, 0) for total in self.sums[m])
            seg_row[m : m + 1, :] = sum(jnp.where(total <= across, 1, 0) for total in self.sums[m])

    def power(self, same, chunks, hh):
        rate = self.decay[2 * self.p.z + hh]
        gap = jnp.asarray(chunks * self.chunk, jnp.int32).astype(F32)
        value = jnp.exp(jnp.full((1, DH), -rate * gap, F32))
        return jnp.where(same, value, 0.0)

    def to_total(self, m, i, hh):
        ends = self.ends[m]
        if self.backward:
            return self.power(ends[i] == ends[0], i, hh)
        return self.power(ends[i + 1] == ends[4], 3 - i, hh)

    def to_place(self, m, i, hh):
        ends = self.ends[m]
        if self.backward:
            return self.power(ends[i + 1] == ends[4], 3 - i, hh)
        return self.power(ends[i] == ends[0], i, hh)

    def from_group(self, m, g, hh):
        f = self.p.f
        if self.backward:
            before = self.groups[m][g - 1] if g > 0 else 0
            same = (self.ends[m][4] == before) & (g > f)
            return self.power(same, 4 * jnp.maximum(g - 1 - f, 0), hh)
        same = (self.ends[m][0] == self.groups[m][g]) & (g < f)
        return self.power(same, 4 * jnp.maximum(f - 1 - g, 0), hh)

    def others(self, i):
        return range(i + 1, 4) if self.backward else range(i)

    def between(self, m, i, j, hh):
        ends = self.ends[m]
        if self.backward:
            return self.power(ends[i + 1] == ends[j], j - 1 - i, hh)
        return self.power(ends[i] == ends[j + 1], i - 1 - j, hh)


class Scan:
    def __init__(self, place, weigh, states, inbox, totals, outbox, result, send, recv):
        self.p, self.weigh = place, weigh
        self.states, self.inbox, self.totals = states, inbox, totals
        self.outbox, self.result = outbox, result
        self.send, self.recv = send, recv

    def copy(self, src, dst, n, where):
        return pltpu.make_async_remote_copy(
            src_ref=src,
            dst_ref=dst,
            send_sem=self.send.at[n],
            recv_sem=self.recv.at[n],
            device_id=where,
            device_id_type=MESH,
        )

    def to_heads(self, i):
        z = self.p.zs[i]
        return self.copy(self.states.at[pl.ds(2 * z, 2)], self.inbox.at[self.p.z], i, self.p.at(z=z))

    def from_heads(self, i):
        z = self.p.zs[i]
        return self.copy(
            self.outbox.at[z], self.result.at[pl.ds(2 * self.p.z, 2)], 9 + i, self.p.at(z=z)
        )

    def total(self, n, origin, where):
        return self.copy(self.totals.at[origin], self.totals.at[origin], n, self.p.at(f=where))

    def start(self):
        p = self.p
        for i in range(3):
            self.to_heads(i).start()
        self.inbox[p.z] = self.states[pl.ds(2 * p.z, 2)]

    def totals_out(self):
        p = self.p
        for i in range(3):
            self.to_heads(i).wait()
        for hh in range(2):
            for m in range(2):
                acc = sum(
                    self.weigh.to_total(m, i, hh) * self.inbox[i, hh, m].astype(F32)
                    for i in range(4)
                )
                self.totals[p.f, hh, m] = acc.astype(BF16)
        for n, where in ((3, p.fx), (4, p.fy), (5, p.fxy)):
            self.total(n, p.f, where).start()
        self.total(12, p.f, p.fc).start()

    def forward(self):
        p = self.p
        for n, where in ((3, p.fx), (4, p.fy), (5, p.fxy)):
            self.total(n, p.f, where).wait()
            self.total(n + 3, where, p.fc).start()

    def results_out(self):
        p = self.p
        self.total(12, p.f, p.fc).wait()
        for n, where in ((3, p.fx), (4, p.fy), (5, p.fxy)):
            self.total(n + 3, where, p.fc).wait()
        for hh in range(2):
            for m in range(2):
                outer = sum(
                    self.weigh.from_group(m, g, hh) * self.totals[g, hh, m].astype(F32)
                    for g in range(8)
                )
                for i in range(4):
                    acc = self.weigh.to_place(m, i, hh) * outer
                    for j in self.weigh.others(i):
                        acc += self.weigh.between(m, i, j, hh) * self.inbox[j, hh, m].astype(F32)
                    self.outbox[i, hh, m] = acc.astype(BF16)
        for i in range(3):
            self.from_heads(i).start()
        self.result[pl.ds(2 * p.z, 2)] = self.outbox[p.z]

    def finish(self):
        for i in range(3):
            self.from_heads(i).wait()


def edge(seg, mark, rate, gap):
    return jnp.where(seg == mark, jnp.exp(-rate * gap), 0.0)


def decays(rate, rows):
    up = lax.broadcasted_iota(jnp.int32, (rows, rows), 0)
    across = lax.broadcasted_iota(jnp.int32, (rows, rows), 1)
    gap = (up - across).astype(F32)
    return jnp.where(gap >= 0.0, jnp.exp(-rate * jnp.maximum(gap, 0.0)), 0.0)


def up_tile(a2, w1, w2, s, dp1, dp2, t):
    at = cols(t * TILE, TILE)
    first = kdot(a2[...], w1[:, at])
    second = kdot(a2[...], w2[:, at])
    ds = dp1[:, at].astype(F32)
    s[:, at] = (first * second).astype(BF16)
    dp1[:, at] = (ds * second).astype(BF16)
    dp2[:, at] = (ds * first).astype(BF16)


def forward_kernel(
    lengths, decay_rate, x, dy,
    wq, wk, wv, wu, wo, w1, w2, wd,
    mix_o, wo_o, w1_o, w2_o, wd_o, q_o, k_o, v_o, u_o, qp_o, kp_o, ob_o, hid_o, dp1_o, dp2_o, s_o,
    state_o, a2_o, a1t_o, a2t_o, gt_o, dyt_o,
    fm, fo, f1, f2, fd, a1, q, k, v, u, qp, kp, att, ob, g, hid, dp1, dp2, s,
    cosine, sine, seg_col, seg_row, a1t, a2t, gt, dyt, states, inbox, totals, outbox, result,
    send, recv, own_sem, save_sem, scan_send, scan_recv,
):
    place = Place()
    f = place.f
    rows, width = x.shape
    chunk = rows // 2
    hidden_size = w1.shape[1]
    half_hidden = hidden_size // 2
    place.greet()

    pieces = []
    for i, w in ((1, wk), (2, wv), (0, wq), (3, wu)):
        pieces.append((w, fm, (0, 128), (0, width), i * width))
    for part in range(2):
        pieces.append((wd, fd, (part * half_hidden, half_hidden), (0, 128), None))
    pieces.append((wo, fo, (0, 128), (0, width), 0))
    for part in range(2):
        for w, full in ((w1, f1), (w2, f2)):
            at = part * half_hidden
            pieces.append((w, full, (0, 128), (at, half_hidden), at))
    count = len(pieces)
    parity = place.z % 2

    def parts(n):
        thin = (3, 2)[n % 2]
        wide = 8 - thin
        near = (wide + (n // 2) % 2) // 2
        fetch = (parity * thin, wide)
        return {
            "all": (0, 8),
            "fetch": fetch,
            "near": (fetch[0], near),
            "far": (fetch[0] + near, wide - near),
            "give": (parity * wide, thin),
            "take": ((1 - parity) * wide, thin),
        }

    def own(n, part="all"):
        w, _, (r, rs), (c, cs), _ = pieces[n]
        at, size = parts(n)[part]
        eighth = rs // 8
        return w.at[pl.ds(pl.multiple_of(r + at * eighth, 16), size * eighth), pl.ds(c, cs)]

    def block(n, origin, part="all"):
        _, full, (r, rs), (c, cs), to = pieces[n]
        at, size = parts(n)[part]
        eighth = rs // 8
        if to is None:
            start = pl.multiple_of(r + at * eighth, 16)
            return full.at[pl.ds(start, size * eighth), cols(origin * 128, 128)]
        start = pl.multiple_of(origin * 128 + at * eighth, 16)
        return full.at[pl.ds(start, size * eighth), pl.ds(to, cs)]

    fc, fx, fy, fxy = place.fc, place.fx, place.fy, place.fxy
    at_c, at_x, at_y = (place.at(f=o) for o in (fc, fx, fy))
    at_z = place.at(z=place.zs[0])

    def step(n, t):
        fetched = own(n, "fetch"), block(n, f, "fetch")
        src, dst, where, lands = [
            (own(n), block(n, f), at_c, (fc, "all")),
            (*fetched, at_x, (fx, "fetch")),
            (*fetched, at_y, (fy, "fetch")),
            (block(n, fx, "near"), None, at_y, (fxy, "near")),
            (block(n, fy, "far"), None, at_x, (fxy, "far")),
            (block(n, fx, "give"), None, at_z, (fx, "take")),
            (block(n, fy, "give"), None, at_z, (fy, "take")),
            (block(n, fxy, "give"), None, at_z, (fxy, "take")),
            (block(n, fx), None, at_c, (flip(fx, 1), "all")),
            (block(n, fy), None, at_c, (flip(fy, 1), "all")),
            (block(n, fxy), None, at_c, (flip(fxy, 1), "all")),
        ][t]
        return src, src if dst is None else dst, where, block(n, *lands)

    def move(n, t, src, dst, where):
        return pltpu.make_async_remote_copy(
            src_ref=src,
            dst_ref=dst,
            send_sem=send.at[n * 11 + t],
            recv_sem=recv.at[n * 11 + t],
            device_id=where,
            device_id_type=MESH,
        )

    def go(n, t):
        src, dst, where, _ = step(n, t)
        move(n, t, src, dst, where).start()

    def got(n, *which):
        for t in which:
            _, _, where, lands = step(n, t)
            move(n, t, lands, lands, where).wait_recv()

    def own_copy(n):
        return pltpu.make_async_copy(own(n), block(n, f), own_sem.at[n])

    saves = []

    def save(src, dst):
        copy = pltpu.make_async_copy(src, dst, save_sem.at[len(saves)])
        copy.start()
        saves.append(copy)

    def save_piece(n):
        full_o = {id(fm): mix_o, id(fo): wo_o, id(f1): w1_o, id(f2): w2_o, id(fd): wd_o}
        _, full, (r, rs), (c, cs), to = pieces[n]
        out = full_o[id(full)]
        if to is None:
            save(full.at[pl.ds(r, rs)], out.at[pl.ds(r, rs)])
        else:
            save(full.at[:, pl.ds(to, cs)], out.at[:, pl.ds(to, cs)])

    def norm_in():
        @pl.loop(0, rows // 128)
        def _(t):
            at = pl.ds(pl.multiple_of(t * 128, 128), 128)
            value = x[at, :].astype(F32)
            scale = lax.rsqrt(jnp.mean(value * value, axis=-1, keepdims=True) + EPSILON)
            a1[at, :] = (value * scale).astype(BF16)

    def turn_over(src, dst):
        @pl.loop(0, width // 128)
        def _(b):
            other_c = (b + f) % 2
            other_x = (b // 2 + f // 2) % 2
            other_y = (b // 4 + f // 4) % 2
            slot = other_c * 4 + other_y * 2 + other_x
            value = src[:, cols(b * 128, 128)].astype(F32)
            dst[pl.ds(pl.multiple_of(slot * 128, 128), 128), :] = value.T.astype(BF16)

    def project(base, pre, low, turn):
        @pl.loop(0, width // TILE)
        def _(t):
            at = cols(t * TILE, TILE)
            acc = kdot(a1[...], fm[:, cols(base + t * TILE, TILE)])
            if not turn:
                low[:, at] = acc.astype(BF16)
                return
            pre[:, at] = acc.astype(BF16)
            acc = acc * lax.logistic(acc)
            turned = []
            for hh in range(TILE // DH):
                piece = acc[:, hh * DH : (hh + 1) * DH]
                turned.append(piece * cosine[...] + pltpu.roll(piece, DH // 2, 1) * sine[...])
            low[:, at] = jnp.concatenate(turned, axis=1).astype(BF16)

    offset = lax.broadcasted_iota(jnp.int32, (chunk, 1), 0).astype(F32)
    weigh = Weigh(place, lengths, decay_rate, chunk, False)
    scan = Scan(place, weigh, states, inbox, totals, outbox, result, scan_send, scan_recv)

    def local_states():
        @pl.loop(0, H)
        def _(h):
            at = cols(h * DH, DH)
            for m in range(2):
                r = slice(m * chunk, (m + 1) * chunk)
                leaving = edge(seg_col[r], weigh.last[m], decay_rate[h], chunk - 1.0 - offset)
                left = (k[r, at].astype(F32) * leaving).astype(BF16)
                states[h, m] = kdot(left, v[r, at], ((0,), (0,))).astype(BF16)

    def attend_local(first, last):
        @pl.loop(first, last)
        def _(h):
            at = cols(h * DH, DH)
            decay = decays(decay_rate[h], chunk)
            for m in range(2):
                r = slice(m * chunk, (m + 1) * chunk)
                within = jnp.where(seg_col[r] == seg_row[m : m + 1], decay, 0.0)
                scores = kdot(q[r, at], k[r, at], ((1,), (1,))) * within
                att[r, at] = kdot(scores.astype(BF16), v[r, at])

    def attend_rest():
        @pl.loop(0, H)
        def _(h):
            at = cols(h * DH, DH)
            for m in range(2):
                r = slice(m * chunk, (m + 1) * chunk)
                entering = edge(seg_col[r], weigh.before[m], decay_rate[h], offset + 1.0)
                ob[r, at] = (att[r, at] + entering * kdot(q[r, at], result[h, m])).astype(BF16)

    def hidden():
        @pl.loop(0, rows // 128)
        def _(t):
            at = pl.ds(pl.multiple_of(t * 128, 128), 128)
            value = ob[at, :].astype(F32)
            scale = lax.rsqrt(jnp.mean(value * value, axis=-1, keepdims=True) + EPSILON)
            g[at, :] = (value * scale * u[at, :].astype(F32)).astype(BF16)

        turn_over(g, gt)
        save(gt, gt_o)

        @pl.loop(0, width // TILE)
        def _(t):
            at = cols(t * TILE, TILE)
            hid[:, at] = x[:, at].astype(F32) + kdot(g[...], fo[:, at])

        @pl.loop(0, rows // 128)
        def _(t):
            at = pl.ds(pl.multiple_of(t * 128, 128), 128)
            value = hid[at, :]
            scale = lax.rsqrt(jnp.mean(value * value, axis=-1, keepdims=True) + EPSILON)
            g[at, :] = (value * scale).astype(BF16)

    def inner(part):
        @pl.loop(0, half_hidden // 128)
        def _(t):
            start = part * half_hidden + t * 128
            rhs = fd[pl.ds(pl.multiple_of(start, 128), 128), :]
            dp1[:, cols(start, 128)] = kdot(dy[...], rhs, ((1,), (1,))).astype(BF16)

    def up():
        @pl.loop(0, half_hidden // TILE)
        def _(t):
            up_tile(g, f1, f2, s, dp1, dp2, t)

    def work(n):
        if n == 0:
            project(width, kp, k, True)
            save(k, k_o)
            save(kp, kp_o)
        elif n == 1:
            project(2 * width, None, v, False)
            local_states()
            scan.start()
            save(v, v_o)
        elif n == 2:
            project(0, qp, q, True)
            save(q, q_o)
            save(qp, qp_o)
        elif n == 3:
            project(3 * width, None, u, False)
            save(u, u_o)
            scan.totals_out()
        elif n == 4:
            attend_local(0, H // 2)
            scan.forward()
        elif n == 5:
            attend_local(H // 2, H)
            scan.results_out()
        elif n == 6:
            inner(0)
            inner(1)
        elif n == 7:
            scan.finish()
            save(result, state_o)
            attend_rest()
            save(ob, ob_o)
            hidden()
            save(hid, hid_o)
            save(g, a2_o)
        elif n == 8:
            up()
            done = pl.ds(0, half_hidden // TILE * TILE)
            save(s.at[:, done], s_o.at[:, done])
            save(dp1, dp1_o)
            save(dp2.at[:, done], dp2_o.at[:, done])
        elif n == 9:
            turn_over(g, a2t)
            save(a2t, a2t_o)

    def early(n):
        if n == 0:
            turn_over(dy, dyt)
            save(dyt, dyt_o)
        elif n == 1:
            turn_over(a1, a1t)
            save(a1t, a1t_o)

    ahead = 2
    for n in range(ahead):
        for t in (1, 2, 0):
            go(n, t)
        own_copy(n).start()
    weigh.tables(cosine, sine, seg_col, seg_row)
    norm_in()
    for n in range(count + 3):
        if n < count:
            got(n, 1)
            go(n, 3)
            go(n, 5)
            got(n, 2)
            go(n, 4)
            go(n, 6)
            if n + ahead < count:
                for t in (1, 2, 0):
                    go(n + ahead, t)
                own_copy(n + ahead).start()
        if 0 <= n - 1 < count:
            got(n - 1, 3, 4)
            go(n - 1, 7)
            got(n - 1, 5)
            go(n - 1, 8)
            got(n - 1, 6)
            go(n - 1, 9)
        if 0 <= n - 2 < count:
            got(n - 2, 7)
            go(n - 2, 10)
        if n - 3 >= 0:
            got(n - 3, 0, 8, 9, 10)
            own_copy(n - 3).wait()
            save_piece(n - 3)
            work(n - 3)
        else:
            early(n)
    for n in range(count):
        for t in range(11):
            src, dst, where, _ = step(n, t)
            move(n, t, src, dst, where).wait_send()
    for copy in saves:
        copy.wait()


def run_forward(lengths, decay_rate, x, dy, weights):
    rows, width = x.shape
    hidden_size = weights[5].shape[1]
    row = jax.ShapeDtypeStruct((rows, width), BF16)
    tall = jax.ShapeDtypeStruct((rows, hidden_size), BF16)
    outs = (
        [
            jax.ShapeDtypeStruct(shape, BF16)
            for shape in (
                (width, 4 * width), (width, width), (width, hidden_size), (width, hidden_size),
                (hidden_size, width),
            )
        ]
        + [row] * 7
        + [jax.ShapeDtypeStruct((rows, width), F32)]
        + [tall] * 3
        + [jax.ShapeDtypeStruct((H, 2, DH, DH), BF16), row]
        + [jax.ShapeDtypeStruct((width, rows), BF16)] * 4
    )
    rv = pltpu.VMEM((rows, width), BF16)
    tv = pltpu.VMEM((rows, hidden_size), BF16)
    scratch = (
        [pltpu.VMEM(o.shape, BF16) for o in outs[:5]]
        + [rv] * 7
        + [pltpu.VMEM((rows, width), F32), rv, rv, pltpu.VMEM((rows, width), F32)]
        + [tv] * 3
        + table_scratch(rows)
        + [pltpu.VMEM((width, rows), BF16)] * 4
        + scan_scratch()
        + [pltpu.SemaphoreType.DMA((121,))] * 2
        + [pltpu.SemaphoreType.DMA((11,)), pltpu.SemaphoreType.DMA((28,))]
        + [pltpu.SemaphoreType.DMA((13,))] * 2
    )
    return pl.pallas_call(
        forward_kernel,
        out_shape=outs,
        in_specs=[SMEM, SMEM] + [VMEM] * 2 + [ANY] * 8,
        out_specs=[ANY] * len(outs),
        scratch_shapes=scratch,
        compiler_params=pltpu.CompilerParams(
            collective_id=0, has_side_effects=True, vmem_limit_bytes=VMEM_BYTES
        ),
        name="forward",
    )(lengths, decay_rate, x, dy, *weights)


def table_scratch(rows):
    return [
        pltpu.VMEM((rows, DH), F32),
        pltpu.VMEM((rows, DH), F32),
        pltpu.VMEM((rows, 1), jnp.int32),
        pltpu.VMEM((2, rows // 2), jnp.int32),
    ]


def scan_scratch():
    return [
        pltpu.VMEM((H, 2, DH, DH), BF16),
        pltpu.VMEM((4, 2, 2, DH, DH), BF16),
        pltpu.VMEM((8, 2, 2, DH, DH), BF16),
        pltpu.VMEM((4, 2, 2, DH, DH), BF16),
        pltpu.VMEM((H, 2, DH, DH), BF16),
    ]


Z_FIRST = (10,)
LAST = 1024


def backward_kernel(
    lengths, decay_rate,
    x_i, dy_i, wm_i, wo_i, w1_i, w2_i, wd_i, q_i, k_i, v_i, u_i, qp_i, kp_i, ob_i, hid_i,
    p1_i, p2_i, s_i, state_i, a2_i, a1t_i, a2t_i, gt_i, dyt_i,
    mixed_o, grad_x_o, gq_o, gk_o, gv_o, gu_o, go_o, g1_o, g2_o, gd_o,
    wd, w1, w2, s, p1, p2, dy, hid, dh, dz, ob, u, q, k, v, dqp, dkp, dv, state_in,
    cosine, sine, seg_col, seg_row, a1t, a2t, gt, dyt, states, inbox, totals, outbox, result,
    give, take, merged, take_a, take_b, half_a, half_b, take2, mine, take3, pair, take4, final,
    z_take, z_sum, z_take2, z_sum2, z_take_a, z_take_b, z_half_a, z_half_b, z_take3, z_final,
    send, recv, free, z_send, z_recv, z_free, load_sem, out_sem, scan_send, scan_recv,
):
    place = Place()
    rows, width = dy.shape
    chunk = rows // 2
    hidden_size = s.shape[1]
    place.greet()

    loads = {}

    def load(name, src, dst):
        copy = pltpu.make_async_copy(src, dst, load_sem.at[len(loads)])
        copy.start()
        loads[name] = copy

    def ready(*names):
        for name in names:
            loads[name].wait()

    done = pl.ds(0, hidden_size // 2 // TILE * TILE)
    for name, src, dst in (
        ("dyt", dyt_i, dyt), ("s", s_i.at[:, done], s.at[:, done]), ("a2t", a2t_i, a2t), ("p1", p1_i, p1),
        ("p2", p2_i.at[:, done], p2.at[:, done]), ("a2", a2_i, dkp), ("w1", w1_i, w1), ("w2", w2_i, w2),
        ("hid", hid_i, hid), ("wd", wd_i, wd), ("dy", dy_i, dy), ("ob", ob_i, ob), ("u", u_i, u), ("q", q_i, q), ("gt", gt_i, gt),
        ("k", k_i, k), ("v", v_i, v), ("state", state_i, state_in), ("a1t", a1t_i, a1t),
    ):
        load(name, src, dst)

    pieces = []
    for start in range(0, hidden_size, 1024):
        size = min(1024, hidden_size - start)
        for left, right, out in ((dyt, s, gd_o), (a2t, p1, g1_o), (a2t, p2, g2_o)):
            pieces.append((left, right, out, start, size))
    for left, right, out in ((gt, dz, go_o), (a1t, u, gu_o), (a1t, dqp, gq_o), (a1t, dkp, gk_o)):
        pieces.append((left, right, out, 0, width))
    for start in range(0, width, LAST):
        pieces.append((a1t, dv, gv_o, start, LAST))
    count = len(pieces)
    level = [n for n in range(count) if n not in Z_FIRST]
    upright = [n for n in range(count) if n in Z_FIRST]
    low, high = place.z % 2, place.z // 2
    f = place.f
    at_c, at_x, at_y = (place.at(f=o) for o in (place.fc, place.fx, place.fy))
    at_z1, at_z2 = (place.at(z=place.zs[i]) for i in range(2))
    partner = [at_c, at_x, at_y, at_y, at_x, at_z1, at_z2]
    z_partner = [at_z1, at_z2, at_x, at_y, at_y, at_x]

    def turn(n, t):
        return n if t == 0 else level.index(n)

    def move(n, t):
        size = pieces[n][4]
        m, slot, half = n % 2, turn(n, t) % 2, size // 2
        a, b, whole = pl.ds(0, half), pl.ds(half, half), pl.ds(0, size)
        src, dst = [
            lambda: (give.at[slot, :, whole], take.at[slot, :, whole]),
            lambda: (merged.at[m, :, 1, :, :, :, a], take_a.at[slot, :, :, :, :, a]),
            lambda: (merged.at[m, 1, :, :, :, :, b], take_b.at[slot, :, :, :, :, a]),
            lambda: (half_a.at[slot, 1, :, :, :, a], take2.at[slot, 0, :, :, :, a]),
            lambda: (half_b.at[slot, 1, :, :, :, a], take2.at[slot, 1, :, :, :, a]),
            lambda: (mine.at[slot, :, 1 - low, :, whole], take3.at[slot, :, :, whole]),
            lambda: (pair.at[slot, 1 - high, :, whole], take4.at[slot, :, whole]),
        ][t]()
        return pltpu.make_async_remote_copy(
            src_ref=src,
            dst_ref=dst,
            send_sem=send.at[2 * t + slot],
            recv_sem=recv.at[2 * t + slot],
            device_id=partner[t],
            device_id_type=MESH,
        )

    def z_move(n, t):
        size = pieces[n][4]
        half = size // 2
        a, b, whole = pl.ds(0, half), pl.ds(half, half), pl.ds(0, size)
        src, dst = [
            lambda: (merged.at[n % 2, :, :, :, 1 - low, :, whole], z_take.at[:, :, :, :, whole]),
            lambda: (z_sum.at[:, :, 1 - high, :, whole], z_take2.at[:, :, :, whole]),
            lambda: (z_sum2.at[:, 1, :, a], z_take_a.at[:, :, a]),
            lambda: (z_sum2.at[1, :, :, b], z_take_b.at[:, :, a]),
            lambda: (z_half_a.at[1, :, a], z_take3.at[0, :, a]),
            lambda: (z_half_b.at[1, :, a], z_take3.at[1, :, a]),
        ][t]()
        return pltpu.make_async_remote_copy(
            src_ref=src,
            dst_ref=dst,
            send_sem=z_send.at[t],
            recv_sem=z_recv.at[t],
            device_id=z_partner[t],
            device_id_type=MESH,
        )

    def order(t):
        return list(range(count)) if t == 0 else level

    def go(n, t):
        if turn(n, t) >= 2:
            pl.semaphore_wait(free.at[t], 1)
        move(n, t).start()

    def reuse(n, t):
        i = turn(n, t)
        if i >= 2:
            move(order(t)[i - 2], t).wait_send()

    def got(n, t):
        move(n, t).wait_recv()

    def used(n, t):
        if turn(n, t) + 2 < len(order(t)):
            pl.semaphore_signal(free.at[t], 1, device_id=partner[t], device_id_type=MESH)

    def z_go(n, t):
        if n != upright[0]:
            pl.semaphore_wait(z_free.at[t], 1)
        z_move(n, t).start()

    def z_reuse(n, t):
        i = upright.index(n)
        if i >= 1:
            z_move(upright[i - 1], t).wait_send()

    def z_used(n, t):
        if n != upright[-1]:
            pl.semaphore_signal(z_free.at[t], 1, device_id=z_partner[t], device_id_type=MESH)

    def give_half(n):
        left, right, _, start, size = pieces[n]
        slot = n % 2
        reuse(n, 0)

        @pl.loop(0, size // TILE)
        def _(t):
            value = kdot(left[rows : 2 * rows, :], right[:, cols(start + t * TILE, TILE)])
            give[slot, :, cols(t * TILE, TILE)] = value.astype(BF16)

        go(n, 0)

    def sent(n):
        if n in level:
            move(n, 1).wait_send()
            move(n, 2).wait_send()
        else:
            z_move(n, 0).wait_send()

    def merge(n):
        left, right, _, start, size = pieces[n]
        slot = n % 2
        got(n, 0)
        if n >= 2:
            sent(n - 2)

        @pl.loop(0, size // TILE)
        def _(t):
            at = cols(t * TILE, TILE)
            value = kdot(left[0:rows, :], right[:, cols(start + t * TILE, TILE)])
            value = (value + take[slot, :, at].astype(F32)).astype(BF16)
            for i in range(16):
                r = i * 32
                merged[slot, i // 8, i // 4 % 2, i // 2 % 2, i % 2, :, at] = value[r : r + 32]

        used(n, 0)
        if n in level:
            go(n, 1)
            go(n, 2)
        else:
            z_go(n, 0)

    def add(a, b):
        return a.astype(F32) + b.astype(F32)

    def halve(n):
        size = pieces[n][4]
        m, slot, half = n % 2, turn(n, 1) % 2, size // 2
        got(n, 1)
        reuse(n, 3)
        for i in (1, 0):
            half_a[slot, i, :, :, :, :half] = add(
                merged[m, i, 0, :, :, :, :half], take_a[slot, i, :, :, :, :half]
            ).astype(BF16)
        used(n, 1)
        go(n, 3)
        got(n, 2)
        reuse(n, 4)
        for i in (1, 0):
            half_b[slot, i, :, :, :, :half] = add(
                merged[m, 0, i, :, :, :, half:size], take_b[slot, i, :, :, :, :half]
            ).astype(BF16)
        used(n, 2)
        go(n, 4)

    def quarter(n):
        size = pieces[n][4]
        slot, half = turn(n, 1) % 2, size // 2
        reuse(n, 5)
        for t, kept, at in ((3, half_a, slice(0, half)), (4, half_b, slice(half, size))):
            got(n, t)
            mine[slot, :, :, :, at] = add(
                kept[slot, 0, :, :, :, :half], take2[slot, t - 3, :, :, :, :half]
            ).astype(BF16)
            used(n, t)
        go(n, 5)

    def along(n):
        size = pieces[n][4]
        slot = turn(n, 1) % 2
        got(n, 5)
        reuse(n, 6)
        for i in range(2):
            pair[slot, i, :, :size] = add(
                mine[slot, i, low, :, :size], take3[slot, i, :, :size]
            ).astype(BF16)
        used(n, 5)
        go(n, 6)

    def result_copy(n, src, sem):
        _, _, out, start, size = pieces[n]
        return pltpu.make_async_copy(src.at[:, pl.ds(0, size)], out.at[:, pl.ds(start, size)], sem)

    def final_copy(n):
        slot = turn(n, 1) % 2
        return result_copy(n, final.at[slot], out_sem.at[slot])

    def end(n):
        size = pieces[n][4]
        i = turn(n, 1)
        slot = i % 2
        got(n, 6)
        if i >= 2:
            final_copy(level[i - 2]).wait()
        final[slot, :, :size] = add(pair[slot, high, :, :size], take4[slot, :, :size])
        used(n, 6)
        final_copy(n).start()

    def z_halve(n):
        size = pieces[n][4]
        z_move(n, 0).wait_recv()
        z_reuse(n, 1)
        for y in range(2):
            z_sum[y, :, :, :, :size] = add(
                merged[n % 2, y, :, :, low, :, :size], z_take[y, :, :, :, :size]
            ).astype(BF16)
        z_used(n, 0)
        z_go(n, 1)

    def z_quarter(n):
        size = pieces[n][4]
        z_move(n, 1).wait_recv()
        z_reuse(n, 2)
        z_reuse(n, 3)
        z_sum2[:, :, :, :size] = add(
            z_sum[:, :, high, :, :size], z_take2[:, :, :, :size]
        ).astype(BF16)
        z_used(n, 1)
        z_go(n, 2)
        z_go(n, 3)

    def z_along(n):
        size = pieces[n][4]
        half = size // 2
        z_move(n, 2).wait_recv()
        z_reuse(n, 4)
        z_half_a[:, :, :half] = add(z_sum2[:, 0, :, :half], z_take_a[:, :, :half]).astype(BF16)
        z_used(n, 2)
        z_go(n, 4)
        z_move(n, 3).wait_recv()
        z_reuse(n, 5)
        z_half_b[:, :, :half] = add(z_sum2[0, :, :, half:size], z_take_b[:, :, :half]).astype(BF16)
        z_used(n, 3)
        z_go(n, 5)

    def z_copy(n):
        return result_copy(n, z_final, out_sem.at[2])

    def z_end(n):
        size = pieces[n][4]
        half = size // 2
        if n != upright[0]:
            z_copy(upright[upright.index(n) - 1]).wait()
        for t, kept, at in ((4, z_half_a, slice(0, half)), (5, z_half_b, slice(half, size))):
            z_move(n, t).wait_recv()
            z_final[:, at] = add(kept[0, :, :half], z_take3[t - 4, :, :half])
            z_used(n, t)
        z_copy(n).start()

    offset = lax.broadcasted_iota(jnp.int32, (chunk, 1), 0).astype(F32)
    weigh = Weigh(place, lengths, decay_rate, chunk, True)
    scan = Scan(place, weigh, states, inbox, totals, outbox, result, scan_send, scan_recv)

    def row_tiles(body):
        @pl.loop(0, rows // 128)
        def _(t):
            body(pl.ds(pl.multiple_of(t * 128, 128), 128))

    def up():
        ready("a2", "w1", "w2")

        @pl.loop(hidden_size // 2 // TILE, hidden_size // TILE)
        def _(t):
            up_tile(dkp, w1, w2, s, p1, p2, t)

    def mix():
        ready("wd")

        @pl.loop(0, width // TILE)
        def _(t):
            at = cols(t * TILE, TILE)
            dqp[:, at] = (hid[:, at] + kdot(s[...], wd[:, at])).astype(BF16)

        load("mixed", dqp, mixed_o)
        load("wo", wo_i, wd.at[pl.ds(0, width)])

    def middle(first, last):
        @pl.loop(first, last)
        def _(t):
            r = pl.ds(pl.multiple_of(t * TILE, TILE), TILE)
            dh[:, cols(t * TILE, TILE)] = kdot(p1[...], w1[r, :], ((1,), (1,))) + kdot(
                p2[...], w2[r, :], ((1,), (1,))
            )

    def middle_rows():
        ready("dy")
        load("wq", wm_i.at[:, pl.ds(0, 2 * width)], w1.at[:, pl.ds(0, 2 * width)])
        load("wv", wm_i.at[:, pl.ds(2 * width, 2 * width)], w2.at[:, pl.ds(0, 2 * width)])

        def body(at):
            value = hid[at, :]
            scale = lax.rsqrt(jnp.mean(value * value, axis=-1, keepdims=True) + EPSILON)
            normed = value * scale
            grad = dh[at, :]
            mean = jnp.mean(grad * normed, axis=-1, keepdims=True)
            grad = dy[at, :].astype(F32) + scale * (grad - normed * mean)
            dh[at, :] = grad
            dz[at, :] = grad.astype(BF16)

        row_tiles(body)
        load("x", x_i, dy)

    def outer():
        ready("wo", "ob", "u")

        @pl.loop(0, width // TILE)
        def _(t):
            r = pl.ds(pl.multiple_of(t * TILE, TILE), TILE)
            hid[:, cols(t * TILE, TILE)] = kdot(dz[...], wd[r, :], ((1,), (1,)))

        def body(at):
            value = ob[at, :].astype(F32)
            scale = lax.rsqrt(jnp.mean(value * value, axis=-1, keepdims=True) + EPSILON)
            normed = value * scale
            grad = hid[at, :]
            dm = grad * u[at, :].astype(F32)
            u[at, :] = (grad * normed).astype(BF16)
            mean = jnp.mean(dm * normed, axis=-1, keepdims=True)
            ob[at, :] = (scale * (dm - normed * mean)).astype(BF16)

        row_tiles(body)

        @pl.loop(0, H)
        def _(h):
            at = cols(h * DH, DH)
            for m in range(2):
                r = slice(m * chunk, (m + 1) * chunk)
                entering = edge(seg_col[r], weigh.before[m], decay_rate[h], offset + 1.0)
                left = (q[r, at].astype(F32) * entering).astype(BF16)
                states[h, m] = kdot(left, ob[r, at], ((0,), (0,))).astype(BF16)

        scan.start()

    def slope(pre):
        sig = lax.logistic(pre)
        return sig * (1.0 + pre * (1.0 - sig))

    def turned_back(grad, r, base, h):
        grad = grad.astype(BF16).astype(F32)
        back = grad * cosine[r, :] - pltpu.roll(grad, DH // 2, 1) * sine[r, :]
        return (slope(s[r, cols(base + h * DH, DH)].astype(F32)) * back).astype(BF16)

    def attend_queries(first, last):
        @pl.loop(first, last)
        def _(h):
            at = cols(h * DH, DH)
            decay = decays(decay_rate[h], chunk)
            for m in range(2):
                r = slice(m * chunk, (m + 1) * chunk)
                within = jnp.where(seg_col[r] == seg_row[m : m + 1], decay, 0.0)
                entering = edge(seg_col[r], weigh.before[m], decay_rate[h], offset + 1.0)
                oh = ob[r, at]
                grads = (kdot(oh, v[r, at], ((1,), (1,))) * within).astype(BF16)
                dq = kdot(grads, k[r, at]) + entering * kdot(oh, state_in[h, m], ((1,), (1,)))
                dqp[r, at] = turned_back(dq, r, 0, h)

    def attend_keys(first, last):
        @pl.loop(first, last)
        def _(h):
            at = cols(h * DH, DH)
            decay = decays(decay_rate[h], chunk)
            for m in range(2):
                r = slice(m * chunk, (m + 1) * chunk)
                within = jnp.where(seg_col[r] == seg_row[m : m + 1], decay, 0.0)
                leaving = edge(seg_col[r], weigh.last[m], decay_rate[h], chunk - 1.0 - offset)
                qh, kh, vh, oh = q[r, at], k[r, at], v[r, at], ob[r, at]
                grads = (kdot(oh, vh, ((1,), (1,))) * within).astype(BF16)
                dk = kdot(grads, qh, ((0,), (0,)))
                dk = dk + leaving * kdot(vh, result[h, m], ((1,), (1,)))
                scores = (kdot(qh, kh, ((1,), (1,))) * within).astype(BF16)
                grad_v = kdot(scores, oh, ((0,), (0,))) + leaving * kdot(kh, result[h, m])
                dv[r, at] = grad_v.astype(BF16)
                dkp[r, at] = turned_back(dk, r, width, h)

    def inputs(first, last):
        @pl.loop(first, last)
        def _(t):
            r = pl.ds(pl.multiple_of(t * TILE, TILE), TILE)
            acc = kdot(dqp[...], w1[r, 0:width], ((1,), (1,)))
            acc += kdot(dkp[...], w1[r, width : 2 * width], ((1,), (1,)))
            acc += kdot(dv[...], w2[r, 0:width], ((1,), (1,)))
            acc += kdot(u[...], w2[r, width : 2 * width], ((1,), (1,)))
            hid[:, cols(t * TILE, TILE)] = acc

    def inputs_rows():
        def body(at):
            value = dy[at, :].astype(F32)
            scale = lax.rsqrt(jnp.mean(value * value, axis=-1, keepdims=True) + EPSILON)
            normed = value * scale
            grad = hid[at, :]
            mean = jnp.mean(grad * normed, axis=-1, keepdims=True)
            dz[at, :] = (dh[at, :] + scale * (grad - normed * mean)).astype(BF16)

        row_tiles(body)
        load("grad_x", dz, grad_x_o)

    def work(n):
        if n == 0:
            weigh.tables(cosine, sine, seg_col, seg_row)
            ready("a2t", "p1", "p2")
        elif n == 1:
            up()
        elif n == 2:
            middle(0, 2)
        elif n == 3:
            middle(2, 4)
            ready("hid")
            middle_rows()
        elif n == 4:
            mix()
            ready("q")
        elif n == 5:
            load("qp", qp_i, s.at[:, pl.ds(0, width)])
            load("kp", kp_i, s.at[:, pl.ds(width, width)])
            outer()
        elif n == 6:
            ready("k", "v", "state", "qp", "kp", "mixed")
            attend_queries(0, H // 2)
        elif n == 7:
            scan.totals_out()
            attend_queries(H // 2, H)
        elif n == 8:
            scan.forward()
            ready("gt", "a1t")
        elif n == 9:
            scan.results_out()
        elif n == 10:
            scan.finish()
            attend_keys(0, H // 2)
        elif n == 11:
            attend_keys(H // 2, H)
            ready("wq", "wv", "x")
        elif n == 13:
            inputs(0, 2)
        elif n == 14:
            inputs(2, 4)
        elif n == 15:
            inputs_rows()

    ready("dyt", "s")
    for n in range(max(level[-1] + 6, upright[-1] + 8)):
        if n < count:
            give_half(n)
        if n - 3 in upright:
            z_halve(n - 3)
        if n - 1 in range(count):
            merge(n - 1)
        if n - 2 in level:
            halve(n - 2)
        if n - 5 in upright:
            z_quarter(n - 5)
        if n - 3 in level:
            quarter(n - 3)
        if n - 6 in upright:
            z_along(n - 6)
        if n - 4 in level:
            along(n - 4)
        if n - 7 in upright:
            z_end(n - 7)
        if n - 5 in level:
            end(n - 5)
        work(n)
    sent(count - 2)
    sent(count - 1)
    for t in (0, 3, 4, 5, 6):
        for n in order(t)[-2:]:
            move(n, t).wait_send()
    for t in range(1, 6):
        z_move(upright[-1], t).wait_send()
    for n in level[-2:]:
        final_copy(n).wait()
    z_copy(upright[-1]).wait()
    ready("grad_x")


def run_backward(lengths, decay_rate, x, dy, kept):
    rows, width = x.shape
    hidden_size = kept[2].shape[1]
    part = width // 32
    row = jax.ShapeDtypeStruct((rows, width), BF16)
    outs = (
        [row] * 2
        + [jax.ShapeDtypeStruct((part, width), F32)] * 5
        + [jax.ShapeDtypeStruct((part, hidden_size), F32)] * 3
    )
    rv = pltpu.VMEM((rows, width), BF16)
    fv = pltpu.VMEM((rows, width), F32)
    tv = pltpu.VMEM((rows, hidden_size), BF16)
    wv = pltpu.VMEM((width, hidden_size), BF16)
    n = 1024
    scratch = (
        [pltpu.VMEM((hidden_size, width), BF16), wv, wv, tv, tv, tv, rv, fv, fv]
        + [rv] * 9
        + [pltpu.VMEM((H, 2, DH, DH), BF16)]
        + table_scratch(rows)
        + [pltpu.VMEM((width, rows), BF16)] * 4
        + scan_scratch()
        + [
            pltpu.VMEM((2, 512, n), BF16),
            pltpu.VMEM((2, 512, n), BF16),
            pltpu.VMEM((2, 2, 2, 2, 2, 32, n), BF16),
            pltpu.VMEM((2, 2, 2, 2, 32, n // 2), BF16),
            pltpu.VMEM((2, 2, 2, 2, 32, n // 2), BF16),
            pltpu.VMEM((2, 2, 2, 2, 32, n // 2), BF16),
            pltpu.VMEM((2, 2, 2, 2, 32, n // 2), BF16),
            pltpu.VMEM((2, 2, 2, 2, 32, n // 2), BF16),
            pltpu.VMEM((2, 2, 2, 32, n), BF16),
            pltpu.VMEM((2, 2, 32, n), BF16),
            pltpu.VMEM((2, 2, 32, n), BF16),
            pltpu.VMEM((2, 32, n), BF16),
            pltpu.VMEM((2, 32, n), F32),
            pltpu.VMEM((2, 2, 2, 32, n), BF16),
            pltpu.VMEM((2, 2, 2, 32, n), BF16),
            pltpu.VMEM((2, 2, 32, n), BF16),
            pltpu.VMEM((2, 2, 32, n), BF16),
            pltpu.VMEM((2, 32, n // 2), BF16),
            pltpu.VMEM((2, 32, n // 2), BF16),
            pltpu.VMEM((2, 32, n // 2), BF16),
            pltpu.VMEM((2, 32, n // 2), BF16),
            pltpu.VMEM((2, 32, n // 2), BF16),
            pltpu.VMEM((32, n), F32),
        ]
        + [pltpu.SemaphoreType.DMA((14,))] * 2
        + [pltpu.SemaphoreType.REGULAR((7,))]
        + [pltpu.SemaphoreType.DMA((6,))] * 2
        + [pltpu.SemaphoreType.REGULAR((6,))]
        + [pltpu.SemaphoreType.DMA((28,)), pltpu.SemaphoreType.DMA((3,))]
        + [pltpu.SemaphoreType.DMA((13,))] * 2
    )
    return pl.pallas_call(
        backward_kernel,
        out_shape=outs,
        in_specs=[SMEM, SMEM] + [ANY] * (2 + len(kept)),
        out_specs=[ANY] * len(outs),
        scratch_shapes=scratch,
        compiler_params=pltpu.CompilerParams(
            collective_id=1, has_side_effects=True, vmem_limit_bytes=VMEM_BYTES
        ),
        name="backward",
    )(lengths, decay_rate, x, dy, *kept)


def hand_over_kernel(*refs):
    count = (len(refs) - 3) // 3
    sources, targets, held = (refs[i * count : (i + 1) * count] for i in range(3))
    turned, sems_in, sems_out = refs[3 * count :]
    fetches = [
        pltpu.make_async_copy(src, dst, sems_in.at[i])
        for i, (src, dst) in enumerate(zip(sources, held))
    ]
    for fetch in fetches:
        fetch.start()
    stores = []
    for i in reversed(range(count)):
        fetches[i].wait()
        src = held[i]
        if i == count - 1:
            for b in range(src.shape[1] // 128):
                at = slice(b * 128, (b + 1) * 128)
                turned[at, :] = src[:, at].T
            src = turned
        store = pltpu.make_async_copy(src, targets[i], sems_out.at[i])
        store.start()
        stores.append(store)
    for store in stores:
        store.wait()


def hand_over(arrays):
    outs = [jax.ShapeDtypeStruct(a.shape, a.dtype) for a in arrays]
    last = arrays[-1]
    outs[-1] = jax.ShapeDtypeStruct(last.shape[::-1], last.dtype)
    return pl.pallas_call(
        hand_over_kernel,
        out_shape=outs,
        in_specs=[ANY] * len(arrays),
        out_specs=[ANY] * len(arrays),
        scratch_shapes=[pltpu.VMEM(a.shape, a.dtype) for a in arrays]
        + [pltpu.VMEM(last.shape[::-1], last.dtype)]
        + [pltpu.SemaphoreType.DMA((len(arrays),))] * 2,
        name="hand_over",
    )(*arrays)


def local_fast(tokens, cotangent, lengths, decay_rate, *weights):
    mb, chunk, width = tokens.shape
    x = tokens.reshape(mb * chunk, width)
    dy = cotangent.reshape(mb * chunk, width)
    kept = run_forward(lengths, decay_rate, x, dy, weights)
    mixed, grad_x, *grads = hand_over(run_backward(lengths, decay_rate, x, dy, kept))
    return (mixed.reshape(tokens.shape), grad_x.reshape(tokens.shape), *grads)


def solution(mesh):
    rows = P(None, AXES, None)
    in_specs = (rows, rows, P(), P()) + (P("fsdp", None),) * 7 + (P(None, "fsdp"),)
    out_specs = (rows, rows) + (P(AXES, None),) * 7 + (P(None, AXES),)
    fast = mesh.shape["fsdp"] == 8 and mesh.shape["head"] == 4
    local = local_fast if fast else local_any
    return jax.shard_map(local, mesh=mesh, in_specs=in_specs, out_specs=out_specs, check_vma=False)
```

```python
import functools
import math

import jax
import jax.numpy as jnp
from jax import lax
from jax.experimental import pallas as pl
from jax.experimental.pallas import tpu as pltpu
from jax.sharding import PartitionSpec as P

H = 8
DH = 128
EPSILON = 1e-06
AXES = ("fsdp", "head")
F32 = jnp.float32
BF16 = jnp.bfloat16
MESH = pl.DeviceIdType.MESH
ANY = pl.BlockSpec(memory_space=pl.ANY)
VMEM = pl.BlockSpec(memory_space=pltpu.VMEM)
SMEM = pl.BlockSpec(memory_space=pltpu.SMEM)
VMEM_BYTES = 63 * 1024 * 1024
TILE = 256


def norm_parts(values):
    inv_scale = lax.rsqrt(jnp.mean(values * values, axis=-1, keepdims=True) + EPSILON)
    return (values * inv_scale, inv_scale)


def norm_back(gradient, normed, inv_scale):
    return inv_scale * (gradient - normed * jnp.mean(gradient * normed, axis=-1, keepdims=True))


def rotate_pairs(values, cosine, sine_vals):
    half_size = values.shape[-1] // 2
    first_half = values[..., :half_size]
    second_half = values[..., half_size:]
    return jnp.concatenate(
        [
            first_half * cosine - second_half * sine_vals,
            first_half * sine_vals + second_half * cosine,
        ],
        axis=-1,
    )


def rotation_tables(positions, head_size):
    half_size = head_size // 2
    shifts = jnp.arange(half_size, dtype=jnp.int32) * 10 // half_size
    speeds = jnp.right_shift(jnp.full((half_size,), 651, jnp.int32), shifts) + 1
    phases = positions[:, None] * speeds[None, :] % 4096
    angles = phases.astype(F32) * (2.0 * math.pi / 4096.0)
    return (jnp.cos(angles)[:, None, :], jnp.sin(angles)[:, None, :])


def silu_slope(values):
    sigmoid_v = jax.nn.sigmoid(values)
    return sigmoid_v * (1.0 + values * (1.0 - sigmoid_v))


def dot(a, b):
    return jnp.dot(a, b, preferred_element_type=F32)


def dot_rows(a, b):
    return lax.dot_general(a, b, (((0,), (0,)), ((), ())), preferred_element_type=F32)


def dot_cols(a, b):
    return lax.dot_general(a, b, (((1,), (1,)), ((), ())), preferred_element_type=F32)


class Wires:
    def __init__(self):
        self.nf = lax.axis_size("fsdp")
        self.nh = lax.axis_size("head")
        self.fast = self.nf == 8 and self.nh == 4
        self.f = lax.axis_index("fsdp")
        self.h = lax.axis_index("head")

    def swap(self, values, fbits=0, hbits=0):
        pairs = []
        for f in range(self.nf):
            for h in range(self.nh):
                pairs.append((f * self.nh + h, (f ^ fbits) * self.nh + (h ^ hbits)))
        return lax.ppermute(values, AXES, pairs)

    def rel(self, values):
        if not self.fast:
            return values
        width = values.shape[1] // self.nf
        return jnp.concatenate(
            [
                lax.dynamic_slice_in_dim(values, (self.f ^ i) * width, width, 1)
                for i in range(self.nf)
            ],
            axis=1,
        )

    def gather(self, shard):
        if not self.fast:
            return lax.all_gather(shard, "fsdp", axis=0, tiled=True)
        half = shard.shape[1] // 2
        core, x, y = 1, 2, 4
        at_c = self.swap(shard, core)
        at_x = self.swap(shard, x)
        at_y = self.swap(shard, y)
        at_xy = jnp.concatenate(
            [self.swap(at_x[:, :half], y), self.swap(at_y[:, half:], x)], axis=1
        )
        at_cx = self.swap(at_x, core)
        at_cy = self.swap(at_y, core)
        at_cxy = self.swap(at_xy, core)
        return jnp.concatenate([shard, at_c, at_x, at_cx, at_y, at_cy, at_xy, at_cxy], axis=0)

    def reduce(self, grad):
        if not self.fast:
            return lax.psum_scatter(grad, AXES, scatter_dimension=0, tiled=True)
        core, x, y = 1, 2, 4
        rows, n = grad.shape[0] // 8, grad.shape[1]
        low = grad.astype(BF16).reshape(2, 2, 2, rows, n)
        merged = (low[:, :, 0].astype(F32) + self.swap(low[:, :, 1], core).astype(F32)).astype(BF16)
        half = n // 2
        a = merged[:, :, :, :half]
        a = (a[:, 0].astype(F32) + self.swap(a[:, 1], x).astype(F32)).astype(BF16)
        a = (a[0].astype(F32) + self.swap(a[1], y).astype(F32)).astype(BF16)
        b = merged[:, :, :, half:]
        b = (b[0].astype(F32) + self.swap(b[1], y).astype(F32)).astype(BF16)
        b = (b[0].astype(F32) + self.swap(b[1], x).astype(F32)).astype(BF16)
        return jnp.concatenate([self.along(a), self.along(b)], axis=1)

    def along(self, part):
        rows, n = part.shape
        part = part.reshape(2, 2, rows // 4, n)
        low, high = self.h % 2, self.h // 2
        keep = lax.dynamic_index_in_dim(part, low, 1, False)
        send = lax.dynamic_index_in_dim(part, 1 - low, 1, False)
        part = (keep.astype(F32) + self.swap(send, 0, 1).astype(F32)).astype(BF16)
        keep = lax.dynamic_index_in_dim(part, high, 0, False)
        send = lax.dynamic_index_in_dim(part, 1 - high, 0, False)
        return keep.astype(F32) + self.swap(send, 0, 2).astype(F32)

    def to_heads(self, states):
        mb, heads, d, _ = states.shape
        mine = heads // self.nh
        parts = jnp.moveaxis(states.reshape(mb, self.nh, mine, d, d), 1, 0)
        return self.scatter(parts)

    def scatter(self, parts):
        if not self.fast:
            return lax.all_to_all(parts, "head", split_axis=0, concat_axis=0, tiled=True)
        got = [lax.dynamic_index_in_dim(parts, self.h, 0, False)]
        for i in range(1, self.nh):
            got.append(self.swap(lax.dynamic_index_in_dim(parts, self.h ^ i, 0, False), 0, i))
        got = jnp.stack(got)
        order = self.h ^ jnp.arange(self.nh)
        return jnp.take(got, order, axis=0)

    def from_heads(self, parts):
        got = self.scatter(parts)
        nh, mb, mine, d, _ = got.shape
        return jnp.moveaxis(got, 0, 1).reshape(mb, nh * mine, d, d)

    def spread(self, total):
        if not self.fast:
            return lax.all_gather(total, "fsdp")
        core, x, y = 1, 2, 4
        at_c = self.swap(total, core)
        pair = jnp.stack([total, at_c])
        at_x = self.swap(pair, x)
        at_y = self.swap(pair, y)
        at_xy = self.swap(pair, x + y)
        got = jnp.concatenate([pair, at_x, at_y, at_xy])
        return jnp.take(got, self.f ^ jnp.arange(self.nf), axis=0)


def chain(wires, states, ends, decay, chunk, backward):
    nf, nh, f = wires.nf, wires.nh, wires.f
    mb, heads = states.shape[:2]
    mine = heads // nh
    rates = lax.dynamic_slice_in_dim(decay, wires.h * mine, mine)
    places = jnp.arange(nh)
    groups = jnp.arange(nf)
    at_group = lax.dynamic_slice_in_dim(ends, f * nh, nh, axis=1)
    before_group = jnp.where(
        f > 0, lax.dynamic_index_in_dim(ends, jnp.maximum(f * nh - 1, 0), 1, False), 0
    )
    before = jnp.concatenate([before_group[:, None], at_group[:, :-1]], axis=1)
    last = at_group[:, -1]
    group_last = ends.reshape(mb, nf, nh)[:, :, -1]
    group_before = jnp.concatenate([jnp.zeros_like(group_last[:, :1]), group_last[:, :-1]], axis=1)

    def factor(same, gap):
        gap = jnp.maximum(gap, 0)
        return jnp.where(
            same[..., None], jnp.exp(-rates * (chunk * gap).astype(F32)[..., None]), 0.0
        )

    own = wires.to_heads(states.astype(BF16)).astype(F32)
    if backward:
        to_total = factor(before == before_group[:, None], jnp.broadcast_to(places, (mb, nh)))
        group_same = (last[:, None] == group_before) & (groups > f)
        group_gap = jnp.broadcast_to((groups - 1 - f) * nh, (mb, nf))
        to_place = factor(at_group == last[:, None], jnp.broadcast_to(nh - 1 - places, (mb, nh)))
        same = (at_group[:, :, None] == before[:, None, :]) & (places[None, :] > places[:, None])
        gap = jnp.broadcast_to(places[None, :] - 1 - places[:, None], (mb, nh, nh))
    else:
        to_total = factor(at_group == last[:, None], jnp.broadcast_to(nh - 1 - places, (mb, nh)))
        group_same = (before_group[:, None] == group_last) & (groups < f)
        group_gap = jnp.broadcast_to((f - 1 - groups) * nh, (mb, nf))
        to_place = factor(before == before_group[:, None], jnp.broadcast_to(places, (mb, nh)))
        same = (before[:, :, None] == at_group[:, None, :]) & (places[None, :] < places[:, None])
        gap = jnp.broadcast_to(places[:, None] - 1 - places[None, :], (mb, nh, nh))
    total = sum(to_total[:, i, :, None, None] * own[i] for i in range(nh))
    totals = wires.spread(total.astype(BF16)).astype(F32)
    from_group = factor(group_same, group_gap)
    outer = sum(from_group[:, i, :, None, None] * totals[i] for i in range(nf))
    between = factor(same, gap)
    result = [
        to_place[:, i, :, None, None] * outer
        + sum(between[:, i, j, :, None, None] * own[j] for j in range(nh) if i != j)
        for i in range(nh)
    ]
    return wires.from_heads(jnp.stack(result).astype(BF16))


def masks(segs, before, last, decay):
    rows = segs.shape[1]
    offsets = jnp.arange(rows, dtype=F32)
    distance = offsets[:, None] - offsets[None, :]
    visible = (segs[:, :, None] == segs[:, None, :]) & (distance >= 0.0)
    within = jnp.where(
        visible[:, None],
        jnp.exp(-decay[:, None, None] * jnp.maximum(distance, 0.0))[None],
        0.0,
    )
    entering = jnp.where(
        (segs == before[:, None])[:, None, :],
        jnp.exp(-decay[:, None] * (offsets + 1.0))[None],
        0.0,
    )
    leaving = jnp.where(
        (segs == last[:, None])[:, None, :],
        jnp.exp(-decay[:, None] * (rows - 1.0 - offsets))[None],
        0.0,
    )
    return within, entering[..., None], leaving[..., None]


def local_any(
    tokens,
    cotangent,
    lengths,
    decay_rate,
    query_weight,
    key_weight,
    value_weight,
    gate_weight,
    out_weight,
    first_weight,
    second_weight,
    down_weight,
):
    wires = Wires()
    mb, chunk, width = tokens.shape
    rows = mb * chunk
    place = wires.f * wires.nh + wires.h
    count = wires.nf * wires.nh

    mix_weights = wires.gather(
        jnp.concatenate([query_weight, key_weight, value_weight, gate_weight], axis=1)
    )
    out_full = wires.gather(out_weight)
    gate_up = wires.gather(jnp.concatenate([first_weight, second_weight], axis=1))
    down_t = wires.gather(down_weight.T)
    hidden_size = down_t.shape[1]

    positions = place * chunk + jnp.arange(chunk, dtype=jnp.int32)
    cosine, sine_vals = rotation_tables(positions, DH)
    cosine, sine_vals = jnp.tile(cosine, (mb, 1, 1)), jnp.tile(sine_vals, (mb, 1, 1))
    seq_ends = jnp.cumsum(lengths, axis=1)
    segs = jnp.sum((seq_ends[:, None, :] <= positions[None, :, None]).astype(jnp.int32), axis=2)
    marks = (jnp.arange(count, dtype=jnp.int32) + 1) * chunk - 1
    ends = jnp.sum((seq_ends[:, None, :] <= marks[None, :, None]).astype(jnp.int32), axis=2)
    last = lax.dynamic_index_in_dim(ends, place, 1, False)
    before = jnp.where(
        place > 0, lax.dynamic_index_in_dim(ends, jnp.maximum(place - 1, 0), 1, False), 0
    )
    within, entering, leaving = masks(segs, before, last, decay_rate)

    def heads(values):
        return values.reshape(mb, chunk, H, DH).transpose(0, 2, 1, 3)

    def flat(values):
        return values.transpose(0, 2, 1, 3).reshape(rows, H * DH)

    def mm(spec, a, b):
        return jnp.einsum(spec, a.astype(BF16), b.astype(BF16), preferred_element_type=F32)

    inputs = tokens.reshape(rows, width).astype(F32)
    normed_in, scale_in = norm_parts(inputs)
    act_rel = wires.rel(normed_in.astype(BF16))
    mixed_pre = dot(act_rel, mix_weights)
    query_pre = mixed_pre[:, :width]
    key_pre = mixed_pre[:, width : 2 * width]
    value_low = mixed_pre[:, 2 * width : 3 * width].astype(BF16)
    gate_vals = mixed_pre[:, 3 * width :]

    def turned(values):
        return rotate_pairs(jax.nn.silu(values).reshape(rows, H, DH), cosine, sine_vals).astype(BF16)

    query_h = heads(turned(query_pre))
    key_h = heads(turned(key_pre))
    value_h = heads(value_low)
    local_state = mm("mhtd,mhte->mhde", key_h * leaving, value_h)
    state_in = chain(wires, local_state, ends, decay_rate, chunk, False)
    scores = (mm("mhsd,mhtd->mhst", query_h, key_h) * within).astype(BF16)
    attended = mm("mhst,mhte->mhse", scores, value_h)
    attended = attended + entering * mm("mhsd,mhde->mhse", query_h, state_in)
    attended = flat(attended.astype(BF16))

    normed_att, scale_att = norm_parts(attended.astype(F32))
    gated_rel = wires.rel((normed_att * gate_vals).astype(BF16))
    hidden = inputs + dot(gated_rel, out_full)
    normed_mid, scale_mid = norm_parts(hidden)
    mid_rel = wires.rel(normed_mid.astype(BF16))
    pre = dot(mid_rel, gate_up)
    first_pre, second_pre = pre[:, :hidden_size], pre[:, hidden_size:]
    product = (first_pre * second_pre).astype(BF16)
    mixed = (hidden + wires.rel(dot_cols(product, down_t))).astype(BF16)

    grad_low = cotangent.reshape(rows, width)
    grad_rel = wires.rel(grad_low)
    share_down = wires.reduce(dot_rows(grad_rel, product)).T
    grad_prod = dot(grad_rel, down_t)
    grad_pre = jnp.concatenate(
        [(grad_prod * second_pre).astype(BF16), (grad_prod * first_pre).astype(BF16)], axis=1
    )
    share_up = wires.reduce(dot_rows(mid_rel, grad_pre))
    grad_mid = wires.rel(dot_cols(grad_pre, gate_up))
    grad_hidden = grad_low.astype(F32) + norm_back(grad_mid, normed_mid, scale_mid)
    grad_hidden_low = grad_hidden.astype(BF16)
    share_out = wires.reduce(dot_rows(gated_rel, grad_hidden_low))
    grad_gated = wires.rel(dot_cols(grad_hidden_low, out_full))
    grad_gate_low = (grad_gated * normed_att).astype(BF16)
    grad_att = heads(norm_back(grad_gated * gate_vals, normed_att, scale_att).astype(BF16))

    grad_state = mm("mhsd,mhse->mhde", query_h * entering, grad_att)
    grad_end = chain(wires, grad_state, ends, decay_rate, chunk, True)
    grad_scores = (mm("mhse,mhte->mhst", grad_att, value_h) * within).astype(BF16)
    grad_q = mm("mhst,mhtd->mhsd", grad_scores, key_h)
    grad_q = grad_q + entering * mm("mhse,mhde->mhsd", grad_att, state_in)
    grad_k = mm("mhst,mhsd->mhtd", grad_scores, query_h)
    grad_k = grad_k + leaving * mm("mhte,mhde->mhtd", value_h, grad_end)
    grad_v = mm("mhst,mhse->mhte", scores, grad_att)
    grad_v = grad_v + leaving * mm("mhtd,mhde->mhte", key_h, grad_end)

    def turned_back(values, pre_values):
        back = flat(values.astype(BF16)).astype(F32).reshape(rows, H, DH)
        back = rotate_pairs(back, cosine, -sine_vals).reshape(rows, width)
        return (silu_slope(pre_values) * back).astype(BF16)

    grad_mix = jnp.concatenate(
        [
            turned_back(grad_q, query_pre),
            turned_back(grad_k, key_pre),
            flat(grad_v.astype(BF16)),
            grad_gate_low,
        ],
        axis=1,
    )
    share_mix = wires.reduce(dot_rows(act_rel, grad_mix))
    grad_act = wires.rel(dot_cols(grad_mix, mix_weights))
    grad_tokens = (grad_hidden + norm_back(grad_act, normed_in, scale_in)).astype(BF16)
    return (
        mixed.reshape(mb, chunk, width),
        grad_tokens.reshape(mb, chunk, width),
        share_mix[:, :width],
        share_mix[:, width : 2 * width],
        share_mix[:, 2 * width : 3 * width],
        share_mix[:, 3 * width :],
        share_out,
        share_up[:, :hidden_size],
        share_up[:, hidden_size:],
        share_down,
    )


def flip(index, bit):
    return index + bit - 2 * bit * ((index // bit) % 2)


def kdot(a, b, dims=((1,), (0,))):
    return lax.dot_general(a, b, (dims, ((), ())), preferred_element_type=F32)


def cols(start, size):
    return pl.ds(pl.multiple_of(start, 128), size)


class Place:
    def __init__(self):
        self.f = lax.axis_index("fsdp")
        self.z = lax.axis_index("head")
        self.fc, self.fx, self.fy = (flip(self.f, b) for b in (1, 2, 4))
        self.fxy = flip(self.fx, 4)
        self.zs = [flip(self.z, 1), flip(self.z, 2), flip(flip(self.z, 1), 2)]

    def at(self, f=None, z=None):
        return {"fsdp": self.f if f is None else f, "head": self.z if z is None else z}

    def greet(self):
        barrier = pltpu.get_barrier_semaphore()
        others = [self.at(f=f) for f in (self.fc, self.fx, self.fy, self.fxy)]
        others += [self.at(z=z) for z in self.zs]
        for other in others:
            pl.semaphore_signal(barrier, inc=1, device_id=other, device_id_type=MESH)
        pl.semaphore_wait(barrier, len(others))


class Weigh:
    def __init__(self, place, lengths, decay, chunk, backward):
        self.p, self.decay, self.chunk, self.backward = place, decay, chunk, backward
        self.sums = []
        for m in range(2):
            total, row = 0, []
            for j in range(lengths.shape[1]):
                total = total + lengths[m, j]
                row.append(total)
            self.sums.append(row)
        first = 4 * place.f
        self.ends = [[self.end(m, first + i) for i in range(-1, 4)] for m in range(2)]
        self.groups = [[self.end(m, 4 * g + 3) for g in range(8)] for m in range(2)]
        own = first + place.z
        self.before = [self.end(m, own - 1) for m in range(2)]
        self.last = [self.end(m, own) for m in range(2)]

    def end(self, m, i):
        position = (i + 1) * self.chunk - 1
        return sum(jnp.where(total <= position, 1, 0) for total in self.sums[m])

    def tables(self, cosine, sine, seg_col, seg_row):
        chunk = self.chunk
        base = (4 * self.p.f + self.p.z) * chunk
        shape = (chunk, DH)
        lane = lax.broadcasted_iota(jnp.int32, shape, 1)
        row = lax.broadcasted_iota(jnp.int32, shape, 0) + base
        half = DH // 2
        turn = lane % half
        speed = jnp.right_shift(jnp.full(shape, 651, jnp.int32), turn * 10 // half) + 1
        angle = ((row * speed) % 4096).astype(F32) * (2.0 * math.pi / 4096.0)
        cos, sin = jnp.cos(angle), jnp.sin(angle)
        sin = jnp.where(lane < half, -sin, sin)
        down = lax.broadcasted_iota(jnp.int32, (chunk, 1), 0) + base
        across = lax.broadcasted_iota(jnp.int32, (1, chunk), 1) + base
        for m in range(2):
            at = slice(m * chunk, (m + 1) * chunk)
            cosine[at, :] = cos
            sine[at, :] = sin
            seg_col[at, :] = sum(jnp.where(total <= down, 1, 0) for total in self.sums[m])
            seg_row[m : m + 1, :] = sum(jnp.where(total <= across, 1, 0) for total in self.sums[m])

    def power(self, same, chunks, hh):
        rate = self.decay[2 * self.p.z + hh]
        gap = jnp.asarray(chunks * self.chunk, jnp.int32).astype(F32)
        value = jnp.exp(jnp.full((1, DH), -rate * gap, F32))
        return jnp.where(same, value, 0.0)

    def to_total(self, m, i, hh):
        ends = self.ends[m]
        if self.backward:
            return self.power(ends[i] == ends[0], i, hh)
        return self.power(ends[i + 1] == ends[4], 3 - i, hh)

    def to_place(self, m, i, hh):
        ends = self.ends[m]
        if self.backward:
            return self.power(ends[i + 1] == ends[4], 3 - i, hh)
        return self.power(ends[i] == ends[0], i, hh)

    def from_group(self, m, g, hh):
        f = self.p.f
        if self.backward:
            before = self.groups[m][g - 1] if g > 0 else 0
            same = (self.ends[m][4] == before) & (g > f)
            return self.power(same, 4 * jnp.maximum(g - 1 - f, 0), hh)
        same = (self.ends[m][0] == self.groups[m][g]) & (g < f)
        return self.power(same, 4 * jnp.maximum(f - 1 - g, 0), hh)

    def others(self, i):
        return range(i + 1, 4) if self.backward else range(i)

    def between(self, m, i, j, hh):
        ends = self.ends[m]
        if self.backward:
            return self.power(ends[i + 1] == ends[j], j - 1 - i, hh)
        return self.power(ends[i] == ends[j + 1], i - 1 - j, hh)


class Scan:
    def __init__(self, place, weigh, states, inbox, totals, outbox, result, send, recv):
        self.p, self.weigh = place, weigh
        self.states, self.inbox, self.totals = states, inbox, totals
        self.outbox, self.result = outbox, result
        self.send, self.recv = send, recv

    def copy(self, src, dst, n, where):
        return pltpu.make_async_remote_copy(
            src_ref=src,
            dst_ref=dst,
            send_sem=self.send.at[n],
            recv_sem=self.recv.at[n],
            device_id=where,
            device_id_type=MESH,
        )

    def to_heads(self, i):
        z = self.p.zs[i]
        return self.copy(self.states.at[pl.ds(2 * z, 2)], self.inbox.at[self.p.z], i, self.p.at(z=z))

    def from_heads(self, i):
        z = self.p.zs[i]
        return self.copy(
            self.outbox.at[z], self.result.at[pl.ds(2 * self.p.z, 2)], 9 + i, self.p.at(z=z)
        )

    def total(self, n, origin, where):
        return self.copy(self.totals.at[origin], self.totals.at[origin], n, self.p.at(f=where))

    def start(self):
        p = self.p
        for i in range(3):
            self.to_heads(i).start()
        self.inbox[p.z] = self.states[pl.ds(2 * p.z, 2)]

    def totals_out(self):
        p = self.p
        for i in range(3):
            self.to_heads(i).wait()
        for hh in range(2):
            for m in range(2):
                acc = sum(
                    self.weigh.to_total(m, i, hh) * self.inbox[i, hh, m].astype(F32)
                    for i in range(4)
                )
                self.totals[p.f, hh, m] = acc.astype(BF16)
        for n, where in ((3, p.fx), (4, p.fy), (5, p.fxy)):
            self.total(n, p.f, where).start()
        self.total(12, p.f, p.fc).start()

    def forward(self):
        p = self.p
        for n, where in ((3, p.fx), (4, p.fy), (5, p.fxy)):
            self.total(n, p.f, where).wait()
            self.total(n + 3, where, p.fc).start()

    def results_out(self):
        p = self.p
        self.total(12, p.f, p.fc).wait()
        for n, where in ((3, p.fx), (4, p.fy), (5, p.fxy)):
            self.total(n + 3, where, p.fc).wait()
        for hh in range(2):
            for m in range(2):
                outer = sum(
                    self.weigh.from_group(m, g, hh) * self.totals[g, hh, m].astype(F32)
                    for g in range(8)
                )
                for i in range(4):
                    acc = self.weigh.to_place(m, i, hh) * outer
                    for j in self.weigh.others(i):
                        acc += self.weigh.between(m, i, j, hh) * self.inbox[j, hh, m].astype(F32)
                    self.outbox[i, hh, m] = acc.astype(BF16)
        for i in range(3):
            self.from_heads(i).start()
        self.result[pl.ds(2 * p.z, 2)] = self.outbox[p.z]

    def finish(self):
        for i in range(3):
            self.from_heads(i).wait()


def edge(seg, mark, rate, gap):
    return jnp.where(seg == mark, jnp.exp(-rate * gap), 0.0)


def decays(rate, rows):
    up = lax.broadcasted_iota(jnp.int32, (rows, rows), 0)
    across = lax.broadcasted_iota(jnp.int32, (rows, rows), 1)
    gap = (up - across).astype(F32)
    return jnp.where(gap >= 0.0, jnp.exp(-rate * jnp.maximum(gap, 0.0)), 0.0)


def up_tile(a2, w1, w2, s, dp1, dp2, t):
    at = cols(t * TILE, TILE)
    first = kdot(a2[...], w1[:, at])
    second = kdot(a2[...], w2[:, at])
    ds = dp1[:, at].astype(F32)
    s[:, at] = (first * second).astype(BF16)
    dp1[:, at] = (ds * second).astype(BF16)
    dp2[:, at] = (ds * first).astype(BF16)


def forward_kernel(
    lengths, decay_rate, x, dy,
    wq, wk, wv, wu, wo, w1, w2, wd,
    mix_o, wo_o, w1_o, w2_o, wd_o, q_o, k_o, v_o, u_o, qp_o, kp_o, ob_o, hid_o, dp1_o, dp2_o, s_o,
    state_o, a2_o, a1t_o, a2t_o, gt_o, dyt_o,
    fm, fo, f1, f2, fd, a1, q, k, v, u, qp, kp, att, ob, g, hid, dp1, dp2, s,
    cosine, sine, seg_col, seg_row, a1t, a2t, gt, dyt, states, inbox, totals, outbox, result,
    send, recv, own_sem, save_sem, scan_send, scan_recv,
):
    place = Place()
    f = place.f
    rows, width = x.shape
    chunk = rows // 2
    hidden_size = w1.shape[1]
    half_hidden = hidden_size // 2
    place.greet()

    pieces = []
    for i, w in ((1, wk), (2, wv), (0, wq), (3, wu)):
        pieces.append((w, fm, (0, 128), (0, width), i * width))
    for part in range(2):
        pieces.append((wd, fd, (part * half_hidden, half_hidden), (0, 128), None))
    pieces.append((wo, fo, (0, 128), (0, width), 0))
    for part in range(2):
        for w, full in ((w1, f1), (w2, f2)):
            at = part * half_hidden
            pieces.append((w, full, (0, 128), (at, half_hidden), at))
    count = len(pieces)
    parity = place.z % 2

    def parts(n):
        thin = (3, 2)[n % 2]
        wide = 8 - thin
        near = (wide + (n // 2) % 2) // 2
        fetch = (parity * thin, wide)
        return {
            "all": (0, 8),
            "fetch": fetch,
            "near": (fetch[0], near),
            "far": (fetch[0] + near, wide - near),
            "give": (parity * wide, thin),
            "take": ((1 - parity) * wide, thin),
        }

    def own(n, part="all"):
        w, _, (r, rs), (c, cs), _ = pieces[n]
        at, size = parts(n)[part]
        eighth = rs // 8
        return w.at[pl.ds(pl.multiple_of(r + at * eighth, 16), size * eighth), pl.ds(c, cs)]

    def block(n, origin, part="all"):
        _, full, (r, rs), (c, cs), to = pieces[n]
        at, size = parts(n)[part]
        eighth = rs // 8
        if to is None:
            start = pl.multiple_of(r + at * eighth, 16)
            return full.at[pl.ds(start, size * eighth), cols(origin * 128, 128)]
        start = pl.multiple_of(origin * 128 + at * eighth, 16)
        return full.at[pl.ds(start, size * eighth), pl.ds(to, cs)]

    fc, fx, fy, fxy = place.fc, place.fx, place.fy, place.fxy
    at_c, at_x, at_y = (place.at(f=o) for o in (fc, fx, fy))
    at_z = place.at(z=place.zs[0])

    def step(n, t):
        fetched = own(n, "fetch"), block(n, f, "fetch")
        src, dst, where, lands = [
            (own(n), block(n, f), at_c, (fc, "all")),
            (*fetched, at_x, (fx, "fetch")),
            (*fetched, at_y, (fy, "fetch")),
            (block(n, fx, "near"), None, at_y, (fxy, "near")),
            (block(n, fy, "far"), None, at_x, (fxy, "far")),
            (block(n, fx, "give"), None, at_z, (fx, "take")),
            (block(n, fy, "give"), None, at_z, (fy, "take")),
            (block(n, fxy, "give"), None, at_z, (fxy, "take")),
            (block(n, fx), None, at_c, (flip(fx, 1), "all")),
            (block(n, fy), None, at_c, (flip(fy, 1), "all")),
            (block(n, fxy), None, at_c, (flip(fxy, 1), "all")),
        ][t]
        return src, src if dst is None else dst, where, block(n, *lands)

    def move(n, t, src, dst, where):
        return pltpu.make_async_remote_copy(
            src_ref=src,
            dst_ref=dst,
            send_sem=send.at[n * 11 + t],
            recv_sem=recv.at[n * 11 + t],
            device_id=where,
            device_id_type=MESH,
        )

    def go(n, t):
        src, dst, where, _ = step(n, t)
        move(n, t, src, dst, where).start()

    def got(n, *which):
        for t in which:
            _, _, where, lands = step(n, t)
            move(n, t, lands, lands, where).wait_recv()

    def own_copy(n):
        return pltpu.make_async_copy(own(n), block(n, f), own_sem.at[n])

    saves = []

    def save(src, dst):
        copy = pltpu.make_async_copy(src, dst, save_sem.at[len(saves)])
        copy.start()
        saves.append(copy)

    def save_piece(n):
        full_o = {id(fm): mix_o, id(fo): wo_o, id(f1): w1_o, id(f2): w2_o, id(fd): wd_o}
        _, full, (r, rs), (c, cs), to = pieces[n]
        out = full_o[id(full)]
        if to is None:
            save(full.at[pl.ds(r, rs)], out.at[pl.ds(r, rs)])
        else:
            save(full.at[:, pl.ds(to, cs)], out.at[:, pl.ds(to, cs)])

    def norm_in():
        @pl.loop(0, rows // 128)
        def _(t):
            at = pl.ds(pl.multiple_of(t * 128, 128), 128)
            value = x[at, :].astype(F32)
            scale = lax.rsqrt(jnp.mean(value * value, axis=-1, keepdims=True) + EPSILON)
            a1[at, :] = (value * scale).astype(BF16)

    def turn_over(src, dst):
        @pl.loop(0, width // 128)
        def _(b):
            other_c = (b + f) % 2
            other_x = (b // 2 + f // 2) % 2
            other_y = (b // 4 + f // 4) % 2
            slot = other_c * 4 + other_y * 2 + other_x
            value = src[:, cols(b * 128, 128)].astype(F32)
            dst[pl.ds(pl.multiple_of(slot * 128, 128), 128), :] = value.T.astype(BF16)

    def project(base, pre, low, turn):
        @pl.loop(0, width // TILE)
        def _(t):
            at = cols(t * TILE, TILE)
            acc = kdot(a1[...], fm[:, cols(base + t * TILE, TILE)])
            if not turn:
                low[:, at] = acc.astype(BF16)
                return
            pre[:, at] = acc.astype(BF16)
            acc = acc * lax.logistic(acc)
            turned = []
            for hh in range(TILE // DH):
                piece = acc[:, hh * DH : (hh + 1) * DH]
                turned.append(piece * cosine[...] + pltpu.roll(piece, DH // 2, 1) * sine[...])
            low[:, at] = jnp.concatenate(turned, axis=1).astype(BF16)

    offset = lax.broadcasted_iota(jnp.int32, (chunk, 1), 0).astype(F32)
    weigh = Weigh(place, lengths, decay_rate, chunk, False)
    scan = Scan(place, weigh, states, inbox, totals, outbox, result, scan_send, scan_recv)

    def local_states():
        @pl.loop(0, H)
        def _(h):
            at = cols(h * DH, DH)
            for m in range(2):
                r = slice(m * chunk, (m + 1) * chunk)
                leaving = edge(seg_col[r], weigh.last[m], decay_rate[h], chunk - 1.0 - offset)
                left = (k[r, at].astype(F32) * leaving).astype(BF16)
                states[h, m] = kdot(left, v[r, at], ((0,), (0,))).astype(BF16)

    def attend_local(first, last):
        @pl.loop(first, last)
        def _(h):
            at = cols(h * DH, DH)
            decay = decays(decay_rate[h], chunk)
            for m in range(2):
                r = slice(m * chunk, (m + 1) * chunk)
                within = jnp.where(seg_col[r] == seg_row[m : m + 1], decay, 0.0)
                scores = kdot(q[r, at], k[r, at], ((1,), (1,))) * within
                att[r, at] = kdot(scores.astype(BF16), v[r, at])

    def attend_rest():
        @pl.loop(0, H)
        def _(h):
            at = cols(h * DH, DH)
            for m in range(2):
                r = slice(m * chunk, (m + 1) * chunk)
                entering = edge(seg_col[r], weigh.before[m], decay_rate[h], offset + 1.0)
                ob[r, at] = (att[r, at] + entering * kdot(q[r, at], result[h, m])).astype(BF16)

    def hidden():
        @pl.loop(0, rows // 128)
        def _(t):
            at = pl.ds(pl.multiple_of(t * 128, 128), 128)
            value = ob[at, :].astype(F32)
            scale = lax.rsqrt(jnp.mean(value * value, axis=-1, keepdims=True) + EPSILON)
            g[at, :] = (value * scale * u[at, :].astype(F32)).astype(BF16)

        turn_over(g, gt)
        save(gt, gt_o)

        @pl.loop(0, width // TILE)
        def _(t):
            at = cols(t * TILE, TILE)
            hid[:, at] = x[:, at].astype(F32) + kdot(g[...], fo[:, at])

        @pl.loop(0, rows // 128)
        def _(t):
            at = pl.ds(pl.multiple_of(t * 128, 128), 128)
            value = hid[at, :]
            scale = lax.rsqrt(jnp.mean(value * value, axis=-1, keepdims=True) + EPSILON)
            g[at, :] = (value * scale).astype(BF16)

    def inner(part):
        @pl.loop(0, half_hidden // 128)
        def _(t):
            start = part * half_hidden + t * 128
            rhs = fd[pl.ds(pl.multiple_of(start, 128), 128), :]
            dp1[:, cols(start, 128)] = kdot(dy[...], rhs, ((1,), (1,))).astype(BF16)

    def up():
        @pl.loop(0, half_hidden // TILE)
        def _(t):
            up_tile(g, f1, f2, s, dp1, dp2, t)

    def work(n):
        if n == 0:
            project(width, kp, k, True)
            save(k, k_o)
            save(kp, kp_o)
        elif n == 1:
            project(2 * width, None, v, False)
            local_states()
            scan.start()
            save(v, v_o)
        elif n == 2:
            project(0, qp, q, True)
            save(q, q_o)
            save(qp, qp_o)
        elif n == 3:
            project(3 * width, None, u, False)
            save(u, u_o)
            scan.totals_out()
        elif n == 4:
            attend_local(0, H // 2)
            scan.forward()
        elif n == 5:
            attend_local(H // 2, H)
            scan.results_out()
        elif n == 6:
            inner(0)
            inner(1)
        elif n == 7:
            scan.finish()
            save(result, state_o)
            attend_rest()
            save(ob, ob_o)
            hidden()
            save(hid, hid_o)
            save(g, a2_o)
        elif n == 8:
            up()
            done = pl.ds(0, half_hidden // TILE * TILE)
            save(s.at[:, done], s_o.at[:, done])
            save(dp1, dp1_o)
            save(dp2.at[:, done], dp2_o.at[:, done])
        elif n == 9:
            turn_over(g, a2t)
            save(a2t, a2t_o)

    def early(n):
        if n == 0:
            turn_over(dy, dyt)
            save(dyt, dyt_o)
        elif n == 1:
            turn_over(a1, a1t)
            save(a1t, a1t_o)

    ahead = 2
    for n in range(ahead):
        for t in (1, 2, 0):
            go(n, t)
        own_copy(n).start()
    weigh.tables(cosine, sine, seg_col, seg_row)
    norm_in()
    for n in range(count + 3):
        if n < count:
            got(n, 1)
            go(n, 3)
            go(n, 5)
            got(n, 2)
            go(n, 4)
            go(n, 6)
            if n + ahead < count:
                for t in (1, 2, 0):
                    go(n + ahead, t)
                own_copy(n + ahead).start()
        if 0 <= n - 1 < count:
            got(n - 1, 3, 4)
            go(n - 1, 7)
            got(n - 1, 5)
            go(n - 1, 8)
            got(n - 1, 6)
            go(n - 1, 9)
        if 0 <= n - 2 < count:
            got(n - 2, 7)
            go(n - 2, 10)
        if n - 3 >= 0:
            got(n - 3, 0, 8, 9, 10)
            own_copy(n - 3).wait()
            save_piece(n - 3)
            work(n - 3)
        else:
            early(n)
    for n in range(count):
        for t in range(11):
            src, dst, where, _ = step(n, t)
            move(n, t, src, dst, where).wait_send()
    for copy in saves:
        copy.wait()


def run_forward(lengths, decay_rate, x, dy, weights):
    rows, width = x.shape
    hidden_size = weights[5].shape[1]
    row = jax.ShapeDtypeStruct((rows, width), BF16)
    tall = jax.ShapeDtypeStruct((rows, hidden_size), BF16)
    outs = (
        [
            jax.ShapeDtypeStruct(shape, BF16)
            for shape in (
                (width, 4 * width), (width, width), (width, hidden_size), (width, hidden_size),
                (hidden_size, width),
            )
        ]
        + [row] * 7
        + [jax.ShapeDtypeStruct((rows, width), F32)]
        + [tall] * 3
        + [jax.ShapeDtypeStruct((H, 2, DH, DH), BF16), row]
        + [jax.ShapeDtypeStruct((width, rows), BF16)] * 4
    )
    rv = pltpu.VMEM((rows, width), BF16)
    tv = pltpu.VMEM((rows, hidden_size), BF16)
    scratch = (
        [pltpu.VMEM(o.shape, BF16) for o in outs[:5]]
        + [rv] * 7
        + [pltpu.VMEM((rows, width), F32), rv, rv, pltpu.VMEM((rows, width), F32)]
        + [tv] * 3
        + table_scratch(rows)
        + [pltpu.VMEM((width, rows), BF16)] * 4
        + scan_scratch()
        + [pltpu.SemaphoreType.DMA((121,))] * 2
        + [pltpu.SemaphoreType.DMA((11,)), pltpu.SemaphoreType.DMA((28,))]
        + [pltpu.SemaphoreType.DMA((13,))] * 2
    )
    return pl.pallas_call(
        forward_kernel,
        out_shape=outs,
        in_specs=[SMEM, SMEM] + [VMEM] * 2 + [ANY] * 8,
        out_specs=[ANY] * len(outs),
        scratch_shapes=scratch,
        compiler_params=pltpu.CompilerParams(
            collective_id=0, has_side_effects=True, vmem_limit_bytes=VMEM_BYTES
        ),
        name="forward",
    )(lengths, decay_rate, x, dy, *weights)


def table_scratch(rows):
    return [
        pltpu.VMEM((rows, DH), F32),
        pltpu.VMEM((rows, DH), F32),
        pltpu.VMEM((rows, 1), jnp.int32),
        pltpu.VMEM((2, rows // 2), jnp.int32),
    ]


def scan_scratch():
    return [
        pltpu.VMEM((H, 2, DH, DH), BF16),
        pltpu.VMEM((4, 2, 2, DH, DH), BF16),
        pltpu.VMEM((8, 2, 2, DH, DH), BF16),
        pltpu.VMEM((4, 2, 2, DH, DH), BF16),
        pltpu.VMEM((H, 2, DH, DH), BF16),
    ]


UPRIGHT = 256
LAG = 2
WITH_UPRIGHT = (0, 1, 2, 3, 10, 11, 12, 13)
LAST = 1024


def backward_kernel(
    lengths, decay_rate,
    x_i, dy_i, wm_i, wo_i, w1_i, w2_i, wd_i, q_i, k_i, v_i, u_i, qp_i, kp_i, ob_i, hid_i,
    p1_i, p2_i, s_i, state_i, a2_i, a1t_i, a2t_i, gt_i, dyt_i,
    mixed_o, grad_x_o, gq_o, gk_o, gv_o, gu_o, go_o, g1_o, g2_o, gd_o,
    wd, w1, w2, s, p1, p2, dy, hid, dh, dz, ob, u, q, k, v, dqp, dkp, dv, state_in,
    cosine, sine, seg_col, seg_row, a1t, a2t, gt, dyt, states, inbox, totals, outbox, result,
    give, take, merged, take_a, take_b, half_a, half_b, take2, mine, take3, pair, take4, final,
    z_take, z_sum, z_take2, z_sum2, z_take_a, z_take_b, z_half_a, z_half_b, z_take3,
    send, recv, free, load_sem, out_sem, scan_send, scan_recv,
):
    place = Place()
    rows, width = dy.shape
    chunk = rows // 2
    hidden_size = s.shape[1]
    place.greet()

    loads = {}

    def load(name, src, dst):
        copy = pltpu.make_async_copy(src, dst, load_sem.at[len(loads)])
        copy.start()
        loads[name] = copy

    def ready(*names):
        for name in names:
            loads[name].wait()

    done = pl.ds(0, hidden_size // 2 // TILE * TILE)
    for name, src, dst in (
        ("dyt", dyt_i, dyt), ("s", s_i.at[:, done], s.at[:, done]), ("a2t", a2t_i, a2t), ("p1", p1_i, p1),
        ("p2", p2_i.at[:, done], p2.at[:, done]), ("a2", a2_i, dkp), ("w1", w1_i, w1), ("w2", w2_i, w2),
        ("hid", hid_i, hid), ("wd", wd_i, wd), ("dy", dy_i, dy), ("ob", ob_i, ob), ("u", u_i, u), ("q", q_i, q), ("gt", gt_i, gt),
        ("k", k_i, k), ("v", v_i, v), ("state", state_i, state_in), ("a1t", a1t_i, a1t),
    ):
        load(name, src, dst)

    pieces = []
    for start in range(0, hidden_size, 1024):
        size = min(1024, hidden_size - start)
        for left, right, out in ((dyt, s, gd_o), (a2t, p1, g1_o), (a2t, p2, g2_o)):
            pieces.append((left, right, out, start, size))
    for left, right, out in ((gt, dz, go_o), (a1t, u, gu_o), (a1t, dqp, gq_o), (a1t, dkp, gk_o)):
        pieces.append((left, right, out, 0, width))
    for start in range(0, width, LAST):
        pieces.append((a1t, dv, gv_o, start, LAST))
    count = len(pieces)
    steps = count + 1 + 4 * LAG
    low, high = place.z % 2, place.z // 2
    f = place.f
    at_c, at_x, at_y = (place.at(f=o) for o in (place.fc, place.fx, place.fy))
    at_z1, at_z2 = (place.at(z=place.zs[i]) for i in range(2))
    partner = [at_c, at_x, at_y, at_y, at_x, at_z1, at_z2]
    partner += [at_z1, at_z2, at_x, at_y, at_y, at_x]
    quarter_size = UPRIGHT // 2
    lo, hi = pl.ds(0, quarter_size), pl.ds(quarter_size, quarter_size)

    def upright(n):
        return n in WITH_UPRIGHT

    def half_of(n):
        return (pieces[n][4] - UPRIGHT * upright(n)) // 2

    def of(n, *which):
        return [t for t in which if t < 7 or upright(n)]

    def move(n, t):
        size = pieces[n][4]
        c, m, half = n % 2, n % 3, half_of(n)
        a, b, ab, last = (pl.ds(*at) for at in ((0, half), (half, half), (0, 2 * half), (2 * half, UPRIGHT)))
        src, dst = [
            lambda: (give.at[c, :, pl.ds(0, size)], take.at[c, :, pl.ds(0, size)]),
            lambda: (merged.at[m, :, 1, :, :, :, a], take_a.at[m, :, :, :, :, a]),
            lambda: (merged.at[m, 1, :, :, :, :, b], take_b.at[m, :, :, :, :, a]),
            lambda: (half_a.at[m, 1, :, :, :, a], take2.at[m, 0, :, :, :, a]),
            lambda: (half_b.at[m, 1, :, :, :, a], take2.at[m, 1, :, :, :, a]),
            lambda: (mine.at[m, :, 1 - low, :, ab], take3.at[m, :, :, ab]),
            lambda: (pair.at[m, 1 - high, :, ab], take4.at[m, :, ab]),
            lambda: (merged.at[m, :, :, :, 1 - low, :, last], z_take.at[m]),
            lambda: (z_sum.at[m, :, :, 1 - high], z_take2.at[m]),
            lambda: (z_sum2.at[m, :, 1, :, lo], z_take_a.at[m]),
            lambda: (z_sum2.at[m, 1, :, :, hi], z_take_b.at[m]),
            lambda: (z_half_a.at[m, 1], z_take3.at[m, 0]),
            lambda: (z_half_b.at[m, 1], z_take3.at[m, 1]),
        ][t]()
        return pltpu.make_async_remote_copy(
            src_ref=src,
            dst_ref=dst,
            send_sem=send.at[3 * t + m],
            recv_sem=recv.at[3 * t + m],
            device_id=partner[t],
            device_id_type=MESH,
        )

    def go(n, t):
        move(n, t).start()

    def reuse(n, *which):
        for t in which:
            earlier = n - (2 if t == 0 else 3)
            if earlier >= 0 and of(earlier, t):
                move(earlier, t).wait_send()

    def got(n, t):
        move(n, t).wait_recv()

    near = (at_c, at_x, at_y, at_z1, at_z2)

    def freed(n):
        if n < steps - 1:
            for i, where in enumerate(near):
                pl.semaphore_signal(free.at[i], 1, device_id=where, device_id_type=MESH)

    def allowed(n):
        if n >= 1:
            for i in range(len(near)):
                pl.semaphore_wait(free.at[i], 1)

    def give_half(n):
        left, right, _, start, size = pieces[n]
        slot = n % 2
        reuse(n, 0)

        @pl.loop(0, size // TILE)
        def _(t):
            value = kdot(left[rows : 2 * rows, :], right[:, cols(start + t * TILE, TILE)])
            give[slot, :, cols(t * TILE, TILE)] = value.astype(BF16)


    def merge(n):
        left, right, _, start, size = pieces[n]
        slot, m = n % 2, n % 3
        got(n, 0)
        reuse(n, 1, 2, 7)

        @pl.loop(0, size // TILE)
        def _(t):
            at = cols(t * TILE, TILE)
            value = kdot(left[0:rows, :], right[:, cols(start + t * TILE, TILE)])
            value = (value + take[slot, :, at].astype(F32)).astype(BF16)
            for i in range(16):
                r = i * 32
                merged[m, i // 8, i // 4 % 2, i // 2 % 2, i % 2, :, at] = value[r : r + 32]

        for t in of(n, 1, 2, 7):
            go(n, t)

    def add(a, b):
        return a.astype(F32) + b.astype(F32)

    def halve(n):
        m, half = n % 3, half_of(n)
        reuse(n, 8)
        if upright(n):
            got(n, 7)
            c = slice(2 * half, 2 * half + UPRIGHT)
            for y in range(2):
                z_sum[m, y] = add(merged[m, y, :, :, low, :, c], z_take[m, y]).astype(BF16)
            go(n, 8)
        got(n, 1)
        reuse(n, 3)
        for i in (1, 0):
            half_a[m, i, :, :, :, :half] = add(
                merged[m, i, 0, :, :, :, :half], take_a[m, i, :, :, :, :half]
            ).astype(BF16)
        go(n, 3)
        got(n, 2)
        reuse(n, 4)
        for i in (1, 0):
            half_b[m, i, :, :, :, :half] = add(
                merged[m, 0, i, :, :, :, half : 2 * half], take_b[m, i, :, :, :, :half]
            ).astype(BF16)
        go(n, 4)

    def quarter(n):
        m, half = n % 3, half_of(n)
        reuse(n, 9, 10)
        if upright(n):
            got(n, 8)
            z_sum2[m] = add(z_sum[m, :, :, high], z_take2[m]).astype(BF16)
            go(n, 9)
            go(n, 10)
        reuse(n, 5)
        for t, kept, at in ((3, half_a, slice(0, half)), (4, half_b, slice(half, 2 * half))):
            got(n, t)
            mine[m, :, :, :, at] = add(
                kept[m, 0, :, :, :, :half], take2[m, t - 3, :, :, :, :half]
            ).astype(BF16)
        go(n, 5)

    def along(n):
        m, whole = n % 3, 2 * half_of(n)
        reuse(n, 11, 12)
        if upright(n):
            got(n, 9)
            z_half_a[m] = add(z_sum2[m, :, 0, :, :quarter_size], z_take_a[m]).astype(BF16)
            go(n, 11)
            got(n, 10)
            z_half_b[m] = add(z_sum2[m, 0, :, :, quarter_size:], z_take_b[m]).astype(BF16)
            go(n, 12)
        got(n, 5)
        reuse(n, 6)
        for i in range(2):
            pair[m, i, :, :whole] = add(
                mine[m, i, low, :, :whole], take3[m, i, :, :whole]
            ).astype(BF16)
        go(n, 6)

    def final_copy(n):
        _, _, out, start, size = pieces[n]
        m = n % 3
        return pltpu.make_async_copy(
            final.at[m, :, pl.ds(0, size)], out.at[:, pl.ds(start, size)], out_sem.at[m]
        )

    def end(n):
        m, whole = n % 3, 2 * half_of(n)
        if n >= 3:
            final_copy(n - 3).wait()
        for t in of(n, 11, 12):
            i, kept = t - 11, (z_half_a, z_half_b)[t - 11]
            got(n, t)
            at = slice(whole + i * quarter_size, whole + (i + 1) * quarter_size)
            final[m, :, at] = add(kept[m, 0], z_take3[m, i])
        got(n, 6)
        final[m, :, :whole] = add(pair[m, high, :, :whole], take4[m, :, :whole])
        final_copy(n).start()

    offset = lax.broadcasted_iota(jnp.int32, (chunk, 1), 0).astype(F32)
    weigh = Weigh(place, lengths, decay_rate, chunk, True)
    scan = Scan(place, weigh, states, inbox, totals, outbox, result, scan_send, scan_recv)

    def row_tiles(body):
        @pl.loop(0, rows // 128)
        def _(t):
            body(pl.ds(pl.multiple_of(t * 128, 128), 128))

    def up():
        ready("a2", "w1", "w2")

        @pl.loop(hidden_size // 2 // TILE, hidden_size // TILE)
        def _(t):
            up_tile(dkp, w1, w2, s, p1, p2, t)

    def mix():
        ready("wd")

        @pl.loop(0, width // TILE)
        def _(t):
            at = cols(t * TILE, TILE)
            dqp[:, at] = (hid[:, at] + kdot(s[...], wd[:, at])).astype(BF16)

        load("mixed", dqp, mixed_o)
        load("wo", wo_i, wd.at[pl.ds(0, width)])

    def middle(first, last):
        @pl.loop(first, last)
        def _(t):
            r = pl.ds(pl.multiple_of(t * TILE, TILE), TILE)
            dh[:, cols(t * TILE, TILE)] = kdot(p1[...], w1[r, :], ((1,), (1,))) + kdot(
                p2[...], w2[r, :], ((1,), (1,))
            )

    def middle_rows():
        ready("dy")
        load("wq", wm_i.at[:, pl.ds(0, 2 * width)], w1.at[:, pl.ds(0, 2 * width)])
        load("wv", wm_i.at[:, pl.ds(2 * width, 2 * width)], w2.at[:, pl.ds(0, 2 * width)])

        def body(at):
            value = hid[at, :]
            scale = lax.rsqrt(jnp.mean(value * value, axis=-1, keepdims=True) + EPSILON)
            normed = value * scale
            grad = dh[at, :]
            mean = jnp.mean(grad * normed, axis=-1, keepdims=True)
            grad = dy[at, :].astype(F32) + scale * (grad - normed * mean)
            dh[at, :] = grad
            dz[at, :] = grad.astype(BF16)

        row_tiles(body)
        load("x", x_i, dy)

    def outer():
        ready("wo", "ob", "u")

        @pl.loop(0, width // TILE)
        def _(t):
            r = pl.ds(pl.multiple_of(t * TILE, TILE), TILE)
            hid[:, cols(t * TILE, TILE)] = kdot(dz[...], wd[r, :], ((1,), (1,)))

        def body(at):
            value = ob[at, :].astype(F32)
            scale = lax.rsqrt(jnp.mean(value * value, axis=-1, keepdims=True) + EPSILON)
            normed = value * scale
            grad = hid[at, :]
            dm = grad * u[at, :].astype(F32)
            u[at, :] = (grad * normed).astype(BF16)
            mean = jnp.mean(dm * normed, axis=-1, keepdims=True)
            ob[at, :] = (scale * (dm - normed * mean)).astype(BF16)

        row_tiles(body)

        @pl.loop(0, H)
        def _(h):
            at = cols(h * DH, DH)
            for m in range(2):
                r = slice(m * chunk, (m + 1) * chunk)
                entering = edge(seg_col[r], weigh.before[m], decay_rate[h], offset + 1.0)
                left = (q[r, at].astype(F32) * entering).astype(BF16)
                states[h, m] = kdot(left, ob[r, at], ((0,), (0,))).astype(BF16)

        scan.start()

    def slope(pre):
        sig = lax.logistic(pre)
        return sig * (1.0 + pre * (1.0 - sig))

    def turned_back(grad, r, base, h):
        grad = grad.astype(BF16).astype(F32)
        back = grad * cosine[r, :] - pltpu.roll(grad, DH // 2, 1) * sine[r, :]
        return (slope(s[r, cols(base + h * DH, DH)].astype(F32)) * back).astype(BF16)

    def attend_queries(first, last):
        @pl.loop(first, last)
        def _(h):
            at = cols(h * DH, DH)
            decay = decays(decay_rate[h], chunk)
            for m in range(2):
                r = slice(m * chunk, (m + 1) * chunk)
                within = jnp.where(seg_col[r] == seg_row[m : m + 1], decay, 0.0)
                entering = edge(seg_col[r], weigh.before[m], decay_rate[h], offset + 1.0)
                oh = ob[r, at]
                grads = (kdot(oh, v[r, at], ((1,), (1,))) * within).astype(BF16)
                dq = kdot(grads, k[r, at]) + entering * kdot(oh, state_in[h, m], ((1,), (1,)))
                dqp[r, at] = turned_back(dq, r, 0, h)

    def attend_keys(first, last):
        @pl.loop(first, last)
        def _(h):
            at = cols(h * DH, DH)
            decay = decays(decay_rate[h], chunk)
            for m in range(2):
                r = slice(m * chunk, (m + 1) * chunk)
                within = jnp.where(seg_col[r] == seg_row[m : m + 1], decay, 0.0)
                leaving = edge(seg_col[r], weigh.last[m], decay_rate[h], chunk - 1.0 - offset)
                qh, kh, vh, oh = q[r, at], k[r, at], v[r, at], ob[r, at]
                grads = (kdot(oh, vh, ((1,), (1,))) * within).astype(BF16)
                dk = kdot(grads, qh, ((0,), (0,)))
                dk = dk + leaving * kdot(vh, result[h, m], ((1,), (1,)))
                scores = (kdot(qh, kh, ((1,), (1,))) * within).astype(BF16)
                grad_v = kdot(scores, oh, ((0,), (0,))) + leaving * kdot(kh, result[h, m])
                dv[r, at] = grad_v.astype(BF16)
                dkp[r, at] = turned_back(dk, r, width, h)

    def inputs(first, last):
        @pl.loop(first, last)
        def _(t):
            r = pl.ds(pl.multiple_of(t * TILE, TILE), TILE)
            acc = kdot(dqp[...], w1[r, 0:width], ((1,), (1,)))
            acc += kdot(dkp[...], w1[r, width : 2 * width], ((1,), (1,)))
            acc += kdot(dv[...], w2[r, 0:width], ((1,), (1,)))
            acc += kdot(u[...], w2[r, width : 2 * width], ((1,), (1,)))
            hid[:, cols(t * TILE, TILE)] = acc

    def inputs_rows():
        def body(at):
            value = dy[at, :].astype(F32)
            scale = lax.rsqrt(jnp.mean(value * value, axis=-1, keepdims=True) + EPSILON)
            normed = value * scale
            grad = hid[at, :]
            mean = jnp.mean(grad * normed, axis=-1, keepdims=True)
            dz[at, :] = (dh[at, :] + scale * (grad - normed * mean)).astype(BF16)

        row_tiles(body)
        load("grad_x", dz, grad_x_o)

    def work(n):
        if n == 0:
            weigh.tables(cosine, sine, seg_col, seg_row)
            ready("a2t", "p1", "p2")
        elif n == 1:
            up()
        elif n == 2:
            middle(0, 2)
        elif n == 3:
            middle(2, 4)
            ready("hid")
            middle_rows()
        elif n == 4:
            mix()
            ready("q")
        elif n == 5:
            load("qp", qp_i, s.at[:, pl.ds(0, width)])
            load("kp", kp_i, s.at[:, pl.ds(width, width)])
            outer()
        elif n == 6:
            ready("k", "v", "state", "qp", "kp", "mixed")
            attend_queries(0, H // 2)
        elif n == 7:
            attend_queries(H // 2, H)
            scan.totals_out()
        elif n == 8:
            ready("gt", "a1t")
        elif n == 9:
            scan.forward()
            scan.results_out()
        elif n == 11:
            scan.finish()
            attend_keys(0, H // 2)
            attend_keys(H // 2, H)
            ready("wq", "wv", "x")
        elif n == 13:
            inputs(0, 2)
        elif n == 14:
            inputs(2, 4)
        elif n == 15:
            inputs_rows()

    ready("dyt", "s")
    for n in range(steps):
        if n < count:
            give_half(n)
        allowed(n)
        if n < count:
            go(n, 0)
        if 0 <= n - 1 < count:
            merge(n - 1)
        if n - 1 - 1 * LAG in range(count):
            halve(n - 1 - 1 * LAG)
        if n - 1 - 2 * LAG in range(count):
            quarter(n - 1 - 2 * LAG)
        if n - 1 - 3 * LAG in range(count):
            along(n - 1 - 3 * LAG)
        if n - 1 - 4 * LAG in range(count):
            end(n - 1 - 4 * LAG)
        freed(n)
        work(n)
    for n in range(count - 3, count):
        for t in range(13):
            if of(n, t) and (t > 0 or n > count - 3):
                move(n, t).wait_send()
        final_copy(n).wait()
    ready("grad_x")


def run_backward(lengths, decay_rate, x, dy, kept):
    rows, width = x.shape
    hidden_size = kept[2].shape[1]
    part = width // 32
    row = jax.ShapeDtypeStruct((rows, width), BF16)
    outs = (
        [row] * 2
        + [jax.ShapeDtypeStruct((part, width), F32)] * 5
        + [jax.ShapeDtypeStruct((part, hidden_size), F32)] * 3
    )
    rv = pltpu.VMEM((rows, width), BF16)
    fv = pltpu.VMEM((rows, width), F32)
    tv = pltpu.VMEM((rows, hidden_size), BF16)
    wv = pltpu.VMEM((width, hidden_size), BF16)
    n = 1024
    h = n // 2
    scratch = (
        [pltpu.VMEM((hidden_size, width), BF16), wv, wv, tv, tv, tv, rv, fv, fv]
        + [rv] * 9
        + [pltpu.VMEM((H, 2, DH, DH), BF16)]
        + table_scratch(rows)
        + [pltpu.VMEM((width, rows), BF16)] * 4
        + scan_scratch()
        + [
            pltpu.VMEM((2, 512, n), BF16),
            pltpu.VMEM((2, 512, n), BF16),
            pltpu.VMEM((3, 2, 2, 2, 2, 32, n), BF16),
            pltpu.VMEM((3, 2, 2, 2, 32, h), BF16),
            pltpu.VMEM((3, 2, 2, 2, 32, h), BF16),
            pltpu.VMEM((3, 2, 2, 2, 32, h), BF16),
            pltpu.VMEM((3, 2, 2, 2, 32, h), BF16),
            pltpu.VMEM((3, 2, 2, 2, 32, h), BF16),
            pltpu.VMEM((3, 2, 2, 32, 2 * h), BF16),
            pltpu.VMEM((3, 2, 32, 2 * h), BF16),
            pltpu.VMEM((3, 2, 32, 2 * h), BF16),
            pltpu.VMEM((3, 32, 2 * h), BF16),
            pltpu.VMEM((3, 32, n), F32),
            pltpu.VMEM((3, 2, 2, 2, 32, UPRIGHT), BF16),
            pltpu.VMEM((3, 2, 2, 2, 32, UPRIGHT), BF16),
            pltpu.VMEM((3, 2, 2, 32, UPRIGHT), BF16),
            pltpu.VMEM((3, 2, 2, 32, UPRIGHT), BF16),
            pltpu.VMEM((3, 2, 32, UPRIGHT // 2), BF16),
            pltpu.VMEM((3, 2, 32, UPRIGHT // 2), BF16),
            pltpu.VMEM((3, 2, 32, UPRIGHT // 2), BF16),
            pltpu.VMEM((3, 2, 32, UPRIGHT // 2), BF16),
            pltpu.VMEM((3, 2, 32, UPRIGHT // 2), BF16),
        ]
        + [pltpu.SemaphoreType.DMA((39,))] * 2
        + [pltpu.SemaphoreType.REGULAR((5,))]
        + [pltpu.SemaphoreType.DMA((28,)), pltpu.SemaphoreType.DMA((3,))]
        + [pltpu.SemaphoreType.DMA((13,))] * 2
    )
    return pl.pallas_call(
        backward_kernel,
        out_shape=outs,
        in_specs=[SMEM, SMEM] + [ANY] * (2 + len(kept)),
        out_specs=[ANY] * len(outs),
        scratch_shapes=scratch,
        compiler_params=pltpu.CompilerParams(
            collective_id=1, has_side_effects=True, vmem_limit_bytes=VMEM_BYTES
        ),
        name="backward",
    )(lengths, decay_rate, x, dy, *kept)


def hand_over_kernel(*refs):
    count = (len(refs) - 2) // 3
    sources, targets, held = (refs[i * count : (i + 1) * count] for i in range(3))
    sems_in, sems_out = refs[3 * count :]
    fetches = [
        pltpu.make_async_copy(src, dst, sems_in.at[i])
        for i, (src, dst) in enumerate(zip(sources, held))
    ]
    for fetch in fetches:
        fetch.start()
    stores = []
    for i in range(count):
        fetches[i].wait()
        store = pltpu.make_async_copy(held[i], targets[i], sems_out.at[i])
        store.start()
        stores.append(store)
    for store in stores:
        store.wait()


def hand_over(arrays):
    return pl.pallas_call(
        hand_over_kernel,
        out_shape=[jax.ShapeDtypeStruct(a.shape, a.dtype) for a in arrays],
        in_specs=[ANY] * len(arrays),
        out_specs=[ANY] * len(arrays),
        scratch_shapes=[pltpu.VMEM(a.shape, a.dtype) for a in arrays]
        + [pltpu.SemaphoreType.DMA((len(arrays),))] * 2,
        name="hand_over",
    )(*arrays)


def local_fast(tokens, cotangent, lengths, decay_rate, *weights):
    mb, chunk, width = tokens.shape
    x = tokens.reshape(mb * chunk, width)
    dy = cotangent.reshape(mb * chunk, width)
    kept = run_forward(lengths, decay_rate, x, dy, weights)
    mixed, grad_x, *grads = hand_over(run_backward(lengths, decay_rate, x, dy, kept))
    return (mixed.reshape(tokens.shape), grad_x.reshape(tokens.shape), *grads[:-1], grads[-1].T)


def solution(mesh):
    rows = P(None, AXES, None)
    in_specs = (rows, rows, P(), P()) + (P("fsdp", None),) * 7 + (P(None, "fsdp"),)
    out_specs = (rows, rows) + (P(AXES, None),) * 7 + (P(None, AXES),)
    fast = mesh.shape["fsdp"] == 8 and mesh.shape["head"] == 4
    local = local_fast if fast else local_any
    return jax.shard_map(local, mesh=mesh, in_specs=in_specs, out_specs=out_specs, check_vma=False)
```

```python
import functools
import math

import jax
import jax.numpy as jnp
from jax import lax
from jax.experimental import pallas as pl
from jax.experimental.pallas import tpu as pltpu
from jax.sharding import PartitionSpec as P

H = 8
DH = 128
EPSILON = 1e-06
AXES = ("fsdp", "head")
F32 = jnp.float32
BF16 = jnp.bfloat16
MESH = pl.DeviceIdType.MESH
ANY = pl.BlockSpec(memory_space=pl.ANY)
VMEM = pl.BlockSpec(memory_space=pltpu.VMEM)
SMEM = pl.BlockSpec(memory_space=pltpu.SMEM)
VMEM_BYTES = 63 * 1024 * 1024
TILE = 256


def norm_parts(values):
    inv_scale = lax.rsqrt(jnp.mean(values * values, axis=-1, keepdims=True) + EPSILON)
    return (values * inv_scale, inv_scale)


def norm_back(gradient, normed, inv_scale):
    return inv_scale * (gradient - normed * jnp.mean(gradient * normed, axis=-1, keepdims=True))


def rotate_pairs(values, cosine, sine_vals):
    half_size = values.shape[-1] // 2
    first_half = values[..., :half_size]
    second_half = values[..., half_size:]
    return jnp.concatenate(
        [
            first_half * cosine - second_half * sine_vals,
            first_half * sine_vals + second_half * cosine,
        ],
        axis=-1,
    )


def rotation_tables(positions, head_size):
    half_size = head_size // 2
    shifts = jnp.arange(half_size, dtype=jnp.int32) * 10 // half_size
    speeds = jnp.right_shift(jnp.full((half_size,), 651, jnp.int32), shifts) + 1
    phases = positions[:, None] * speeds[None, :] % 4096
    angles = phases.astype(F32) * (2.0 * math.pi / 4096.0)
    return (jnp.cos(angles)[:, None, :], jnp.sin(angles)[:, None, :])


def silu_slope(values):
    sigmoid_v = jax.nn.sigmoid(values)
    return sigmoid_v * (1.0 + values * (1.0 - sigmoid_v))


def dot(a, b):
    return jnp.dot(a, b, preferred_element_type=F32)


def dot_rows(a, b):
    return lax.dot_general(a, b, (((0,), (0,)), ((), ())), preferred_element_type=F32)


def dot_cols(a, b):
    return lax.dot_general(a, b, (((1,), (1,)), ((), ())), preferred_element_type=F32)


class Wires:
    def __init__(self):
        self.nf = lax.axis_size("fsdp")
        self.nh = lax.axis_size("head")
        self.fast = self.nf == 8 and self.nh == 4
        self.f = lax.axis_index("fsdp")
        self.h = lax.axis_index("head")

    def swap(self, values, fbits=0, hbits=0):
        pairs = []
        for f in range(self.nf):
            for h in range(self.nh):
                pairs.append((f * self.nh + h, (f ^ fbits) * self.nh + (h ^ hbits)))
        return lax.ppermute(values, AXES, pairs)

    def rel(self, values):
        if not self.fast:
            return values
        width = values.shape[1] // self.nf
        return jnp.concatenate(
            [
                lax.dynamic_slice_in_dim(values, (self.f ^ i) * width, width, 1)
                for i in range(self.nf)
            ],
            axis=1,
        )

    def gather(self, shard):
        if not self.fast:
            return lax.all_gather(shard, "fsdp", axis=0, tiled=True)
        half = shard.shape[1] // 2
        core, x, y = 1, 2, 4
        at_c = self.swap(shard, core)
        at_x = self.swap(shard, x)
        at_y = self.swap(shard, y)
        at_xy = jnp.concatenate(
            [self.swap(at_x[:, :half], y), self.swap(at_y[:, half:], x)], axis=1
        )
        at_cx = self.swap(at_x, core)
        at_cy = self.swap(at_y, core)
        at_cxy = self.swap(at_xy, core)
        return jnp.concatenate([shard, at_c, at_x, at_cx, at_y, at_cy, at_xy, at_cxy], axis=0)

    def reduce(self, grad):
        if not self.fast:
            return lax.psum_scatter(grad, AXES, scatter_dimension=0, tiled=True)
        core, x, y = 1, 2, 4
        rows, n = grad.shape[0] // 8, grad.shape[1]
        low = grad.astype(BF16).reshape(2, 2, 2, rows, n)
        merged = (low[:, :, 0].astype(F32) + self.swap(low[:, :, 1], core).astype(F32)).astype(BF16)
        half = n // 2
        a = merged[:, :, :, :half]
        a = (a[:, 0].astype(F32) + self.swap(a[:, 1], x).astype(F32)).astype(BF16)
        a = (a[0].astype(F32) + self.swap(a[1], y).astype(F32)).astype(BF16)
        b = merged[:, :, :, half:]
        b = (b[0].astype(F32) + self.swap(b[1], y).astype(F32)).astype(BF16)
        b = (b[0].astype(F32) + self.swap(b[1], x).astype(F32)).astype(BF16)
        return jnp.concatenate([self.along(a), self.along(b)], axis=1)

    def along(self, part):
        rows, n = part.shape
        part = part.reshape(2, 2, rows // 4, n)
        low, high = self.h % 2, self.h // 2
        keep = lax.dynamic_index_in_dim(part, low, 1, False)
        send = lax.dynamic_index_in_dim(part, 1 - low, 1, False)
        part = (keep.astype(F32) + self.swap(send, 0, 1).astype(F32)).astype(BF16)
        keep = lax.dynamic_index_in_dim(part, high, 0, False)
        send = lax.dynamic_index_in_dim(part, 1 - high, 0, False)
        return keep.astype(F32) + self.swap(send, 0, 2).astype(F32)

    def to_heads(self, states):
        mb, heads, d, _ = states.shape
        mine = heads // self.nh
        parts = jnp.moveaxis(states.reshape(mb, self.nh, mine, d, d), 1, 0)
        return self.scatter(parts)

    def scatter(self, parts):
        if not self.fast:
            return lax.all_to_all(parts, "head", split_axis=0, concat_axis=0, tiled=True)
        got = [lax.dynamic_index_in_dim(parts, self.h, 0, False)]
        for i in range(1, self.nh):
            got.append(self.swap(lax.dynamic_index_in_dim(parts, self.h ^ i, 0, False), 0, i))
        got = jnp.stack(got)
        order = self.h ^ jnp.arange(self.nh)
        return jnp.take(got, order, axis=0)

    def from_heads(self, parts):
        got = self.scatter(parts)
        nh, mb, mine, d, _ = got.shape
        return jnp.moveaxis(got, 0, 1).reshape(mb, nh * mine, d, d)

    def spread(self, total):
        if not self.fast:
            return lax.all_gather(total, "fsdp")
        core, x, y = 1, 2, 4
        at_c = self.swap(total, core)
        pair = jnp.stack([total, at_c])
        at_x = self.swap(pair, x)
        at_y = self.swap(pair, y)
        at_xy = self.swap(pair, x + y)
        got = jnp.concatenate([pair, at_x, at_y, at_xy])
        return jnp.take(got, self.f ^ jnp.arange(self.nf), axis=0)


def chain(wires, states, ends, decay, chunk, backward):
    nf, nh, f = wires.nf, wires.nh, wires.f
    mb, heads = states.shape[:2]
    mine = heads // nh
    rates = lax.dynamic_slice_in_dim(decay, wires.h * mine, mine)
    places = jnp.arange(nh)
    groups = jnp.arange(nf)
    at_group = lax.dynamic_slice_in_dim(ends, f * nh, nh, axis=1)
    before_group = jnp.where(
        f > 0, lax.dynamic_index_in_dim(ends, jnp.maximum(f * nh - 1, 0), 1, False), 0
    )
    before = jnp.concatenate([before_group[:, None], at_group[:, :-1]], axis=1)
    last = at_group[:, -1]
    group_last = ends.reshape(mb, nf, nh)[:, :, -1]
    group_before = jnp.concatenate([jnp.zeros_like(group_last[:, :1]), group_last[:, :-1]], axis=1)

    def factor(same, gap):
        gap = jnp.maximum(gap, 0)
        return jnp.where(
            same[..., None], jnp.exp(-rates * (chunk * gap).astype(F32)[..., None]), 0.0
        )

    own = wires.to_heads(states.astype(BF16)).astype(F32)
    if backward:
        to_total = factor(before == before_group[:, None], jnp.broadcast_to(places, (mb, nh)))
        group_same = (last[:, None] == group_before) & (groups > f)
        group_gap = jnp.broadcast_to((groups - 1 - f) * nh, (mb, nf))
        to_place = factor(at_group == last[:, None], jnp.broadcast_to(nh - 1 - places, (mb, nh)))
        same = (at_group[:, :, None] == before[:, None, :]) & (places[None, :] > places[:, None])
        gap = jnp.broadcast_to(places[None, :] - 1 - places[:, None], (mb, nh, nh))
    else:
        to_total = factor(at_group == last[:, None], jnp.broadcast_to(nh - 1 - places, (mb, nh)))
        group_same = (before_group[:, None] == group_last) & (groups < f)
        group_gap = jnp.broadcast_to((f - 1 - groups) * nh, (mb, nf))
        to_place = factor(before == before_group[:, None], jnp.broadcast_to(places, (mb, nh)))
        same = (before[:, :, None] == at_group[:, None, :]) & (places[None, :] < places[:, None])
        gap = jnp.broadcast_to(places[:, None] - 1 - places[None, :], (mb, nh, nh))
    total = sum(to_total[:, i, :, None, None] * own[i] for i in range(nh))
    totals = wires.spread(total.astype(BF16)).astype(F32)
    from_group = factor(group_same, group_gap)
    outer = sum(from_group[:, i, :, None, None] * totals[i] for i in range(nf))
    between = factor(same, gap)
    result = [
        to_place[:, i, :, None, None] * outer
        + sum(between[:, i, j, :, None, None] * own[j] for j in range(nh) if i != j)
        for i in range(nh)
    ]
    return wires.from_heads(jnp.stack(result).astype(BF16))


def masks(segs, before, last, decay):
    rows = segs.shape[1]
    offsets = jnp.arange(rows, dtype=F32)
    distance = offsets[:, None] - offsets[None, :]
    visible = (segs[:, :, None] == segs[:, None, :]) & (distance >= 0.0)
    within = jnp.where(
        visible[:, None],
        jnp.exp(-decay[:, None, None] * jnp.maximum(distance, 0.0))[None],
        0.0,
    )
    entering = jnp.where(
        (segs == before[:, None])[:, None, :],
        jnp.exp(-decay[:, None] * (offsets + 1.0))[None],
        0.0,
    )
    leaving = jnp.where(
        (segs == last[:, None])[:, None, :],
        jnp.exp(-decay[:, None] * (rows - 1.0 - offsets))[None],
        0.0,
    )
    return within, entering[..., None], leaving[..., None]


def local_any(
    tokens,
    cotangent,
    lengths,
    decay_rate,
    query_weight,
    key_weight,
    value_weight,
    gate_weight,
    out_weight,
    first_weight,
    second_weight,
    down_weight,
):
    wires = Wires()
    mb, chunk, width = tokens.shape
    rows = mb * chunk
    place = wires.f * wires.nh + wires.h
    count = wires.nf * wires.nh

    mix_weights = wires.gather(
        jnp.concatenate([query_weight, key_weight, value_weight, gate_weight], axis=1)
    )
    out_full = wires.gather(out_weight)
    gate_up = wires.gather(jnp.concatenate([first_weight, second_weight], axis=1))
    down_t = wires.gather(down_weight.T)
    hidden_size = down_t.shape[1]

    positions = place * chunk + jnp.arange(chunk, dtype=jnp.int32)
    cosine, sine_vals = rotation_tables(positions, DH)
    cosine, sine_vals = jnp.tile(cosine, (mb, 1, 1)), jnp.tile(sine_vals, (mb, 1, 1))
    seq_ends = jnp.cumsum(lengths, axis=1)
    segs = jnp.sum((seq_ends[:, None, :] <= positions[None, :, None]).astype(jnp.int32), axis=2)
    marks = (jnp.arange(count, dtype=jnp.int32) + 1) * chunk - 1
    ends = jnp.sum((seq_ends[:, None, :] <= marks[None, :, None]).astype(jnp.int32), axis=2)
    last = lax.dynamic_index_in_dim(ends, place, 1, False)
    before = jnp.where(
        place > 0, lax.dynamic_index_in_dim(ends, jnp.maximum(place - 1, 0), 1, False), 0
    )
    within, entering, leaving = masks(segs, before, last, decay_rate)

    def heads(values):
        return values.reshape(mb, chunk, H, DH).transpose(0, 2, 1, 3)

    def flat(values):
        return values.transpose(0, 2, 1, 3).reshape(rows, H * DH)

    def mm(spec, a, b):
        return jnp.einsum(spec, a.astype(BF16), b.astype(BF16), preferred_element_type=F32)

    inputs = tokens.reshape(rows, width).astype(F32)
    normed_in, scale_in = norm_parts(inputs)
    act_rel = wires.rel(normed_in.astype(BF16))
    mixed_pre = dot(act_rel, mix_weights)
    query_pre = mixed_pre[:, :width]
    key_pre = mixed_pre[:, width : 2 * width]
    value_low = mixed_pre[:, 2 * width : 3 * width].astype(BF16)
    gate_vals = mixed_pre[:, 3 * width :]

    def turned(values):
        return rotate_pairs(jax.nn.silu(values).reshape(rows, H, DH), cosine, sine_vals).astype(BF16)

    query_h = heads(turned(query_pre))
    key_h = heads(turned(key_pre))
    value_h = heads(value_low)
    local_state = mm("mhtd,mhte->mhde", key_h * leaving, value_h)
    state_in = chain(wires, local_state, ends, decay_rate, chunk, False)
    scores = (mm("mhsd,mhtd->mhst", query_h, key_h) * within).astype(BF16)
    attended = mm("mhst,mhte->mhse", scores, value_h)
    attended = attended + entering * mm("mhsd,mhde->mhse", query_h, state_in)
    attended = flat(attended.astype(BF16))

    normed_att, scale_att = norm_parts(attended.astype(F32))
    gated_rel = wires.rel((normed_att * gate_vals).astype(BF16))
    hidden = inputs + dot(gated_rel, out_full)
    normed_mid, scale_mid = norm_parts(hidden)
    mid_rel = wires.rel(normed_mid.astype(BF16))
    pre = dot(mid_rel, gate_up)
    first_pre, second_pre = pre[:, :hidden_size], pre[:, hidden_size:]
    product = (first_pre * second_pre).astype(BF16)
    mixed = (hidden + wires.rel(dot_cols(product, down_t))).astype(BF16)

    grad_low = cotangent.reshape(rows, width)
    grad_rel = wires.rel(grad_low)
    share_down = wires.reduce(dot_rows(grad_rel, product)).T
    grad_prod = dot(grad_rel, down_t)
    grad_pre = jnp.concatenate(
        [(grad_prod * second_pre).astype(BF16), (grad_prod * first_pre).astype(BF16)], axis=1
    )
    share_up = wires.reduce(dot_rows(mid_rel, grad_pre))
    grad_mid = wires.rel(dot_cols(grad_pre, gate_up))
    grad_hidden = grad_low.astype(F32) + norm_back(grad_mid, normed_mid, scale_mid)
    grad_hidden_low = grad_hidden.astype(BF16)
    share_out = wires.reduce(dot_rows(gated_rel, grad_hidden_low))
    grad_gated = wires.rel(dot_cols(grad_hidden_low, out_full))
    grad_gate_low = (grad_gated * normed_att).astype(BF16)
    grad_att = heads(norm_back(grad_gated * gate_vals, normed_att, scale_att).astype(BF16))

    grad_state = mm("mhsd,mhse->mhde", query_h * entering, grad_att)
    grad_end = chain(wires, grad_state, ends, decay_rate, chunk, True)
    grad_scores = (mm("mhse,mhte->mhst", grad_att, value_h) * within).astype(BF16)
    grad_q = mm("mhst,mhtd->mhsd", grad_scores, key_h)
    grad_q = grad_q + entering * mm("mhse,mhde->mhsd", grad_att, state_in)
    grad_k = mm("mhst,mhsd->mhtd", grad_scores, query_h)
    grad_k = grad_k + leaving * mm("mhte,mhde->mhtd", value_h, grad_end)
    grad_v = mm("mhst,mhse->mhte", scores, grad_att)
    grad_v = grad_v + leaving * mm("mhtd,mhde->mhte", key_h, grad_end)

    def turned_back(values, pre_values):
        back = flat(values.astype(BF16)).astype(F32).reshape(rows, H, DH)
        back = rotate_pairs(back, cosine, -sine_vals).reshape(rows, width)
        return (silu_slope(pre_values) * back).astype(BF16)

    grad_mix = jnp.concatenate(
        [
            turned_back(grad_q, query_pre),
            turned_back(grad_k, key_pre),
            flat(grad_v.astype(BF16)),
            grad_gate_low,
        ],
        axis=1,
    )
    share_mix = wires.reduce(dot_rows(act_rel, grad_mix))
    grad_act = wires.rel(dot_cols(grad_mix, mix_weights))
    grad_tokens = (grad_hidden + norm_back(grad_act, normed_in, scale_in)).astype(BF16)
    return (
        mixed.reshape(mb, chunk, width),
        grad_tokens.reshape(mb, chunk, width),
        share_mix[:, :width],
        share_mix[:, width : 2 * width],
        share_mix[:, 2 * width : 3 * width],
        share_mix[:, 3 * width :],
        share_out,
        share_up[:, :hidden_size],
        share_up[:, hidden_size:],
        share_down,
    )


def flip(index, bit):
    return index + bit - 2 * bit * ((index // bit) % 2)


def kdot(a, b, dims=((1,), (0,))):
    return lax.dot_general(a, b, (dims, ((), ())), preferred_element_type=F32)


def cols(start, size):
    return pl.ds(pl.multiple_of(start, 128), size)


class Place:
    def __init__(self):
        self.f = lax.axis_index("fsdp")
        self.z = lax.axis_index("head")
        self.fc, self.fx, self.fy = (flip(self.f, b) for b in (1, 2, 4))
        self.fxy = flip(self.fx, 4)
        self.zs = [flip(self.z, 1), flip(self.z, 2), flip(flip(self.z, 1), 2)]

    def at(self, f=None, z=None):
        return {"fsdp": self.f if f is None else f, "head": self.z if z is None else z}

    def greet(self):
        barrier = pltpu.get_barrier_semaphore()
        others = [self.at(f=f) for f in (self.fc, self.fx, self.fy, self.fxy)]
        others += [self.at(z=z) for z in self.zs]
        for other in others:
            pl.semaphore_signal(barrier, inc=1, device_id=other, device_id_type=MESH)
        pl.semaphore_wait(barrier, len(others))


class Weigh:
    def __init__(self, place, lengths, decay, chunk, backward):
        self.p, self.decay, self.chunk, self.backward = place, decay, chunk, backward
        self.sums = []
        for m in range(2):
            total, row = 0, []
            for j in range(lengths.shape[1]):
                total = total + lengths[m, j]
                row.append(total)
            self.sums.append(row)
        first = 4 * place.f
        self.ends = [[self.end(m, first + i) for i in range(-1, 4)] for m in range(2)]
        self.groups = [[self.end(m, 4 * g + 3) for g in range(8)] for m in range(2)]
        own = first + place.z
        self.before = [self.end(m, own - 1) for m in range(2)]
        self.last = [self.end(m, own) for m in range(2)]

    def end(self, m, i):
        position = (i + 1) * self.chunk - 1
        return sum(jnp.where(total <= position, 1, 0) for total in self.sums[m])

    def tables(self, cosine, sine, seg_col, seg_row):
        chunk = self.chunk
        base = (4 * self.p.f + self.p.z) * chunk
        shape = (chunk, DH)
        lane = lax.broadcasted_iota(jnp.int32, shape, 1)
        row = lax.broadcasted_iota(jnp.int32, shape, 0) + base
        half = DH // 2
        turn = lane % half
        speed = jnp.right_shift(jnp.full(shape, 651, jnp.int32), turn * 10 // half) + 1
        angle = ((row * speed) % 4096).astype(F32) * (2.0 * math.pi / 4096.0)
        cos, sin = jnp.cos(angle), jnp.sin(angle)
        sin = jnp.where(lane < half, -sin, sin)
        down = lax.broadcasted_iota(jnp.int32, (chunk, 1), 0) + base
        across = lax.broadcasted_iota(jnp.int32, (1, chunk), 1) + base
        for m in range(2):
            at = slice(m * chunk, (m + 1) * chunk)
            cosine[at, :] = cos
            sine[at, :] = sin
            seg_col[at, :] = sum(jnp.where(total <= down, 1, 0) for total in self.sums[m])
            seg_row[m : m + 1, :] = sum(jnp.where(total <= across, 1, 0) for total in self.sums[m])

    def power(self, same, chunks, hh):
        rate = self.decay[2 * self.p.z + hh]
        gap = jnp.asarray(chunks * self.chunk, jnp.int32).astype(F32)
        value = jnp.exp(jnp.full((1, DH), -rate * gap, F32))
        return jnp.where(same, value, 0.0)

    def to_total(self, m, i, hh):
        ends = self.ends[m]
        if self.backward:
            return self.power(ends[i] == ends[0], i, hh)
        return self.power(ends[i + 1] == ends[4], 3 - i, hh)

    def to_place(self, m, i, hh):
        ends = self.ends[m]
        if self.backward:
            return self.power(ends[i + 1] == ends[4], 3 - i, hh)
        return self.power(ends[i] == ends[0], i, hh)

    def from_group(self, m, g, hh):
        f = self.p.f
        if self.backward:
            before = self.groups[m][g - 1] if g > 0 else 0
            same = (self.ends[m][4] == before) & (g > f)
            return self.power(same, 4 * jnp.maximum(g - 1 - f, 0), hh)
        same = (self.ends[m][0] == self.groups[m][g]) & (g < f)
        return self.power(same, 4 * jnp.maximum(f - 1 - g, 0), hh)

    def others(self, i):
        return range(i + 1, 4) if self.backward else range(i)

    def between(self, m, i, j, hh):
        ends = self.ends[m]
        if self.backward:
            return self.power(ends[i + 1] == ends[j], j - 1 - i, hh)
        return self.power(ends[i] == ends[j + 1], i - 1 - j, hh)


class Scan:
    def __init__(self, place, weigh, states, inbox, totals, outbox, result, send, recv):
        self.p, self.weigh = place, weigh
        self.states, self.inbox, self.totals = states, inbox, totals
        self.outbox, self.result = outbox, result
        self.send, self.recv = send, recv

    def copy(self, src, dst, n, where):
        return pltpu.make_async_remote_copy(
            src_ref=src,
            dst_ref=dst,
            send_sem=self.send.at[n],
            recv_sem=self.recv.at[n],
            device_id=where,
            device_id_type=MESH,
        )

    def to_heads(self, i):
        z = self.p.zs[i]
        return self.copy(self.states.at[pl.ds(2 * z, 2)], self.inbox.at[self.p.z], i, self.p.at(z=z))

    def from_heads(self, i):
        z = self.p.zs[i]
        return self.copy(
            self.outbox.at[z], self.result.at[pl.ds(2 * self.p.z, 2)], 9 + i, self.p.at(z=z)
        )

    def total(self, n, origin, where):
        return self.copy(self.totals.at[origin], self.totals.at[origin], n, self.p.at(f=where))

    def start(self):
        p = self.p
        for i in range(3):
            self.to_heads(i).start()
        self.inbox[p.z] = self.states[pl.ds(2 * p.z, 2)]

    def totals_out(self):
        p = self.p
        for i in range(3):
            self.to_heads(i).wait()
        for hh in range(2):
            for m in range(2):
                acc = sum(
                    self.weigh.to_total(m, i, hh) * self.inbox[i, hh, m].astype(F32)
                    for i in range(4)
                )
                self.totals[p.f, hh, m] = acc.astype(BF16)
        for n, where in ((3, p.fx), (4, p.fy), (5, p.fxy)):
            self.total(n, p.f, where).start()
        self.total(12, p.f, p.fc).start()

    def forward(self):
        p = self.p
        for n, where in ((3, p.fx), (4, p.fy), (5, p.fxy)):
            self.total(n, p.f, where).wait()
            self.total(n + 3, where, p.fc).start()

    def results_out(self):
        p = self.p
        self.total(12, p.f, p.fc).wait()
        for n, where in ((3, p.fx), (4, p.fy), (5, p.fxy)):
            self.total(n + 3, where, p.fc).wait()
        for hh in range(2):
            for m in range(2):
                outer = sum(
                    self.weigh.from_group(m, g, hh) * self.totals[g, hh, m].astype(F32)
                    for g in range(8)
                )
                for i in range(4):
                    acc = self.weigh.to_place(m, i, hh) * outer
                    for j in self.weigh.others(i):
                        acc += self.weigh.between(m, i, j, hh) * self.inbox[j, hh, m].astype(F32)
                    self.outbox[i, hh, m] = acc.astype(BF16)
        for i in range(3):
            self.from_heads(i).start()
        self.result[pl.ds(2 * p.z, 2)] = self.outbox[p.z]

    def finish(self):
        for i in range(3):
            self.from_heads(i).wait()


def edge(seg, mark, rate, gap):
    return jnp.where(seg == mark, jnp.exp(-rate * gap), 0.0)


def decays(rate, rows):
    up = lax.broadcasted_iota(jnp.int32, (rows, rows), 0)
    across = lax.broadcasted_iota(jnp.int32, (rows, rows), 1)
    gap = (up - across).astype(F32)
    return jnp.where(gap >= 0.0, jnp.exp(-rate * jnp.maximum(gap, 0.0)), 0.0)


def up_tile(a2, w1, w2, s, dp1, dp2, t):
    at = cols(t * TILE, TILE)
    first = kdot(a2[...], w1[:, at])
    second = kdot(a2[...], w2[:, at])
    ds = dp1[:, at].astype(F32)
    s[:, at] = (first * second).astype(BF16)
    dp1[:, at] = (ds * second).astype(BF16)
    dp2[:, at] = (ds * first).astype(BF16)


def forward_kernel(
    lengths, decay_rate, x, dy,
    wq, wk, wv, wu, wo, w1, w2, wd,
    mix_o, wo_o, w1_o, w2_o, wd_o, q_o, k_o, v_o, u_o, qp_o, kp_o, ob_o, hid_o, dp1_o, dp2_o, s_o,
    state_o, a2_o, a1t_o, a2t_o, gt_o, dyt_o,
    fm, fo, f1, f2, fd, a1, q, k, v, u, qp, kp, att, ob, g, hid, dp1, dp2, s,
    cosine, sine, seg_col, seg_row, a1t, a2t, gt, dyt, states, inbox, totals, outbox, result,
    send, recv, own_sem, save_sem, scan_send, scan_recv,
):
    place = Place()
    f = place.f
    rows, width = x.shape
    chunk = rows // 2
    hidden_size = w1.shape[1]
    half_hidden = hidden_size // 2
    place.greet()

    pieces = []
    for i, w in ((1, wk), (2, wv), (0, wq), (3, wu)):
        pieces.append((w, fm, (0, 128), (0, width), i * width))
    for part in range(2):
        pieces.append((wd, fd, (part * half_hidden, half_hidden), (0, 128), None))
    pieces.append((wo, fo, (0, 128), (0, width), 0))
    for part in range(2):
        for w, full in ((w1, f1), (w2, f2)):
            at = part * half_hidden
            pieces.append((w, full, (0, 128), (at, half_hidden), at))
    w, full, _, (at, size), _ = pieces.pop()
    first = (size // 2 + 127) // 128 * 128
    pieces.append((w, full, (0, 128), (at, first), at))
    pieces.append((w, full, (0, 128), (at + first, size - first), at + first))
    count = len(pieces)
    parity = place.z % 2

    def parts(n):
        thin = (3, 2)[n % 2]
        wide = 8 - thin
        near = (wide + (n // 2) % 2) // 2
        fetch = (parity * thin, wide)
        return {
            "all": (0, 8),
            "fetch": fetch,
            "near": (fetch[0], near),
            "far": (fetch[0] + near, wide - near),
            "give": (parity * wide, thin),
            "take": ((1 - parity) * wide, thin),
        }

    def own(n, part="all"):
        w, _, (r, rs), (c, cs), _ = pieces[n]
        at, size = parts(n)[part]
        eighth = rs // 8
        return w.at[pl.ds(pl.multiple_of(r + at * eighth, 16), size * eighth), pl.ds(c, cs)]

    def block(n, origin, part="all"):
        _, full, (r, rs), (c, cs), to = pieces[n]
        at, size = parts(n)[part]
        eighth = rs // 8
        if to is None:
            start = pl.multiple_of(r + at * eighth, 16)
            return full.at[pl.ds(start, size * eighth), cols(origin * 128, 128)]
        start = pl.multiple_of(origin * 128 + at * eighth, 16)
        return full.at[pl.ds(start, size * eighth), pl.ds(to, cs)]

    fc, fx, fy, fxy = place.fc, place.fx, place.fy, place.fxy
    at_c, at_x, at_y = (place.at(f=o) for o in (fc, fx, fy))
    at_z = place.at(z=place.zs[0])

    def step(n, t):
        fetched = own(n, "fetch"), block(n, f, "fetch")
        src, dst, where, lands = [
            (own(n), block(n, f), at_c, (fc, "all")),
            (*fetched, at_x, (fx, "fetch")),
            (*fetched, at_y, (fy, "fetch")),
            (block(n, fx, "near"), None, at_y, (fxy, "near")),
            (block(n, fy, "far"), None, at_x, (fxy, "far")),
            (block(n, fx, "give"), None, at_z, (fx, "take")),
            (block(n, fy, "give"), None, at_z, (fy, "take")),
            (block(n, fxy, "give"), None, at_z, (fxy, "take")),
            (block(n, fx), None, at_c, (flip(fx, 1), "all")),
            (block(n, fy), None, at_c, (flip(fy, 1), "all")),
            (block(n, fxy), None, at_c, (flip(fxy, 1), "all")),
        ][t]
        return src, src if dst is None else dst, where, block(n, *lands)

    def move(n, t, src, dst, where):
        return pltpu.make_async_remote_copy(
            src_ref=src,
            dst_ref=dst,
            send_sem=send.at[n * 11 + t],
            recv_sem=recv.at[n * 11 + t],
            device_id=where,
            device_id_type=MESH,
        )

    def go(n, t):
        src, dst, where, _ = step(n, t)
        move(n, t, src, dst, where).start()

    def got(n, *which):
        for t in which:
            _, _, where, lands = step(n, t)
            move(n, t, lands, lands, where).wait_recv()

    def own_copy(n):
        return pltpu.make_async_copy(own(n), block(n, f), own_sem.at[n])

    saves = []

    def save(src, dst):
        copy = pltpu.make_async_copy(src, dst, save_sem.at[len(saves)])
        copy.start()
        saves.append(copy)

    def save_piece(n):
        full_o = {id(fm): mix_o, id(fo): wo_o, id(f1): w1_o, id(f2): w2_o, id(fd): wd_o}
        _, full, (r, rs), (c, cs), to = pieces[n]
        out = full_o[id(full)]
        if to is None:
            save(full.at[pl.ds(r, rs)], out.at[pl.ds(r, rs)])
        else:
            save(full.at[:, pl.ds(to, cs)], out.at[:, pl.ds(to, cs)])

    def norm_in():
        @pl.loop(0, rows // 128)
        def _(t):
            at = pl.ds(pl.multiple_of(t * 128, 128), 128)
            value = x[at, :].astype(F32)
            scale = lax.rsqrt(jnp.mean(value * value, axis=-1, keepdims=True) + EPSILON)
            a1[at, :] = (value * scale).astype(BF16)

    def turn_over(src, dst):
        @pl.loop(0, width // 128)
        def _(b):
            other_c = (b + f) % 2
            other_x = (b // 2 + f // 2) % 2
            other_y = (b // 4 + f // 4) % 2
            slot = other_c * 4 + other_y * 2 + other_x
            value = src[:, cols(b * 128, 128)].astype(F32)
            dst[pl.ds(pl.multiple_of(slot * 128, 128), 128), :] = value.T.astype(BF16)

    def project(base, pre, low, turn):
        @pl.loop(0, width // TILE)
        def _(t):
            at = cols(t * TILE, TILE)
            acc = kdot(a1[...], fm[:, cols(base + t * TILE, TILE)])
            if not turn:
                low[:, at] = acc.astype(BF16)
                return
            pre[:, at] = acc.astype(BF16)
            acc = acc * lax.logistic(acc)
            turned = []
            for hh in range(TILE // DH):
                piece = acc[:, hh * DH : (hh + 1) * DH]
                turned.append(piece * cosine[...] + pltpu.roll(piece, DH // 2, 1) * sine[...])
            low[:, at] = jnp.concatenate(turned, axis=1).astype(BF16)

    offset = lax.broadcasted_iota(jnp.int32, (chunk, 1), 0).astype(F32)
    weigh = Weigh(place, lengths, decay_rate, chunk, False)
    scan = Scan(place, weigh, states, inbox, totals, outbox, result, scan_send, scan_recv)

    def local_states():
        @pl.loop(0, H)
        def _(h):
            at = cols(h * DH, DH)
            for m in range(2):
                r = slice(m * chunk, (m + 1) * chunk)
                leaving = edge(seg_col[r], weigh.last[m], decay_rate[h], chunk - 1.0 - offset)
                left = (k[r, at].astype(F32) * leaving).astype(BF16)
                states[h, m] = kdot(left, v[r, at], ((0,), (0,))).astype(BF16)

    def attend_local(first, last):
        @pl.loop(first, last)
        def _(h):
            at = cols(h * DH, DH)
            decay = decays(decay_rate[h], chunk)
            for m in range(2):
                r = slice(m * chunk, (m + 1) * chunk)
                within = jnp.where(seg_col[r] == seg_row[m : m + 1], decay, 0.0)
                scores = kdot(q[r, at], k[r, at], ((1,), (1,))) * within
                att[r, at] = kdot(scores.astype(BF16), v[r, at])

    def attend_rest():
        @pl.loop(0, H)
        def _(h):
            at = cols(h * DH, DH)
            for m in range(2):
                r = slice(m * chunk, (m + 1) * chunk)
                entering = edge(seg_col[r], weigh.before[m], decay_rate[h], offset + 1.0)
                ob[r, at] = (att[r, at] + entering * kdot(q[r, at], result[h, m])).astype(BF16)

    def hidden():
        @pl.loop(0, rows // 128)
        def _(t):
            at = pl.ds(pl.multiple_of(t * 128, 128), 128)
            value = ob[at, :].astype(F32)
            scale = lax.rsqrt(jnp.mean(value * value, axis=-1, keepdims=True) + EPSILON)
            g[at, :] = (value * scale * u[at, :].astype(F32)).astype(BF16)

        turn_over(g, gt)
        save(gt, gt_o)

        @pl.loop(0, width // TILE)
        def _(t):
            at = cols(t * TILE, TILE)
            hid[:, at] = x[:, at].astype(F32) + kdot(g[...], fo[:, at])

        @pl.loop(0, rows // 128)
        def _(t):
            at = pl.ds(pl.multiple_of(t * 128, 128), 128)
            value = hid[at, :]
            scale = lax.rsqrt(jnp.mean(value * value, axis=-1, keepdims=True) + EPSILON)
            g[at, :] = (value * scale).astype(BF16)

    def inner(part):
        @pl.loop(0, half_hidden // 128)
        def _(t):
            start = part * half_hidden + t * 128
            rhs = fd[pl.ds(pl.multiple_of(start, 128), 128), :]
            dp1[:, cols(start, 128)] = kdot(dy[...], rhs, ((1,), (1,))).astype(BF16)

    def up():
        @pl.loop(0, half_hidden // TILE)
        def _(t):
            up_tile(g, f1, f2, s, dp1, dp2, t)

    def work(n):
        if n == 0:
            project(width, kp, k, True)
            save(k, k_o)
            save(kp, kp_o)
        elif n == 1:
            project(2 * width, None, v, False)
            local_states()
            scan.start()
            save(v, v_o)
        elif n == 2:
            project(0, qp, q, True)
            save(q, q_o)
            save(qp, qp_o)
        elif n == 3:
            project(3 * width, None, u, False)
            save(u, u_o)
            scan.totals_out()
        elif n == 4:
            attend_local(0, H // 2)
            scan.forward()
        elif n == 5:
            attend_local(H // 2, H)
            scan.results_out()
        elif n == 6:
            inner(0)
            inner(1)
        elif n == 7:
            scan.finish()
            save(result, state_o)
            attend_rest()
            save(ob, ob_o)
            hidden()
            save(hid, hid_o)
            save(g, a2_o)
        elif n == 8:
            up()
            done = pl.ds(0, half_hidden // TILE * TILE)
            save(s.at[:, done], s_o.at[:, done])
            save(dp1, dp1_o)
            save(dp2.at[:, done], dp2_o.at[:, done])
        elif n == 9:
            turn_over(g, a2t)
            save(a2t, a2t_o)

    def early(n):
        if n == 0:
            turn_over(dy, dyt)
            save(dyt, dyt_o)
        elif n == 1:
            turn_over(a1, a1t)
            save(a1t, a1t_o)

    ahead = 2
    for n in range(ahead):
        for t in (1, 2, 0):
            go(n, t)
        own_copy(n).start()
    weigh.tables(cosine, sine, seg_col, seg_row)
    norm_in()
    for n in range(count + 3):
        if n < count:
            got(n, 1)
            go(n, 3)
            go(n, 5)
            got(n, 2)
            go(n, 4)
            go(n, 6)
            if n + ahead < count:
                for t in (1, 2, 0):
                    go(n + ahead, t)
                own_copy(n + ahead).start()
        if 0 <= n - 1 < count:
            got(n - 1, 3, 4)
            go(n - 1, 7)
            got(n - 1, 5)
            go(n - 1, 8)
            got(n - 1, 6)
            go(n - 1, 9)
        if 0 <= n - 2 < count:
            got(n - 2, 7)
            go(n - 2, 10)
        if n - 3 >= 0:
            got(n - 3, 0, 8, 9, 10)
            own_copy(n - 3).wait()
            save_piece(n - 3)
            work(n - 3)
        else:
            early(n)
    for n in range(count):
        for t in range(11):
            src, dst, where, _ = step(n, t)
            move(n, t, src, dst, where).wait_send()
    for copy in saves:
        copy.wait()


def run_forward(lengths, decay_rate, x, dy, weights):
    rows, width = x.shape
    hidden_size = weights[5].shape[1]
    row = jax.ShapeDtypeStruct((rows, width), BF16)
    tall = jax.ShapeDtypeStruct((rows, hidden_size), BF16)
    outs = (
        [
            jax.ShapeDtypeStruct(shape, BF16)
            for shape in (
                (width, 4 * width), (width, width), (width, hidden_size), (width, hidden_size),
                (hidden_size, width),
            )
        ]
        + [row] * 7
        + [jax.ShapeDtypeStruct((rows, width), F32)]
        + [tall] * 3
        + [jax.ShapeDtypeStruct((H, 2, DH, DH), BF16), row]
        + [jax.ShapeDtypeStruct((width, rows), BF16)] * 4
    )
    rv = pltpu.VMEM((rows, width), BF16)
    tv = pltpu.VMEM((rows, hidden_size), BF16)
    scratch = (
        [pltpu.VMEM(o.shape, BF16) for o in outs[:5]]
        + [rv] * 7
        + [pltpu.VMEM((rows, width), F32), rv, rv, pltpu.VMEM((rows, width), F32)]
        + [tv] * 3
        + table_scratch(rows)
        + [pltpu.VMEM((width, rows), BF16)] * 4
        + scan_scratch()
        + [pltpu.SemaphoreType.DMA((132,))] * 2
        + [pltpu.SemaphoreType.DMA((12,)), pltpu.SemaphoreType.DMA((29,))]
        + [pltpu.SemaphoreType.DMA((13,))] * 2
    )
    return pl.pallas_call(
        forward_kernel,
        out_shape=outs,
        in_specs=[SMEM, SMEM] + [VMEM] * 2 + [ANY] * 8,
        out_specs=[ANY] * len(outs),
        scratch_shapes=scratch,
        compiler_params=pltpu.CompilerParams(
            collective_id=0, has_side_effects=True, vmem_limit_bytes=VMEM_BYTES
        ),
        name="forward",
    )(lengths, decay_rate, x, dy, *weights)


def table_scratch(rows):
    return [
        pltpu.VMEM((rows, DH), F32),
        pltpu.VMEM((rows, DH), F32),
        pltpu.VMEM((rows, 1), jnp.int32),
        pltpu.VMEM((2, rows // 2), jnp.int32),
    ]


def scan_scratch():
    return [
        pltpu.VMEM((H, 2, DH, DH), BF16),
        pltpu.VMEM((4, 2, 2, DH, DH), BF16),
        pltpu.VMEM((8, 2, 2, DH, DH), BF16),
        pltpu.VMEM((4, 2, 2, DH, DH), BF16),
        pltpu.VMEM((H, 2, DH, DH), BF16),
    ]


UPRIGHT = 256
LAG = 2
WITH_UPRIGHT = (0, 1, 2, 3, 4, 8, 9, 10, 11, 12, 13)
LAST = 1024


def backward_kernel(
    lengths, decay_rate,
    x_i, dy_i, wm_i, wo_i, w1_i, w2_i, wd_i, q_i, k_i, v_i, u_i, qp_i, kp_i, ob_i, hid_i,
    p1_i, p2_i, s_i, state_i, a2_i, a1t_i, a2t_i, gt_i, dyt_i,
    mixed_o, grad_x_o, gq_o, gk_o, gv_o, gu_o, go_o, g1_o, g2_o, gd_o,
    wd, w1, w2, s, p1, p2, dy, hid, dh, dz, ob, u, q, k, v, dqp, dkp, dv, state_in,
    cosine, sine, seg_col, seg_row, a1t, a2t, gt, dyt, states, inbox, totals, outbox, result,
    give, take, merged, take_a, take_b, half_a, half_b, take2, mine, take3, pair, take4, final,
    z_take, z_sum, z_take2, z_sum2, z_take_a, z_take_b, z_half_a, z_half_b, z_take3,
    send, recv, free, load_sem, out_sem, scan_send, scan_recv,
):
    place = Place()
    rows, width = dy.shape
    chunk = rows // 2
    hidden_size = s.shape[1]
    place.greet()

    loads = {}

    def load(name, src, dst):
        copy = pltpu.make_async_copy(src, dst, load_sem.at[len(loads)])
        copy.start()
        loads[name] = copy

    def ready(*names):
        for name in names:
            loads[name].wait()

    done = pl.ds(0, hidden_size // 2 // TILE * TILE)
    for name, src, dst in (
        ("dyt", dyt_i, dyt), ("s", s_i.at[:, done], s.at[:, done]), ("a2t", a2t_i, a2t), ("p1", p1_i, p1),
        ("p2", p2_i.at[:, done], p2.at[:, done]), ("a2", a2_i, dkp), ("w1", w1_i, w1), ("w2", w2_i, w2),
        ("hid", hid_i, hid), ("wd", wd_i, wd), ("dy", dy_i, dy), ("ob", ob_i, ob), ("u", u_i, u), ("q", q_i, q), ("gt", gt_i, gt),
        ("k", k_i, k), ("v", v_i, v), ("state", state_i, state_in), ("a1t", a1t_i, a1t),
    ):
        load(name, src, dst)

    pieces = []
    for start in range(0, hidden_size, 1024):
        size = min(1024, hidden_size - start)
        for left, right, out in ((dyt, s, gd_o), (a2t, p1, g1_o), (a2t, p2, g2_o)):
            pieces.append((left, right, out, start, size))
    for left, right, out in ((gt, dz, go_o), (a1t, u, gu_o), (a1t, dqp, gq_o), (a1t, dkp, gk_o)):
        pieces.append((left, right, out, 0, width))
    for start in range(0, width, LAST):
        pieces.append((a1t, dv, gv_o, start, LAST))
    count = len(pieces)
    steps = count + 1 + 4 * LAG
    low, high = place.z % 2, place.z // 2
    f = place.f
    at_c, at_x, at_y = (place.at(f=o) for o in (place.fc, place.fx, place.fy))
    at_z1, at_z2 = (place.at(z=place.zs[i]) for i in range(2))
    partner = [at_c, at_x, at_y, at_y, at_x, at_z1, at_z2]
    partner += [at_z1, at_z2, at_x, at_y, at_y, at_x]
    quarter_size = UPRIGHT // 2
    lo, hi = pl.ds(0, quarter_size), pl.ds(quarter_size, quarter_size)

    def upright(n):
        return n in WITH_UPRIGHT

    def half_of(n):
        return (pieces[n][4] - UPRIGHT * upright(n)) // 2

    def of(n, *which):
        return [t for t in which if t < 7 or upright(n)]

    def move(n, t):
        size = pieces[n][4]
        c, m, half = n % 2, n % 3, half_of(n)
        a, b, ab, last = (pl.ds(*at) for at in ((0, half), (half, half), (0, 2 * half), (2 * half, UPRIGHT)))
        src, dst = [
            lambda: (give.at[c, :, pl.ds(0, size)], take.at[c, :, pl.ds(0, size)]),
            lambda: (merged.at[m, :, 1, :, :, :, a], take_a.at[m, :, :, :, :, a]),
            lambda: (merged.at[m, 1, :, :, :, :, b], take_b.at[m, :, :, :, :, a]),
            lambda: (half_a.at[m, 1, :, :, :, a], take2.at[m, 0, :, :, :, a]),
            lambda: (half_b.at[m, 1, :, :, :, a], take2.at[m, 1, :, :, :, a]),
            lambda: (mine.at[m, :, 1 - low, :, ab], take3.at[m, :, :, ab]),
            lambda: (pair.at[m, 1 - high, :, ab], take4.at[m, :, ab]),
            lambda: (merged.at[m, :, :, :, 1 - low, :, last], z_take.at[m]),
            lambda: (z_sum.at[m, :, :, 1 - high], z_take2.at[m]),
            lambda: (z_sum2.at[m, :, 1, :, lo], z_take_a.at[m]),
            lambda: (z_sum2.at[m, 1, :, :, hi], z_take_b.at[m]),
            lambda: (z_half_a.at[m, 1], z_take3.at[m, 0]),
            lambda: (z_half_b.at[m, 1], z_take3.at[m, 1]),
        ][t]()
        return pltpu.make_async_remote_copy(
            src_ref=src,
            dst_ref=dst,
            send_sem=send.at[3 * t + m],
            recv_sem=recv.at[3 * t + m],
            device_id=partner[t],
            device_id_type=MESH,
        )

    def go(n, t):
        move(n, t).start()

    def reuse(n, *which):
        for t in which:
            earlier = n - (2 if t == 0 else 3)
            if earlier >= 0 and of(earlier, t):
                move(earlier, t).wait_send()

    def got(n, t):
        move(n, t).wait_recv()

    near = (at_c, at_x, at_y, at_z1, at_z2)

    def freed(n):
        if n < steps - 1:
            for i, where in enumerate(near):
                pl.semaphore_signal(free.at[i], 1, device_id=where, device_id_type=MESH)

    def allowed(n):
        if n >= 1:
            for i in range(len(near)):
                pl.semaphore_wait(free.at[i], 1)

    def give_half(n):
        left, right, _, start, size = pieces[n]
        slot = n % 2
        reuse(n, 0)

        @pl.loop(0, size // TILE)
        def _(t):
            value = kdot(left[rows : 2 * rows, :], right[:, cols(start + t * TILE, TILE)])
            give[slot, :, cols(t * TILE, TILE)] = value.astype(BF16)


    def merge(n):
        left, right, _, start, size = pieces[n]
        slot, m = n % 2, n % 3
        got(n, 0)
        reuse(n, 1, 2, 7)

        @pl.loop(0, size // TILE)
        def _(t):
            at = cols(t * TILE, TILE)
            value = kdot(left[0:rows, :], right[:, cols(start + t * TILE, TILE)])
            value = (value + take[slot, :, at].astype(F32)).astype(BF16)
            for i in range(16):
                r = i * 32
                merged[m, i // 8, i // 4 % 2, i // 2 % 2, i % 2, :, at] = value[r : r + 32]

        for t in of(n, 1, 2, 7):
            go(n, t)

    def add(a, b):
        return a.astype(F32) + b.astype(F32)

    def halve(n):
        m, half = n % 3, half_of(n)
        reuse(n, 8)
        if upright(n):
            got(n, 7)
            c = slice(2 * half, 2 * half + UPRIGHT)
            for y in range(2):
                z_sum[m, y] = add(merged[m, y, :, :, low, :, c], z_take[m, y]).astype(BF16)
            go(n, 8)
        got(n, 1)
        reuse(n, 3)
        for i in (1, 0):
            half_a[m, i, :, :, :, :half] = add(
                merged[m, i, 0, :, :, :, :half], take_a[m, i, :, :, :, :half]
            ).astype(BF16)
        go(n, 3)
        got(n, 2)
        reuse(n, 4)
        for i in (1, 0):
            half_b[m, i, :, :, :, :half] = add(
                merged[m, 0, i, :, :, :, half : 2 * half], take_b[m, i, :, :, :, :half]
            ).astype(BF16)
        go(n, 4)

    def quarter(n):
        m, half = n % 3, half_of(n)
        reuse(n, 9, 10)
        if upright(n):
            got(n, 8)
            z_sum2[m] = add(z_sum[m, :, :, high], z_take2[m]).astype(BF16)
            go(n, 9)
            go(n, 10)
        reuse(n, 5)
        for t, kept, at in ((3, half_a, slice(0, half)), (4, half_b, slice(half, 2 * half))):
            got(n, t)
            mine[m, :, :, :, at] = add(
                kept[m, 0, :, :, :, :half], take2[m, t - 3, :, :, :, :half]
            ).astype(BF16)
        go(n, 5)

    def along(n):
        m, whole = n % 3, 2 * half_of(n)
        reuse(n, 11, 12)
        if upright(n):
            got(n, 9)
            z_half_a[m] = add(z_sum2[m, :, 0, :, :quarter_size], z_take_a[m]).astype(BF16)
            go(n, 11)
            got(n, 10)
            z_half_b[m] = add(z_sum2[m, 0, :, :, quarter_size:], z_take_b[m]).astype(BF16)
            go(n, 12)
        got(n, 5)
        reuse(n, 6)
        for i in range(2):
            pair[m, i, :, :whole] = add(
                mine[m, i, low, :, :whole], take3[m, i, :, :whole]
            ).astype(BF16)
        go(n, 6)

    def final_copy(n):
        _, _, out, start, size = pieces[n]
        m = n % 3
        return pltpu.make_async_copy(
            final.at[m, :, pl.ds(0, size)], out.at[:, pl.ds(start, size)], out_sem.at[m]
        )

    def end(n):
        m, whole = n % 3, 2 * half_of(n)
        if n >= 3:
            final_copy(n - 3).wait()
        for t in of(n, 11, 12):
            i, kept = t - 11, (z_half_a, z_half_b)[t - 11]
            got(n, t)
            at = slice(whole + i * quarter_size, whole + (i + 1) * quarter_size)
            final[m, :, at] = add(kept[m, 0], z_take3[m, i])
        got(n, 6)
        final[m, :, :whole] = add(pair[m, high, :, :whole], take4[m, :, :whole])
        final_copy(n).start()

    offset = lax.broadcasted_iota(jnp.int32, (chunk, 1), 0).astype(F32)
    weigh = Weigh(place, lengths, decay_rate, chunk, True)
    scan = Scan(place, weigh, states, inbox, totals, outbox, result, scan_send, scan_recv)

    def row_tiles(body):
        @pl.loop(0, rows // 128)
        def _(t):
            body(pl.ds(pl.multiple_of(t * 128, 128), 128))

    def up():
        ready("a2", "w1", "w2")

        @pl.loop(hidden_size // 2 // TILE, hidden_size // TILE)
        def _(t):
            up_tile(dkp, w1, w2, s, p1, p2, t)

    def mix():
        ready("wd")

        @pl.loop(0, width // TILE)
        def _(t):
            at = cols(t * TILE, TILE)
            dqp[:, at] = (hid[:, at] + kdot(s[...], wd[:, at])).astype(BF16)

        load("mixed", dqp, mixed_o)
        load("wo", wo_i, wd.at[pl.ds(0, width)])

    def middle(first, last):
        @pl.loop(first, last)
        def _(t):
            r = pl.ds(pl.multiple_of(t * TILE, TILE), TILE)
            dh[:, cols(t * TILE, TILE)] = kdot(p1[...], w1[r, :], ((1,), (1,))) + kdot(
                p2[...], w2[r, :], ((1,), (1,))
            )

    def middle_rows():
        ready("dy")
        load("wq", wm_i.at[:, pl.ds(0, 2 * width)], w1.at[:, pl.ds(0, 2 * width)])
        load("wv", wm_i.at[:, pl.ds(2 * width, 2 * width)], w2.at[:, pl.ds(0, 2 * width)])

        def body(at):
            value = hid[at, :]
            scale = lax.rsqrt(jnp.mean(value * value, axis=-1, keepdims=True) + EPSILON)
            normed = value * scale
            grad = dh[at, :]
            mean = jnp.mean(grad * normed, axis=-1, keepdims=True)
            grad = dy[at, :].astype(F32) + scale * (grad - normed * mean)
            dh[at, :] = grad
            dz[at, :] = grad.astype(BF16)

        row_tiles(body)
        load("x", x_i, dy)

    def outer():
        ready("wo", "ob", "u")

        @pl.loop(0, width // TILE)
        def _(t):
            r = pl.ds(pl.multiple_of(t * TILE, TILE), TILE)
            hid[:, cols(t * TILE, TILE)] = kdot(dz[...], wd[r, :], ((1,), (1,)))

        def body(at):
            value = ob[at, :].astype(F32)
            scale = lax.rsqrt(jnp.mean(value * value, axis=-1, keepdims=True) + EPSILON)
            normed = value * scale
            grad = hid[at, :]
            dm = grad * u[at, :].astype(F32)
            u[at, :] = (grad * normed).astype(BF16)
            mean = jnp.mean(dm * normed, axis=-1, keepdims=True)
            ob[at, :] = (scale * (dm - normed * mean)).astype(BF16)

        row_tiles(body)

        @pl.loop(0, H)
        def _(h):
            at = cols(h * DH, DH)
            for m in range(2):
                r = slice(m * chunk, (m + 1) * chunk)
                entering = edge(seg_col[r], weigh.before[m], decay_rate[h], offset + 1.0)
                left = (q[r, at].astype(F32) * entering).astype(BF16)
                states[h, m] = kdot(left, ob[r, at], ((0,), (0,))).astype(BF16)

        scan.start()

    def slope(pre):
        sig = lax.logistic(pre)
        return sig * (1.0 + pre * (1.0 - sig))

    def turned_back(grad, r, base, h):
        grad = grad.astype(BF16).astype(F32)
        back = grad * cosine[r, :] - pltpu.roll(grad, DH // 2, 1) * sine[r, :]
        return (slope(s[r, cols(base + h * DH, DH)].astype(F32)) * back).astype(BF16)

    def attend_queries(first, last):
        @pl.loop(first, last)
        def _(h):
            at = cols(h * DH, DH)
            decay = decays(decay_rate[h], chunk)
            for m in range(2):
                r = slice(m * chunk, (m + 1) * chunk)
                within = jnp.where(seg_col[r] == seg_row[m : m + 1], decay, 0.0)
                entering = edge(seg_col[r], weigh.before[m], decay_rate[h], offset + 1.0)
                oh = ob[r, at]
                grads = (kdot(oh, v[r, at], ((1,), (1,))) * within).astype(BF16)
                dq = kdot(grads, k[r, at]) + entering * kdot(oh, state_in[h, m], ((1,), (1,)))
                dqp[r, at] = turned_back(dq, r, 0, h)

    def attend_keys(first, last):
        @pl.loop(first, last)
        def _(h):
            at = cols(h * DH, DH)
            decay = decays(decay_rate[h], chunk)
            for m in range(2):
                r = slice(m * chunk, (m + 1) * chunk)
                within = jnp.where(seg_col[r] == seg_row[m : m + 1], decay, 0.0)
                leaving = edge(seg_col[r], weigh.last[m], decay_rate[h], chunk - 1.0 - offset)
                qh, kh, vh, oh = q[r, at], k[r, at], v[r, at], ob[r, at]
                grads = (kdot(oh, vh, ((1,), (1,))) * within).astype(BF16)
                dk = kdot(grads, qh, ((0,), (0,)))
                dk = dk + leaving * kdot(vh, result[h, m], ((1,), (1,)))
                scores = (kdot(qh, kh, ((1,), (1,))) * within).astype(BF16)
                grad_v = kdot(scores, oh, ((0,), (0,))) + leaving * kdot(kh, result[h, m])
                dv[r, at] = grad_v.astype(BF16)
                dkp[r, at] = turned_back(dk, r, width, h)

    def inputs(first, last):
        @pl.loop(first, last)
        def _(t):
            r = pl.ds(pl.multiple_of(t * TILE, TILE), TILE)
            acc = kdot(dqp[...], w1[r, 0:width], ((1,), (1,)))
            acc += kdot(dkp[...], w1[r, width : 2 * width], ((1,), (1,)))
            acc += kdot(dv[...], w2[r, 0:width], ((1,), (1,)))
            acc += kdot(u[...], w2[r, width : 2 * width], ((1,), (1,)))
            hid[:, cols(t * TILE, TILE)] = acc

    def inputs_rows():
        def body(at):
            value = dy[at, :].astype(F32)
            scale = lax.rsqrt(jnp.mean(value * value, axis=-1, keepdims=True) + EPSILON)
            normed = value * scale
            grad = hid[at, :]
            mean = jnp.mean(grad * normed, axis=-1, keepdims=True)
            dz[at, :] = (dh[at, :] + scale * (grad - normed * mean)).astype(BF16)

        row_tiles(body)
        load("grad_x", dz, grad_x_o)

    def work(n):
        if n == 0:
            weigh.tables(cosine, sine, seg_col, seg_row)
            ready("a2t", "p1", "p2")
        elif n == 1:
            up()
        elif n == 2:
            middle(0, 2)
        elif n == 3:
            middle(2, 4)
            ready("hid")
            middle_rows()
        elif n == 4:
            mix()
            ready("q")
        elif n == 5:
            load("qp", qp_i, s.at[:, pl.ds(0, width)])
            load("kp", kp_i, s.at[:, pl.ds(width, width)])
            outer()
        elif n == 6:
            ready("k", "v", "state", "qp", "kp", "mixed")
            attend_queries(0, H // 2)
        elif n == 7:
            attend_queries(H // 2, H)
            scan.totals_out()
        elif n == 8:
            ready("gt", "a1t")
        elif n == 9:
            scan.forward()
            scan.results_out()
        elif n == 11:
            scan.finish()
            attend_keys(0, H // 2)
            attend_keys(H // 2, H)
            ready("wq", "wv", "x")
        elif n == 13:
            inputs(0, 2)
        elif n == 14:
            inputs(2, 4)
        elif n == 15:
            inputs_rows()

    ready("dyt", "s")
    for n in range(steps):
        if n < count:
            give_half(n)
        allowed(n)
        if n < count:
            go(n, 0)
        if 0 <= n - 1 < count:
            merge(n - 1)
        if n - 1 - 1 * LAG in range(count):
            halve(n - 1 - 1 * LAG)
        if n - 1 - 2 * LAG in range(count):
            quarter(n - 1 - 2 * LAG)
        if n - 1 - 3 * LAG in range(count):
            along(n - 1 - 3 * LAG)
        if n - 1 - 4 * LAG in range(count):
            end(n - 1 - 4 * LAG)
        freed(n)
        work(n)
    for n in range(count - 3, count):
        for t in range(13):
            if of(n, t) and (t > 0 or n > count - 3):
                move(n, t).wait_send()
        final_copy(n).wait()
    ready("grad_x")


def run_backward(lengths, decay_rate, x, dy, kept):
    rows, width = x.shape
    hidden_size = kept[2].shape[1]
    part = width // 32
    row = jax.ShapeDtypeStruct((rows, width), BF16)
    outs = (
        [row] * 2
        + [jax.ShapeDtypeStruct((part, width), F32)] * 5
        + [jax.ShapeDtypeStruct((part, hidden_size), F32)] * 3
    )
    rv = pltpu.VMEM((rows, width), BF16)
    fv = pltpu.VMEM((rows, width), F32)
    tv = pltpu.VMEM((rows, hidden_size), BF16)
    wv = pltpu.VMEM((width, hidden_size), BF16)
    n = 1024
    h = n // 2
    scratch = (
        [pltpu.VMEM((hidden_size, width), BF16), wv, wv, tv, tv, tv, rv, fv, fv]
        + [rv] * 9
        + [pltpu.VMEM((H, 2, DH, DH), BF16)]
        + table_scratch(rows)
        + [pltpu.VMEM((width, rows), BF16)] * 4
        + scan_scratch()
        + [
            pltpu.VMEM((2, 512, n), BF16),
            pltpu.VMEM((2, 512, n), BF16),
            pltpu.VMEM((3, 2, 2, 2, 2, 32, n), BF16),
            pltpu.VMEM((3, 2, 2, 2, 32, h), BF16),
            pltpu.VMEM((3, 2, 2, 2, 32, h), BF16),
            pltpu.VMEM((3, 2, 2, 2, 32, h), BF16),
            pltpu.VMEM((3, 2, 2, 2, 32, h), BF16),
            pltpu.VMEM((3, 2, 2, 2, 32, h), BF16),
            pltpu.VMEM((3, 2, 2, 32, 2 * h), BF16),
            pltpu.VMEM((3, 2, 32, 2 * h), BF16),
            pltpu.VMEM((3, 2, 32, 2 * h), BF16),
            pltpu.VMEM((3, 32, 2 * h), BF16),
            pltpu.VMEM((3, 32, n), F32),
            pltpu.VMEM((3, 2, 2, 2, 32, UPRIGHT), BF16),
            pltpu.VMEM((3, 2, 2, 2, 32, UPRIGHT), BF16),
            pltpu.VMEM((3, 2, 2, 32, UPRIGHT), BF16),
            pltpu.VMEM((3, 2, 2, 32, UPRIGHT), BF16),
            pltpu.VMEM((3, 2, 32, UPRIGHT // 2), BF16),
            pltpu.VMEM((3, 2, 32, UPRIGHT // 2), BF16),
            pltpu.VMEM((3, 2, 32, UPRIGHT // 2), BF16),
            pltpu.VMEM((3, 2, 32, UPRIGHT // 2), BF16),
            pltpu.VMEM((3, 2, 32, UPRIGHT // 2), BF16),
        ]
        + [pltpu.SemaphoreType.DMA((39,))] * 2
        + [pltpu.SemaphoreType.REGULAR((5,))]
        + [pltpu.SemaphoreType.DMA((28,)), pltpu.SemaphoreType.DMA((3,))]
        + [pltpu.SemaphoreType.DMA((13,))] * 2
    )
    return pl.pallas_call(
        backward_kernel,
        out_shape=outs,
        in_specs=[SMEM, SMEM] + [ANY] * (2 + len(kept)),
        out_specs=[ANY] * len(outs),
        scratch_shapes=scratch,
        compiler_params=pltpu.CompilerParams(
            collective_id=1, has_side_effects=True, vmem_limit_bytes=VMEM_BYTES
        ),
        name="backward",
    )(lengths, decay_rate, x, dy, *kept)


def hand_over_kernel(*refs):
    count = (len(refs) - 2) // 3
    sources, targets, held = (refs[i * count : (i + 1) * count] for i in range(3))
    sems_in, sems_out = refs[3 * count :]
    fetches = [
        pltpu.make_async_copy(src, dst, sems_in.at[i])
        for i, (src, dst) in enumerate(zip(sources, held))
    ]
    for fetch in fetches:
        fetch.start()
    stores = []
    for i in range(count):
        fetches[i].wait()
        store = pltpu.make_async_copy(held[i], targets[i], sems_out.at[i])
        store.start()
        stores.append(store)
    for store in stores:
        store.wait()


def hand_over(arrays):
    return pl.pallas_call(
        hand_over_kernel,
        out_shape=[jax.ShapeDtypeStruct(a.shape, a.dtype) for a in arrays],
        in_specs=[ANY] * len(arrays),
        out_specs=[ANY] * len(arrays),
        scratch_shapes=[pltpu.VMEM(a.shape, a.dtype) for a in arrays]
        + [pltpu.SemaphoreType.DMA((len(arrays),))] * 2,
        name="hand_over",
    )(*arrays)


def local_fast(tokens, cotangent, lengths, decay_rate, *weights):
    mb, chunk, width = tokens.shape
    x = tokens.reshape(mb * chunk, width)
    dy = cotangent.reshape(mb * chunk, width)
    kept = run_forward(lengths, decay_rate, x, dy, weights)
    mixed, grad_x, *grads = hand_over(run_backward(lengths, decay_rate, x, dy, kept))
    return (mixed.reshape(tokens.shape), grad_x.reshape(tokens.shape), *grads[:-1], grads[-1].T)


def solution(mesh):
    rows = P(None, AXES, None)
    in_specs = (rows, rows, P(), P()) + (P("fsdp", None),) * 7 + (P(None, "fsdp"),)
    out_specs = (rows, rows) + (P(AXES, None),) * 7 + (P(None, AXES),)
    fast = mesh.shape["fsdp"] == 8 and mesh.shape["head"] == 4
    local = local_fast if fast else local_any
    return jax.shard_map(local, mesh=mesh, in_specs=in_specs, out_specs=out_specs, check_vma=False)
```

```python
import functools
import math

import jax
import jax.numpy as jnp
from jax import lax
from jax.experimental import pallas as pl
from jax.experimental.pallas import tpu as pltpu
from jax.sharding import PartitionSpec as P

H = 8
DH = 128
EPSILON = 1e-06
AXES = ("fsdp", "head")
F32 = jnp.float32
BF16 = jnp.bfloat16
MESH = pl.DeviceIdType.MESH
ANY = pl.BlockSpec(memory_space=pl.ANY)
VMEM = pl.BlockSpec(memory_space=pltpu.VMEM)
SMEM = pl.BlockSpec(memory_space=pltpu.SMEM)
VMEM_BYTES = 63 * 1024 * 1024
TILE = 256


def norm_parts(values):
    inv_scale = lax.rsqrt(jnp.mean(values * values, axis=-1, keepdims=True) + EPSILON)
    return (values * inv_scale, inv_scale)


def norm_back(gradient, normed, inv_scale):
    return inv_scale * (gradient - normed * jnp.mean(gradient * normed, axis=-1, keepdims=True))


def rotate_pairs(values, cosine, sine_vals):
    half_size = values.shape[-1] // 2
    first_half = values[..., :half_size]
    second_half = values[..., half_size:]
    return jnp.concatenate(
        [
            first_half * cosine - second_half * sine_vals,
            first_half * sine_vals + second_half * cosine,
        ],
        axis=-1,
    )


def rotation_tables(positions, head_size):
    half_size = head_size // 2
    shifts = jnp.arange(half_size, dtype=jnp.int32) * 10 // half_size
    speeds = jnp.right_shift(jnp.full((half_size,), 651, jnp.int32), shifts) + 1
    phases = positions[:, None] * speeds[None, :] % 4096
    angles = phases.astype(F32) * (2.0 * math.pi / 4096.0)
    return (jnp.cos(angles)[:, None, :], jnp.sin(angles)[:, None, :])


def silu_slope(values):
    sigmoid_v = jax.nn.sigmoid(values)
    return sigmoid_v * (1.0 + values * (1.0 - sigmoid_v))


def dot(a, b):
    return jnp.dot(a, b, preferred_element_type=F32)


def dot_rows(a, b):
    return lax.dot_general(a, b, (((0,), (0,)), ((), ())), preferred_element_type=F32)


def dot_cols(a, b):
    return lax.dot_general(a, b, (((1,), (1,)), ((), ())), preferred_element_type=F32)


class Wires:
    def __init__(self):
        self.nf = lax.axis_size("fsdp")
        self.nh = lax.axis_size("head")
        self.fast = self.nf == 8 and self.nh == 4
        self.f = lax.axis_index("fsdp")
        self.h = lax.axis_index("head")

    def swap(self, values, fbits=0, hbits=0):
        pairs = []
        for f in range(self.nf):
            for h in range(self.nh):
                pairs.append((f * self.nh + h, (f ^ fbits) * self.nh + (h ^ hbits)))
        return lax.ppermute(values, AXES, pairs)

    def rel(self, values):
        if not self.fast:
            return values
        width = values.shape[1] // self.nf
        return jnp.concatenate(
            [
                lax.dynamic_slice_in_dim(values, (self.f ^ i) * width, width, 1)
                for i in range(self.nf)
            ],
            axis=1,
        )

    def gather(self, shard):
        if not self.fast:
            return lax.all_gather(shard, "fsdp", axis=0, tiled=True)
        half = shard.shape[1] // 2
        core, x, y = 1, 2, 4
        at_c = self.swap(shard, core)
        at_x = self.swap(shard, x)
        at_y = self.swap(shard, y)
        at_xy = jnp.concatenate(
            [self.swap(at_x[:, :half], y), self.swap(at_y[:, half:], x)], axis=1
        )
        at_cx = self.swap(at_x, core)
        at_cy = self.swap(at_y, core)
        at_cxy = self.swap(at_xy, core)
        return jnp.concatenate([shard, at_c, at_x, at_cx, at_y, at_cy, at_xy, at_cxy], axis=0)

    def reduce(self, grad):
        if not self.fast:
            return lax.psum_scatter(grad, AXES, scatter_dimension=0, tiled=True)
        core, x, y = 1, 2, 4
        rows, n = grad.shape[0] // 8, grad.shape[1]
        low = grad.astype(BF16).reshape(2, 2, 2, rows, n)
        merged = (low[:, :, 0].astype(F32) + self.swap(low[:, :, 1], core).astype(F32)).astype(BF16)
        half = n // 2
        a = merged[:, :, :, :half]
        a = (a[:, 0].astype(F32) + self.swap(a[:, 1], x).astype(F32)).astype(BF16)
        a = (a[0].astype(F32) + self.swap(a[1], y).astype(F32)).astype(BF16)
        b = merged[:, :, :, half:]
        b = (b[0].astype(F32) + self.swap(b[1], y).astype(F32)).astype(BF16)
        b = (b[0].astype(F32) + self.swap(b[1], x).astype(F32)).astype(BF16)
        return jnp.concatenate([self.along(a), self.along(b)], axis=1)

    def along(self, part):
        rows, n = part.shape
        part = part.reshape(2, 2, rows // 4, n)
        low, high = self.h % 2, self.h // 2
        keep = lax.dynamic_index_in_dim(part, low, 1, False)
        send = lax.dynamic_index_in_dim(part, 1 - low, 1, False)
        part = (keep.astype(F32) + self.swap(send, 0, 1).astype(F32)).astype(BF16)
        keep = lax.dynamic_index_in_dim(part, high, 0, False)
        send = lax.dynamic_index_in_dim(part, 1 - high, 0, False)
        return keep.astype(F32) + self.swap(send, 0, 2).astype(F32)

    def to_heads(self, states):
        mb, heads, d, _ = states.shape
        mine = heads // self.nh
        parts = jnp.moveaxis(states.reshape(mb, self.nh, mine, d, d), 1, 0)
        return self.scatter(parts)

    def scatter(self, parts):
        if not self.fast:
            return lax.all_to_all(parts, "head", split_axis=0, concat_axis=0, tiled=True)
        got = [lax.dynamic_index_in_dim(parts, self.h, 0, False)]
        for i in range(1, self.nh):
            got.append(self.swap(lax.dynamic_index_in_dim(parts, self.h ^ i, 0, False), 0, i))
        got = jnp.stack(got)
        order = self.h ^ jnp.arange(self.nh)
        return jnp.take(got, order, axis=0)

    def from_heads(self, parts):
        got = self.scatter(parts)
        nh, mb, mine, d, _ = got.shape
        return jnp.moveaxis(got, 0, 1).reshape(mb, nh * mine, d, d)

    def spread(self, total):
        if not self.fast:
            return lax.all_gather(total, "fsdp")
        core, x, y = 1, 2, 4
        at_c = self.swap(total, core)
        pair = jnp.stack([total, at_c])
        at_x = self.swap(pair, x)
        at_y = self.swap(pair, y)
        at_xy = self.swap(pair, x + y)
        got = jnp.concatenate([pair, at_x, at_y, at_xy])
        return jnp.take(got, self.f ^ jnp.arange(self.nf), axis=0)


def chain(wires, states, ends, decay, chunk, backward):
    nf, nh, f = wires.nf, wires.nh, wires.f
    mb, heads = states.shape[:2]
    mine = heads // nh
    rates = lax.dynamic_slice_in_dim(decay, wires.h * mine, mine)
    places = jnp.arange(nh)
    groups = jnp.arange(nf)
    at_group = lax.dynamic_slice_in_dim(ends, f * nh, nh, axis=1)
    before_group = jnp.where(
        f > 0, lax.dynamic_index_in_dim(ends, jnp.maximum(f * nh - 1, 0), 1, False), 0
    )
    before = jnp.concatenate([before_group[:, None], at_group[:, :-1]], axis=1)
    last = at_group[:, -1]
    group_last = ends.reshape(mb, nf, nh)[:, :, -1]
    group_before = jnp.concatenate([jnp.zeros_like(group_last[:, :1]), group_last[:, :-1]], axis=1)

    def factor(same, gap):
        gap = jnp.maximum(gap, 0)
        return jnp.where(
            same[..., None], jnp.exp(-rates * (chunk * gap).astype(F32)[..., None]), 0.0
        )

    own = wires.to_heads(states.astype(BF16)).astype(F32)
    if backward:
        to_total = factor(before == before_group[:, None], jnp.broadcast_to(places, (mb, nh)))
        group_same = (last[:, None] == group_before) & (groups > f)
        group_gap = jnp.broadcast_to((groups - 1 - f) * nh, (mb, nf))
        to_place = factor(at_group == last[:, None], jnp.broadcast_to(nh - 1 - places, (mb, nh)))
        same = (at_group[:, :, None] == before[:, None, :]) & (places[None, :] > places[:, None])
        gap = jnp.broadcast_to(places[None, :] - 1 - places[:, None], (mb, nh, nh))
    else:
        to_total = factor(at_group == last[:, None], jnp.broadcast_to(nh - 1 - places, (mb, nh)))
        group_same = (before_group[:, None] == group_last) & (groups < f)
        group_gap = jnp.broadcast_to((f - 1 - groups) * nh, (mb, nf))
        to_place = factor(before == before_group[:, None], jnp.broadcast_to(places, (mb, nh)))
        same = (before[:, :, None] == at_group[:, None, :]) & (places[None, :] < places[:, None])
        gap = jnp.broadcast_to(places[:, None] - 1 - places[None, :], (mb, nh, nh))
    total = sum(to_total[:, i, :, None, None] * own[i] for i in range(nh))
    totals = wires.spread(total.astype(BF16)).astype(F32)
    from_group = factor(group_same, group_gap)
    outer = sum(from_group[:, i, :, None, None] * totals[i] for i in range(nf))
    between = factor(same, gap)
    result = [
        to_place[:, i, :, None, None] * outer
        + sum(between[:, i, j, :, None, None] * own[j] for j in range(nh) if i != j)
        for i in range(nh)
    ]
    return wires.from_heads(jnp.stack(result).astype(BF16))


def masks(segs, before, last, decay):
    rows = segs.shape[1]
    offsets = jnp.arange(rows, dtype=F32)
    distance = offsets[:, None] - offsets[None, :]
    visible = (segs[:, :, None] == segs[:, None, :]) & (distance >= 0.0)
    within = jnp.where(
        visible[:, None],
        jnp.exp(-decay[:, None, None] * jnp.maximum(distance, 0.0))[None],
        0.0,
    )
    entering = jnp.where(
        (segs == before[:, None])[:, None, :],
        jnp.exp(-decay[:, None] * (offsets + 1.0))[None],
        0.0,
    )
    leaving = jnp.where(
        (segs == last[:, None])[:, None, :],
        jnp.exp(-decay[:, None] * (rows - 1.0 - offsets))[None],
        0.0,
    )
    return within, entering[..., None], leaving[..., None]


def local_any(
    tokens,
    cotangent,
    lengths,
    decay_rate,
    query_weight,
    key_weight,
    value_weight,
    gate_weight,
    out_weight,
    first_weight,
    second_weight,
    down_weight,
):
    wires = Wires()
    mb, chunk, width = tokens.shape
    rows = mb * chunk
    place = wires.f * wires.nh + wires.h
    count = wires.nf * wires.nh

    mix_weights = wires.gather(
        jnp.concatenate([query_weight, key_weight, value_weight, gate_weight], axis=1)
    )
    out_full = wires.gather(out_weight)
    gate_up = wires.gather(jnp.concatenate([first_weight, second_weight], axis=1))
    down_t = wires.gather(down_weight.T)
    hidden_size = down_t.shape[1]

    positions = place * chunk + jnp.arange(chunk, dtype=jnp.int32)
    cosine, sine_vals = rotation_tables(positions, DH)
    cosine, sine_vals = jnp.tile(cosine, (mb, 1, 1)), jnp.tile(sine_vals, (mb, 1, 1))
    seq_ends = jnp.cumsum(lengths, axis=1)
    segs = jnp.sum((seq_ends[:, None, :] <= positions[None, :, None]).astype(jnp.int32), axis=2)
    marks = (jnp.arange(count, dtype=jnp.int32) + 1) * chunk - 1
    ends = jnp.sum((seq_ends[:, None, :] <= marks[None, :, None]).astype(jnp.int32), axis=2)
    last = lax.dynamic_index_in_dim(ends, place, 1, False)
    before = jnp.where(
        place > 0, lax.dynamic_index_in_dim(ends, jnp.maximum(place - 1, 0), 1, False), 0
    )
    within, entering, leaving = masks(segs, before, last, decay_rate)

    def heads(values):
        return values.reshape(mb, chunk, H, DH).transpose(0, 2, 1, 3)

    def flat(values):
        return values.transpose(0, 2, 1, 3).reshape(rows, H * DH)

    def mm(spec, a, b):
        return jnp.einsum(spec, a.astype(BF16), b.astype(BF16), preferred_element_type=F32)

    inputs = tokens.reshape(rows, width).astype(F32)
    normed_in, scale_in = norm_parts(inputs)
    act_rel = wires.rel(normed_in.astype(BF16))
    mixed_pre = dot(act_rel, mix_weights)
    query_pre = mixed_pre[:, :width]
    key_pre = mixed_pre[:, width : 2 * width]
    value_low = mixed_pre[:, 2 * width : 3 * width].astype(BF16)
    gate_vals = mixed_pre[:, 3 * width :]

    def turned(values):
        return rotate_pairs(jax.nn.silu(values).reshape(rows, H, DH), cosine, sine_vals).astype(BF16)

    query_h = heads(turned(query_pre))
    key_h = heads(turned(key_pre))
    value_h = heads(value_low)
    local_state = mm("mhtd,mhte->mhde", key_h * leaving, value_h)
    state_in = chain(wires, local_state, ends, decay_rate, chunk, False)
    scores = (mm("mhsd,mhtd->mhst", query_h, key_h) * within).astype(BF16)
    attended = mm("mhst,mhte->mhse", scores, value_h)
    attended = attended + entering * mm("mhsd,mhde->mhse", query_h, state_in)
    attended = flat(attended.astype(BF16))

    normed_att, scale_att = norm_parts(attended.astype(F32))
    gated_rel = wires.rel((normed_att * gate_vals).astype(BF16))
    hidden = inputs + dot(gated_rel, out_full)
    normed_mid, scale_mid = norm_parts(hidden)
    mid_rel = wires.rel(normed_mid.astype(BF16))
    pre = dot(mid_rel, gate_up)
    first_pre, second_pre = pre[:, :hidden_size], pre[:, hidden_size:]
    product = (first_pre * second_pre).astype(BF16)
    mixed = (hidden + wires.rel(dot_cols(product, down_t))).astype(BF16)

    grad_low = cotangent.reshape(rows, width)
    grad_rel = wires.rel(grad_low)
    share_down = wires.reduce(dot_rows(grad_rel, product)).T
    grad_prod = dot(grad_rel, down_t)
    grad_pre = jnp.concatenate(
        [(grad_prod * second_pre).astype(BF16), (grad_prod * first_pre).astype(BF16)], axis=1
    )
    share_up = wires.reduce(dot_rows(mid_rel, grad_pre))
    grad_mid = wires.rel(dot_cols(grad_pre, gate_up))
    grad_hidden = grad_low.astype(F32) + norm_back(grad_mid, normed_mid, scale_mid)
    grad_hidden_low = grad_hidden.astype(BF16)
    share_out = wires.reduce(dot_rows(gated_rel, grad_hidden_low))
    grad_gated = wires.rel(dot_cols(grad_hidden_low, out_full))
    grad_gate_low = (grad_gated * normed_att).astype(BF16)
    grad_att = heads(norm_back(grad_gated * gate_vals, normed_att, scale_att).astype(BF16))

    grad_state = mm("mhsd,mhse->mhde", query_h * entering, grad_att)
    grad_end = chain(wires, grad_state, ends, decay_rate, chunk, True)
    grad_scores = (mm("mhse,mhte->mhst", grad_att, value_h) * within).astype(BF16)
    grad_q = mm("mhst,mhtd->mhsd", grad_scores, key_h)
    grad_q = grad_q + entering * mm("mhse,mhde->mhsd", grad_att, state_in)
    grad_k = mm("mhst,mhsd->mhtd", grad_scores, query_h)
    grad_k = grad_k + leaving * mm("mhte,mhde->mhtd", value_h, grad_end)
    grad_v = mm("mhst,mhse->mhte", scores, grad_att)
    grad_v = grad_v + leaving * mm("mhtd,mhde->mhte", key_h, grad_end)

    def turned_back(values, pre_values):
        back = flat(values.astype(BF16)).astype(F32).reshape(rows, H, DH)
        back = rotate_pairs(back, cosine, -sine_vals).reshape(rows, width)
        return (silu_slope(pre_values) * back).astype(BF16)

    grad_mix = jnp.concatenate(
        [
            turned_back(grad_q, query_pre),
            turned_back(grad_k, key_pre),
            flat(grad_v.astype(BF16)),
            grad_gate_low,
        ],
        axis=1,
    )
    share_mix = wires.reduce(dot_rows(act_rel, grad_mix))
    grad_act = wires.rel(dot_cols(grad_mix, mix_weights))
    grad_tokens = (grad_hidden + norm_back(grad_act, normed_in, scale_in)).astype(BF16)
    return (
        mixed.reshape(mb, chunk, width),
        grad_tokens.reshape(mb, chunk, width),
        share_mix[:, :width],
        share_mix[:, width : 2 * width],
        share_mix[:, 2 * width : 3 * width],
        share_mix[:, 3 * width :],
        share_out,
        share_up[:, :hidden_size],
        share_up[:, hidden_size:],
        share_down,
    )


def flip(index, bit):
    return index + bit - 2 * bit * ((index // bit) % 2)


def kdot(a, b, dims=((1,), (0,))):
    return lax.dot_general(a, b, (dims, ((), ())), preferred_element_type=F32)


def cols(start, size):
    return pl.ds(pl.multiple_of(start, 128), size)


class Place:
    def __init__(self):
        self.f = lax.axis_index("fsdp")
        self.z = lax.axis_index("head")
        self.fc, self.fx, self.fy = (flip(self.f, b) for b in (1, 2, 4))
        self.fxy = flip(self.fx, 4)
        self.zs = [flip(self.z, 1), flip(self.z, 2), flip(flip(self.z, 1), 2)]

    def at(self, f=None, z=None):
        return {"fsdp": self.f if f is None else f, "head": self.z if z is None else z}

    def greet(self):
        barrier = pltpu.get_barrier_semaphore()
        others = [self.at(f=f) for f in (self.fc, self.fx, self.fy, self.fxy)]
        others += [self.at(z=z) for z in self.zs]
        for other in others:
            pl.semaphore_signal(barrier, inc=1, device_id=other, device_id_type=MESH)
        pl.semaphore_wait(barrier, len(others))


class Weigh:
    def __init__(self, place, lengths, decay, chunk, backward):
        self.p, self.decay, self.chunk, self.backward = place, decay, chunk, backward
        self.sums = []
        for m in range(2):
            total, row = 0, []
            for j in range(lengths.shape[1]):
                total = total + lengths[m, j]
                row.append(total)
            self.sums.append(row)
        first = 4 * place.f
        self.ends = [[self.end(m, first + i) for i in range(-1, 4)] for m in range(2)]
        self.groups = [[self.end(m, 4 * g + 3) for g in range(8)] for m in range(2)]
        own = first + place.z
        self.before = [self.end(m, own - 1) for m in range(2)]
        self.last = [self.end(m, own) for m in range(2)]

    def end(self, m, i):
        position = (i + 1) * self.chunk - 1
        return sum(jnp.where(total <= position, 1, 0) for total in self.sums[m])

    def tables(self, cosine, sine, seg_col, seg_row):
        chunk = self.chunk
        base = (4 * self.p.f + self.p.z) * chunk
        shape = (chunk, DH)
        lane = lax.broadcasted_iota(jnp.int32, shape, 1)
        row = lax.broadcasted_iota(jnp.int32, shape, 0) + base
        half = DH // 2
        turn = lane % half
        speed = jnp.right_shift(jnp.full(shape, 651, jnp.int32), turn * 10 // half) + 1
        angle = ((row * speed) % 4096).astype(F32) * (2.0 * math.pi / 4096.0)
        cos, sin = jnp.cos(angle), jnp.sin(angle)
        sin = jnp.where(lane < half, -sin, sin)
        down = lax.broadcasted_iota(jnp.int32, (chunk, 1), 0) + base
        across = lax.broadcasted_iota(jnp.int32, (1, chunk), 1) + base
        for m in range(2):
            at = slice(m * chunk, (m + 1) * chunk)
            cosine[at, :] = cos
            sine[at, :] = sin
            seg_col[at, :] = sum(jnp.where(total <= down, 1, 0) for total in self.sums[m])
            seg_row[m : m + 1, :] = sum(jnp.where(total <= across, 1, 0) for total in self.sums[m])

    def power(self, same, chunks, hh):
        rate = self.decay[2 * self.p.z + hh]
        gap = jnp.asarray(chunks * self.chunk, jnp.int32).astype(F32)
        value = jnp.exp(jnp.full((1, DH), -rate * gap, F32))
        return jnp.where(same, value, 0.0)

    def to_total(self, m, i, hh):
        ends = self.ends[m]
        if self.backward:
            return self.power(ends[i] == ends[0], i, hh)
        return self.power(ends[i + 1] == ends[4], 3 - i, hh)

    def to_place(self, m, i, hh):
        ends = self.ends[m]
        if self.backward:
            return self.power(ends[i + 1] == ends[4], 3 - i, hh)
        return self.power(ends[i] == ends[0], i, hh)

    def from_group(self, m, g, hh):
        f = self.p.f
        if self.backward:
            before = self.groups[m][g - 1] if g > 0 else 0
            same = (self.ends[m][4] == before) & (g > f)
            return self.power(same, 4 * jnp.maximum(g - 1 - f, 0), hh)
        same = (self.ends[m][0] == self.groups[m][g]) & (g < f)
        return self.power(same, 4 * jnp.maximum(f - 1 - g, 0), hh)

    def others(self, i):
        return range(i + 1, 4) if self.backward else range(i)

    def between(self, m, i, j, hh):
        ends = self.ends[m]
        if self.backward:
            return self.power(ends[i + 1] == ends[j], j - 1 - i, hh)
        return self.power(ends[i] == ends[j + 1], i - 1 - j, hh)


class Scan:
    def __init__(self, place, weigh, states, inbox, totals, outbox, result, send, recv):
        self.p, self.weigh = place, weigh
        self.states, self.inbox, self.totals = states, inbox, totals
        self.outbox, self.result = outbox, result
        self.send, self.recv = send, recv

    def copy(self, src, dst, n, where):
        return pltpu.make_async_remote_copy(
            src_ref=src,
            dst_ref=dst,
            send_sem=self.send.at[n],
            recv_sem=self.recv.at[n],
            device_id=where,
            device_id_type=MESH,
        )

    def to_heads(self, i):
        z = self.p.zs[i]
        return self.copy(self.states.at[pl.ds(2 * z, 2)], self.inbox.at[self.p.z], i, self.p.at(z=z))

    def from_heads(self, i):
        z = self.p.zs[i]
        return self.copy(
            self.outbox.at[z], self.result.at[pl.ds(2 * self.p.z, 2)], 9 + i, self.p.at(z=z)
        )

    def total(self, n, origin, where):
        return self.copy(self.totals.at[origin], self.totals.at[origin], n, self.p.at(f=where))

    def start(self):
        p = self.p
        for i in range(3):
            self.to_heads(i).start()
        self.inbox[p.z] = self.states[pl.ds(2 * p.z, 2)]

    def totals_out(self):
        p = self.p
        for i in range(3):
            self.to_heads(i).wait()
        for hh in range(2):
            for m in range(2):
                acc = sum(
                    self.weigh.to_total(m, i, hh) * self.inbox[i, hh, m].astype(F32)
                    for i in range(4)
                )
                self.totals[p.f, hh, m] = acc.astype(BF16)
        for n, where in ((3, p.fx), (4, p.fy), (5, p.fxy)):
            self.total(n, p.f, where).start()
        self.total(12, p.f, p.fc).start()

    def forward(self):
        p = self.p
        for n, where in ((3, p.fx), (4, p.fy), (5, p.fxy)):
            self.total(n, p.f, where).wait()
            self.total(n + 3, where, p.fc).start()

    def results_out(self):
        p = self.p
        self.total(12, p.f, p.fc).wait()
        for n, where in ((3, p.fx), (4, p.fy), (5, p.fxy)):
            self.total(n + 3, where, p.fc).wait()
        for hh in range(2):
            for m in range(2):
                outer = sum(
                    self.weigh.from_group(m, g, hh) * self.totals[g, hh, m].astype(F32)
                    for g in range(8)
                )
                for i in range(4):
                    acc = self.weigh.to_place(m, i, hh) * outer
                    for j in self.weigh.others(i):
                        acc += self.weigh.between(m, i, j, hh) * self.inbox[j, hh, m].astype(F32)
                    self.outbox[i, hh, m] = acc.astype(BF16)
        for i in range(3):
            self.from_heads(i).start()
        self.result[pl.ds(2 * p.z, 2)] = self.outbox[p.z]

    def finish(self):
        for i in range(3):
            self.from_heads(i).wait()


def edge(seg, mark, rate, gap):
    return jnp.where(seg == mark, jnp.exp(-rate * gap), 0.0)


def decays(rate, rows):
    up = lax.broadcasted_iota(jnp.int32, (rows, rows), 0)
    across = lax.broadcasted_iota(jnp.int32, (rows, rows), 1)
    gap = (up - across).astype(F32)
    return jnp.where(gap >= 0.0, jnp.exp(-rate * jnp.maximum(gap, 0.0)), 0.0)


def up_tile(a2, w1, w2, s, dp1, dp2, t):
    at = cols(t * TILE, TILE)
    first = kdot(a2[...], w1[:, at])
    second = kdot(a2[...], w2[:, at])
    ds = dp1[:, at].astype(F32)
    s[:, at] = (first * second).astype(BF16)
    dp1[:, at] = (ds * second).astype(BF16)
    dp2[:, at] = (ds * first).astype(BF16)


def forward_kernel(
    lengths, decay_rate, x, dy,
    wq, wk, wv, wu, wo, w1, w2, wd,
    mix_o, wo_o, w1_o, w2_o, wd_o, q_o, k_o, v_o, u_o, qp_o, kp_o, ob_o, hid_o, dp1_o, dp2_o, s_o,
    state_o, a2_o, a1t_o, a2t_o, gt_o, dyt_o,
    fm, fo, f1, f2, fd, a1, q, k, v, u, qp, kp, att, ob, g, hid, dp1, dp2, s,
    cosine, sine, seg_col, seg_row, a1t, a2t, gt, dyt, states, inbox, totals, outbox, result,
    send, recv, own_sem, save_sem, scan_send, scan_recv,
):
    place = Place()
    f = place.f
    rows, width = x.shape
    chunk = rows // 2
    hidden_size = w1.shape[1]
    half_hidden = hidden_size // 2
    place.greet()

    pieces = []
    for i, w in ((1, wk), (2, wv), (0, wq), (3, wu)):
        pieces.append((w, fm, (0, 128), (0, width), i * width))
    for part in range(2):
        pieces.append((wd, fd, (part * half_hidden, half_hidden), (0, 128), None))
    pieces.append((wo, fo, (0, 128), (0, width), 0))
    for part in range(2):
        for w, full in ((w1, f1), (w2, f2)):
            at = part * half_hidden
            pieces.append((w, full, (0, 128), (at, half_hidden), at))
    w, full, _, (at, size), _ = pieces.pop()
    first = (size // 2 + 127) // 128 * 128
    pieces.append((w, full, (0, 128), (at, first), at))
    pieces.append((w, full, (0, 128), (at + first, size - first), at + first))
    count = len(pieces)
    parity = place.z % 2

    def parts(n):
        thin = (3, 2)[n % 2]
        wide = 8 - thin
        near = (wide + (n // 2) % 2) // 2
        fetch = (parity * thin, wide)
        return {
            "all": (0, 8),
            "fetch": fetch,
            "near": (fetch[0], near),
            "far": (fetch[0] + near, wide - near),
            "give": (parity * wide, thin),
            "take": ((1 - parity) * wide, thin),
        }

    def own(n, part="all"):
        w, _, (r, rs), (c, cs), _ = pieces[n]
        at, size = parts(n)[part]
        eighth = rs // 8
        return w.at[pl.ds(pl.multiple_of(r + at * eighth, 16), size * eighth), pl.ds(c, cs)]

    def block(n, origin, part="all"):
        _, full, (r, rs), (c, cs), to = pieces[n]
        at, size = parts(n)[part]
        eighth = rs // 8
        if to is None:
            start = pl.multiple_of(r + at * eighth, 16)
            return full.at[pl.ds(start, size * eighth), cols(origin * 128, 128)]
        start = pl.multiple_of(origin * 128 + at * eighth, 16)
        return full.at[pl.ds(start, size * eighth), pl.ds(to, cs)]

    fc, fx, fy, fxy = place.fc, place.fx, place.fy, place.fxy
    at_c, at_x, at_y = (place.at(f=o) for o in (fc, fx, fy))
    at_z = place.at(z=place.zs[0])

    def step(n, t):
        fetched = own(n, "fetch"), block(n, f, "fetch")
        src, dst, where, lands = [
            (own(n), block(n, f), at_c, (fc, "all")),
            (*fetched, at_x, (fx, "fetch")),
            (*fetched, at_y, (fy, "fetch")),
            (block(n, fx, "near"), None, at_y, (fxy, "near")),
            (block(n, fy, "far"), None, at_x, (fxy, "far")),
            (block(n, fx, "give"), None, at_z, (fx, "take")),
            (block(n, fy, "give"), None, at_z, (fy, "take")),
            (block(n, fxy, "give"), None, at_z, (fxy, "take")),
            (block(n, fx), None, at_c, (flip(fx, 1), "all")),
            (block(n, fy), None, at_c, (flip(fy, 1), "all")),
            (block(n, fxy), None, at_c, (flip(fxy, 1), "all")),
        ][t]
        return src, src if dst is None else dst, where, block(n, *lands)

    def move(n, t, src, dst, where):
        return pltpu.make_async_remote_copy(
            src_ref=src,
            dst_ref=dst,
            send_sem=send.at[n * 11 + t],
            recv_sem=recv.at[n * 11 + t],
            device_id=where,
            device_id_type=MESH,
        )

    def go(n, t):
        src, dst, where, _ = step(n, t)
        move(n, t, src, dst, where).start()

    def got(n, *which):
        for t in which:
            _, _, where, lands = step(n, t)
            move(n, t, lands, lands, where).wait_recv()

    def own_copy(n):
        return pltpu.make_async_copy(own(n), block(n, f), own_sem.at[n])

    saves = []

    def save(src, dst):
        copy = pltpu.make_async_copy(src, dst, save_sem.at[len(saves)])
        copy.start()
        saves.append(copy)

    def save_piece(n):
        full_o = {id(fm): mix_o, id(fo): wo_o, id(f1): w1_o, id(f2): w2_o, id(fd): wd_o}
        _, full, (r, rs), (c, cs), to = pieces[n]
        out = full_o[id(full)]
        if to is None:
            save(full.at[pl.ds(r, rs)], out.at[pl.ds(r, rs)])
        else:
            save(full.at[:, pl.ds(to, cs)], out.at[:, pl.ds(to, cs)])

    def norm_in():
        @pl.loop(0, rows // 128)
        def _(t):
            at = pl.ds(pl.multiple_of(t * 128, 128), 128)
            value = x[at, :].astype(F32)
            scale = lax.rsqrt(jnp.mean(value * value, axis=-1, keepdims=True) + EPSILON)
            a1[at, :] = (value * scale).astype(BF16)

    def turn_over(src, dst):
        @pl.loop(0, width // 128)
        def _(b):
            other_c = (b + f) % 2
            other_x = (b // 2 + f // 2) % 2
            other_y = (b // 4 + f // 4) % 2
            slot = other_c * 4 + other_y * 2 + other_x
            value = src[:, cols(b * 128, 128)].astype(F32)
            dst[pl.ds(pl.multiple_of(slot * 128, 128), 128), :] = value.T.astype(BF16)

    def project(base, pre, low, turn):
        @pl.loop(0, width // TILE)
        def _(t):
            at = cols(t * TILE, TILE)
            acc = kdot(a1[...], fm[:, cols(base + t * TILE, TILE)])
            if not turn:
                low[:, at] = acc.astype(BF16)
                return
            pre[:, at] = acc.astype(BF16)
            acc = acc * lax.logistic(acc)
            turned = []
            for hh in range(TILE // DH):
                piece = acc[:, hh * DH : (hh + 1) * DH]
                turned.append(piece * cosine[...] + pltpu.roll(piece, DH // 2, 1) * sine[...])
            low[:, at] = jnp.concatenate(turned, axis=1).astype(BF16)

    offset = lax.broadcasted_iota(jnp.int32, (chunk, 1), 0).astype(F32)
    weigh = Weigh(place, lengths, decay_rate, chunk, False)
    scan = Scan(place, weigh, states, inbox, totals, outbox, result, scan_send, scan_recv)

    def local_states():
        @pl.loop(0, H)
        def _(h):
            at = cols(h * DH, DH)
            for m in range(2):
                r = slice(m * chunk, (m + 1) * chunk)
                leaving = edge(seg_col[r], weigh.last[m], decay_rate[h], chunk - 1.0 - offset)
                left = (k[r, at].astype(F32) * leaving).astype(BF16)
                states[h, m] = kdot(left, v[r, at], ((0,), (0,))).astype(BF16)

    def attend_local(first, last):
        @pl.loop(first, last)
        def _(h):
            at = cols(h * DH, DH)
            decay = decays(decay_rate[h], chunk)
            for m in range(2):
                r = slice(m * chunk, (m + 1) * chunk)
                within = jnp.where(seg_col[r] == seg_row[m : m + 1], decay, 0.0)
                scores = kdot(q[r, at], k[r, at], ((1,), (1,))) * within
                att[r, at] = kdot(scores.astype(BF16), v[r, at])

    def attend_rest():
        @pl.loop(0, H)
        def _(h):
            at = cols(h * DH, DH)
            for m in range(2):
                r = slice(m * chunk, (m + 1) * chunk)
                entering = edge(seg_col[r], weigh.before[m], decay_rate[h], offset + 1.0)
                ob[r, at] = (att[r, at] + entering * kdot(q[r, at], result[h, m])).astype(BF16)

    def hidden():
        @pl.loop(0, rows // 128)
        def _(t):
            at = pl.ds(pl.multiple_of(t * 128, 128), 128)
            value = ob[at, :].astype(F32)
            scale = lax.rsqrt(jnp.mean(value * value, axis=-1, keepdims=True) + EPSILON)
            g[at, :] = (value * scale * u[at, :].astype(F32)).astype(BF16)

        turn_over(g, gt)
        save(gt, gt_o)

        @pl.loop(0, width // TILE)
        def _(t):
            at = cols(t * TILE, TILE)
            hid[:, at] = x[:, at].astype(F32) + kdot(g[...], fo[:, at])

        @pl.loop(0, rows // 128)
        def _(t):
            at = pl.ds(pl.multiple_of(t * 128, 128), 128)
            value = hid[at, :]
            scale = lax.rsqrt(jnp.mean(value * value, axis=-1, keepdims=True) + EPSILON)
            g[at, :] = (value * scale).astype(BF16)

    def inner(part):
        @pl.loop(0, half_hidden // 128)
        def _(t):
            start = part * half_hidden + t * 128
            rhs = fd[pl.ds(pl.multiple_of(start, 128), 128), :]
            dp1[:, cols(start, 128)] = kdot(dy[...], rhs, ((1,), (1,))).astype(BF16)

    def up():
        @pl.loop(0, half_hidden // TILE)
        def _(t):
            up_tile(g, f1, f2, s, dp1, dp2, t)

    def work(n):
        if n == 0:
            project(width, kp, k, True)
            save(k, k_o)
            save(kp, kp_o)
        elif n == 1:
            project(2 * width, None, v, False)
            local_states()
            scan.start()
            save(v, v_o)
        elif n == 2:
            project(0, qp, q, True)
            save(q, q_o)
            save(qp, qp_o)
        elif n == 3:
            project(3 * width, None, u, False)
            save(u, u_o)
            scan.totals_out()
        elif n == 4:
            attend_local(0, H // 2)
            scan.forward()
        elif n == 5:
            attend_local(H // 2, H)
            scan.results_out()
        elif n == 6:
            inner(0)
            inner(1)
        elif n == 7:
            scan.finish()
            save(result, state_o)
            attend_rest()
            save(ob, ob_o)
            hidden()
            save(hid, hid_o)
            save(g, a2_o)
        elif n == 8:
            up()
            done = pl.ds(0, half_hidden // TILE * TILE)
            save(s.at[:, done], s_o.at[:, done])
            save(dp1, dp1_o)
            save(dp2.at[:, done], dp2_o.at[:, done])
        elif n == 9:
            turn_over(g, a2t)
            save(a2t, a2t_o)

    def early(n):
        if n == 0:
            turn_over(dy, dyt)
            save(dyt, dyt_o)
        elif n == 1:
            turn_over(a1, a1t)
            save(a1t, a1t_o)

    ahead = 2
    for n in range(ahead):
        for t in (1, 2, 0):
            go(n, t)
        own_copy(n).start()
    weigh.tables(cosine, sine, seg_col, seg_row)
    norm_in()
    for n in range(count + 3):
        if n < count:
            got(n, 1)
            go(n, 3)
            go(n, 5)
            got(n, 2)
            go(n, 4)
            go(n, 6)
            if n + ahead < count:
                for t in (1, 2, 0):
                    go(n + ahead, t)
                own_copy(n + ahead).start()
        if 0 <= n - 1 < count:
            got(n - 1, 3, 4)
            go(n - 1, 7)
            got(n - 1, 5)
            go(n - 1, 8)
            got(n - 1, 6)
            go(n - 1, 9)
        if 0 <= n - 2 < count:
            got(n - 2, 7)
            go(n - 2, 10)
        if n - 3 >= 0:
            got(n - 3, 0, 8, 9, 10)
            own_copy(n - 3).wait()
            save_piece(n - 3)
            work(n - 3)
        else:
            early(n)
    for n in range(count):
        for t in range(11):
            src, dst, where, _ = step(n, t)
            move(n, t, src, dst, where).wait_send()
    for copy in saves:
        copy.wait()


def run_forward(lengths, decay_rate, x, dy, weights):
    rows, width = x.shape
    hidden_size = weights[5].shape[1]
    row = jax.ShapeDtypeStruct((rows, width), BF16)
    tall = jax.ShapeDtypeStruct((rows, hidden_size), BF16)
    outs = (
        [
            jax.ShapeDtypeStruct(shape, BF16)
            for shape in (
                (width, 4 * width), (width, width), (width, hidden_size), (width, hidden_size),
                (hidden_size, width),
            )
        ]
        + [row] * 7
        + [jax.ShapeDtypeStruct((rows, width), F32)]
        + [tall] * 3
        + [jax.ShapeDtypeStruct((H, 2, DH, DH), BF16), row]
        + [jax.ShapeDtypeStruct((width, rows), BF16)] * 4
    )
    rv = pltpu.VMEM((rows, width), BF16)
    tv = pltpu.VMEM((rows, hidden_size), BF16)
    scratch = (
        [pltpu.VMEM(o.shape, BF16) for o in outs[:5]]
        + [rv] * 7
        + [pltpu.VMEM((rows, width), F32), rv, rv, pltpu.VMEM((rows, width), F32)]
        + [tv] * 3
        + table_scratch(rows)
        + [pltpu.VMEM((width, rows), BF16)] * 4
        + scan_scratch()
        + [pltpu.SemaphoreType.DMA((132,))] * 2
        + [pltpu.SemaphoreType.DMA((12,)), pltpu.SemaphoreType.DMA((29,))]
        + [pltpu.SemaphoreType.DMA((13,))] * 2
    )
    return pl.pallas_call(
        forward_kernel,
        out_shape=outs,
        in_specs=[SMEM, SMEM] + [VMEM] * 2 + [ANY] * 8,
        out_specs=[ANY] * len(outs),
        scratch_shapes=scratch,
        compiler_params=pltpu.CompilerParams(
            collective_id=0, has_side_effects=True, vmem_limit_bytes=VMEM_BYTES
        ),
        name="forward",
    )(lengths, decay_rate, x, dy, *weights)


def table_scratch(rows):
    return [
        pltpu.VMEM((rows, DH), F32),
        pltpu.VMEM((rows, DH), F32),
        pltpu.VMEM((rows, 1), jnp.int32),
        pltpu.VMEM((2, rows // 2), jnp.int32),
    ]


def scan_scratch():
    return [
        pltpu.VMEM((H, 2, DH, DH), BF16),
        pltpu.VMEM((4, 2, 2, DH, DH), BF16),
        pltpu.VMEM((8, 2, 2, DH, DH), BF16),
        pltpu.VMEM((4, 2, 2, DH, DH), BF16),
        pltpu.VMEM((H, 2, DH, DH), BF16),
    ]


UPRIGHT = 256
LAG = 2
WITH_UPRIGHT = (0, 1, 2, 3, 4, 8, 9, 10, 11, 12, 13)
LAST = 1024


def backward_kernel(
    lengths, decay_rate,
    x_i, dy_i, wm_i, wo_i, w1_i, w2_i, wd_i, q_i, k_i, v_i, u_i, qp_i, kp_i, ob_i, hid_i,
    p1_i, p2_i, s_i, state_i, a2_i, a1t_i, a2t_i, gt_i, dyt_i,
    mixed_o, grad_x_o, gq_o, gk_o, gv_o, gu_o, go_o, g1_o, g2_o, gd_o,
    wd, w1, w2, s, p1, p2, dy, hid, dh, dz, ob, u, q, k, v, dqp, dkp, dv, state_in,
    cosine, sine, seg_col, seg_row, a1t, a2t, gt, dyt, states, inbox, totals, outbox, result,
    give, take, merged, take_a, take_b, half_a, half_b, take2, mine, take3, pair, take4, final,
    z_take, z_sum, z_take2, z_sum2, z_take_a, z_take_b, z_half_a, z_half_b, z_take3,
    send, recv, free, load_sem, out_sem, scan_send, scan_recv,
):
    place = Place()
    rows, width = dy.shape
    chunk = rows // 2
    hidden_size = s.shape[1]
    place.greet()

    loads = {}

    def load(name, src, dst):
        copy = pltpu.make_async_copy(src, dst, load_sem.at[len(loads)])
        copy.start()
        loads[name] = copy

    def ready(*names):
        for name in names:
            loads[name].wait()

    done = pl.ds(0, hidden_size // 2 // TILE * TILE)
    for name, src, dst in (
        ("dyt", dyt_i, dyt), ("s", s_i.at[:, done], s.at[:, done]), ("a2t", a2t_i, a2t), ("p1", p1_i, p1),
        ("p2", p2_i.at[:, done], p2.at[:, done]), ("a2", a2_i, dkp), ("w1", w1_i, w1), ("w2", w2_i, w2),
        ("hid", hid_i, hid), ("wd", wd_i, wd), ("dy", dy_i, dy), ("ob", ob_i, ob), ("u", u_i, u), ("q", q_i, q), ("gt", gt_i, gt),
        ("k", k_i, k), ("v", v_i, v), ("state", state_i, state_in), ("a1t", a1t_i, a1t),
    ):
        load(name, src, dst)

    pieces = []
    for start in range(0, hidden_size, 1024):
        size = min(1024, hidden_size - start)
        for left, right, out in ((dyt, s, gd_o), (a2t, p1, g1_o), (a2t, p2, g2_o)):
            pieces.append((left, right, out, start, size))
    for left, right, out in ((gt, dz, go_o), (a1t, u, gu_o), (a1t, dqp, gq_o), (a1t, dkp, gk_o)):
        pieces.append((left, right, out, 0, width))
    for start in range(0, width, LAST):
        pieces.append((a1t, dv, gv_o, start, LAST))
    count = len(pieces)
    steps = count + 1 + 4 * LAG
    low, high = place.z % 2, place.z // 2
    f = place.f
    at_c, at_x, at_y = (place.at(f=o) for o in (place.fc, place.fx, place.fy))
    at_z1, at_z2 = (place.at(z=place.zs[i]) for i in range(2))
    partner = [at_c, at_x, at_y, at_y, at_x, at_z1, at_z2]
    partner += [at_z1, at_z2, at_x, at_y, at_y, at_x]
    quarter_size = UPRIGHT // 2
    lo, hi = pl.ds(0, quarter_size), pl.ds(quarter_size, quarter_size)

    def upright(n):
        return n in WITH_UPRIGHT

    def half_of(n):
        return (pieces[n][4] - UPRIGHT * upright(n)) // 2

    def of(n, *which):
        return [t for t in which if t < 7 or upright(n)]

    def move(n, t):
        size = pieces[n][4]
        c, m, half = n % 2, n % 3, half_of(n)
        a, b, ab, last = (pl.ds(*at) for at in ((0, half), (half, half), (0, 2 * half), (2 * half, UPRIGHT)))
        src, dst = [
            lambda: (give.at[c, :, pl.ds(0, size)], take.at[c, :, pl.ds(0, size)]),
            lambda: (merged.at[m, :, 1, :, :, :, a], take_a.at[m, :, :, :, :, a]),
            lambda: (merged.at[m, 1, :, :, :, :, b], take_b.at[m, :, :, :, :, a]),
            lambda: (half_a.at[m, 1, :, :, :, a], take2.at[m, 0, :, :, :, a]),
            lambda: (half_b.at[m, 1, :, :, :, a], take2.at[m, 1, :, :, :, a]),
            lambda: (mine.at[m, :, 1 - low, :, ab], take3.at[m, :, :, ab]),
            lambda: (pair.at[m, 1 - high, :, ab], take4.at[m, :, ab]),
            lambda: (merged.at[m, :, :, :, 1 - low, :, last], z_take.at[m]),
            lambda: (z_sum.at[m, :, :, 1 - high], z_take2.at[m]),
            lambda: (z_sum2.at[m, :, 1, :, lo], z_take_a.at[m]),
            lambda: (z_sum2.at[m, 1, :, :, hi], z_take_b.at[m]),
            lambda: (z_half_a.at[m, 1], z_take3.at[m, 0]),
            lambda: (z_half_b.at[m, 1], z_take3.at[m, 1]),
        ][t]()
        return pltpu.make_async_remote_copy(
            src_ref=src,
            dst_ref=dst,
            send_sem=send.at[3 * t + m],
            recv_sem=recv.at[3 * t + m],
            device_id=partner[t],
            device_id_type=MESH,
        )

    def go(n, t):
        move(n, t).start()

    def reuse(n, *which):
        for t in which:
            earlier = n - (2 if t == 0 else 3)
            if earlier >= 0 and of(earlier, t):
                move(earlier, t).wait_send()

    def got(n, t):
        move(n, t).wait_recv()

    near = (at_c, at_x, at_y, at_z1, at_z2)

    def freed(n):
        if n < steps - 1:
            for i, where in enumerate(near):
                pl.semaphore_signal(free.at[i], 1, device_id=where, device_id_type=MESH)

    def allowed(n):
        if n >= 1:
            for i in range(len(near)):
                pl.semaphore_wait(free.at[i], 1)

    def give_half(n):
        left, right, _, start, size = pieces[n]
        slot = n % 2
        reuse(n, 0)

        @pl.loop(0, size // TILE)
        def _(t):
            value = kdot(left[rows : 2 * rows, :], right[:, cols(start + t * TILE, TILE)])
            give[slot, :, cols(t * TILE, TILE)] = value.astype(BF16)


    def merge(n):
        left, right, _, start, size = pieces[n]
        slot, m = n % 2, n % 3
        got(n, 0)
        reuse(n, 1, 2, 7)

        @pl.loop(0, size // TILE)
        def _(t):
            at = cols(t * TILE, TILE)
            value = kdot(left[0:rows, :], right[:, cols(start + t * TILE, TILE)])
            value = (value + take[slot, :, at].astype(F32)).astype(BF16)
            for i in range(16):
                r = i * 32
                merged[m, i // 8, i // 4 % 2, i // 2 % 2, i % 2, :, at] = value[r : r + 32]

        for t in of(n, 7, 1, 2):
            go(n, t)

    def add(a, b):
        return a.astype(F32) + b.astype(F32)

    def halve(n):
        m, half = n % 3, half_of(n)
        reuse(n, 8)
        if upright(n):
            got(n, 7)
            c = slice(2 * half, 2 * half + UPRIGHT)
            for y in range(2):
                z_sum[m, y] = add(merged[m, y, :, :, low, :, c], z_take[m, y]).astype(BF16)
            go(n, 8)
        got(n, 1)
        reuse(n, 3)
        for i in (1, 0):
            half_a[m, i, :, :, :, :half] = add(
                merged[m, i, 0, :, :, :, :half], take_a[m, i, :, :, :, :half]
            ).astype(BF16)
        go(n, 3)
        got(n, 2)
        reuse(n, 4)
        for i in (1, 0):
            half_b[m, i, :, :, :, :half] = add(
                merged[m, 0, i, :, :, :, half : 2 * half], take_b[m, i, :, :, :, :half]
            ).astype(BF16)
        go(n, 4)

    def quarter(n):
        m, half = n % 3, half_of(n)
        reuse(n, 9, 10)
        if upright(n):
            got(n, 8)
            z_sum2[m] = add(z_sum[m, :, :, high], z_take2[m]).astype(BF16)
            go(n, 9)
            go(n, 10)
        reuse(n, 5)
        for t, kept, at in ((3, half_a, slice(0, half)), (4, half_b, slice(half, 2 * half))):
            got(n, t)
            mine[m, :, :, :, at] = add(
                kept[m, 0, :, :, :, :half], take2[m, t - 3, :, :, :, :half]
            ).astype(BF16)
        go(n, 5)

    def along(n):
        m, whole = n % 3, 2 * half_of(n)
        reuse(n, 11, 12)
        if upright(n):
            got(n, 9)
            z_half_a[m] = add(z_sum2[m, :, 0, :, :quarter_size], z_take_a[m]).astype(BF16)
            go(n, 11)
            got(n, 10)
            z_half_b[m] = add(z_sum2[m, 0, :, :, quarter_size:], z_take_b[m]).astype(BF16)
            go(n, 12)
        got(n, 5)
        reuse(n, 6)
        for i in range(2):
            pair[m, i, :, :whole] = add(
                mine[m, i, low, :, :whole], take3[m, i, :, :whole]
            ).astype(BF16)
        go(n, 6)

    def final_copy(n):
        _, _, out, start, size = pieces[n]
        m = n % 3
        return pltpu.make_async_copy(
            final.at[m, :, pl.ds(0, size)], out.at[:, pl.ds(start, size)], out_sem.at[m]
        )

    def end(n):
        m, whole = n % 3, 2 * half_of(n)
        if n >= 3:
            final_copy(n - 3).wait()
        for t in of(n, 11, 12):
            i, kept = t - 11, (z_half_a, z_half_b)[t - 11]
            got(n, t)
            at = slice(whole + i * quarter_size, whole + (i + 1) * quarter_size)
            final[m, :, at] = add(kept[m, 0], z_take3[m, i])
        got(n, 6)
        final[m, :, :whole] = add(pair[m, high, :, :whole], take4[m, :, :whole])
        final_copy(n).start()

    offset = lax.broadcasted_iota(jnp.int32, (chunk, 1), 0).astype(F32)
    weigh = Weigh(place, lengths, decay_rate, chunk, True)
    scan = Scan(place, weigh, states, inbox, totals, outbox, result, scan_send, scan_recv)

    def row_tiles(body):
        @pl.loop(0, rows // 128)
        def _(t):
            body(pl.ds(pl.multiple_of(t * 128, 128), 128))

    def up():
        ready("a2", "w1", "w2")

        @pl.loop(hidden_size // 2 // TILE, hidden_size // TILE)
        def _(t):
            up_tile(dkp, w1, w2, s, p1, p2, t)

    def mix():
        ready("wd")

        @pl.loop(0, width // TILE)
        def _(t):
            at = cols(t * TILE, TILE)
            dqp[:, at] = (hid[:, at] + kdot(s[...], wd[:, at])).astype(BF16)

        load("mixed", dqp, mixed_o)
        load("wo", wo_i, wd.at[pl.ds(0, width)])

    def middle(first, last):
        @pl.loop(first, last)
        def _(t):
            r = pl.ds(pl.multiple_of(t * TILE, TILE), TILE)
            dh[:, cols(t * TILE, TILE)] = kdot(p1[...], w1[r, :], ((1,), (1,))) + kdot(
                p2[...], w2[r, :], ((1,), (1,))
            )

    def middle_rows():
        ready("dy")
        load("wq", wm_i.at[:, pl.ds(0, 2 * width)], w1.at[:, pl.ds(0, 2 * width)])
        load("wv", wm_i.at[:, pl.ds(2 * width, 2 * width)], w2.at[:, pl.ds(0, 2 * width)])

        def body(at):
            value = hid[at, :]
            scale = lax.rsqrt(jnp.mean(value * value, axis=-1, keepdims=True) + EPSILON)
            normed = value * scale
            grad = dh[at, :]
            mean = jnp.mean(grad * normed, axis=-1, keepdims=True)
            grad = dy[at, :].astype(F32) + scale * (grad - normed * mean)
            dh[at, :] = grad
            dz[at, :] = grad.astype(BF16)

        row_tiles(body)
        load("x", x_i, dy)

    def outer():
        ready("wo", "ob", "u")

        @pl.loop(0, width // TILE)
        def _(t):
            r = pl.ds(pl.multiple_of(t * TILE, TILE), TILE)
            hid[:, cols(t * TILE, TILE)] = kdot(dz[...], wd[r, :], ((1,), (1,)))

        def body(at):
            value = ob[at, :].astype(F32)
            scale = lax.rsqrt(jnp.mean(value * value, axis=-1, keepdims=True) + EPSILON)
            normed = value * scale
            grad = hid[at, :]
            dm = grad * u[at, :].astype(F32)
            u[at, :] = (grad * normed).astype(BF16)
            mean = jnp.mean(dm * normed, axis=-1, keepdims=True)
            ob[at, :] = (scale * (dm - normed * mean)).astype(BF16)

        row_tiles(body)

        @pl.loop(0, H)
        def _(h):
            at = cols(h * DH, DH)
            for m in range(2):
                r = slice(m * chunk, (m + 1) * chunk)
                entering = edge(seg_col[r], weigh.before[m], decay_rate[h], offset + 1.0)
                left = (q[r, at].astype(F32) * entering).astype(BF16)
                states[h, m] = kdot(left, ob[r, at], ((0,), (0,))).astype(BF16)

        scan.start()

    def slope(pre):
        sig = lax.logistic(pre)
        return sig * (1.0 + pre * (1.0 - sig))

    def turned_back(grad, r, base, h):
        grad = grad.astype(BF16).astype(F32)
        back = grad * cosine[r, :] - pltpu.roll(grad, DH // 2, 1) * sine[r, :]
        return (slope(s[r, cols(base + h * DH, DH)].astype(F32)) * back).astype(BF16)

    def attend_queries(first, last):
        @pl.loop(first, last)
        def _(h):
            at = cols(h * DH, DH)
            decay = decays(decay_rate[h], chunk)
            for m in range(2):
                r = slice(m * chunk, (m + 1) * chunk)
                within = jnp.where(seg_col[r] == seg_row[m : m + 1], decay, 0.0)
                entering = edge(seg_col[r], weigh.before[m], decay_rate[h], offset + 1.0)
                oh = ob[r, at]
                grads = (kdot(oh, v[r, at], ((1,), (1,))) * within).astype(BF16)
                dq = kdot(grads, k[r, at]) + entering * kdot(oh, state_in[h, m], ((1,), (1,)))
                dqp[r, at] = turned_back(dq, r, 0, h)

    def attend_keys(first, last):
        @pl.loop(first, last)
        def _(h):
            at = cols(h * DH, DH)
            decay = decays(decay_rate[h], chunk)
            for m in range(2):
                r = slice(m * chunk, (m + 1) * chunk)
                within = jnp.where(seg_col[r] == seg_row[m : m + 1], decay, 0.0)
                leaving = edge(seg_col[r], weigh.last[m], decay_rate[h], chunk - 1.0 - offset)
                qh, kh, vh, oh = q[r, at], k[r, at], v[r, at], ob[r, at]
                grads = (kdot(oh, vh, ((1,), (1,))) * within).astype(BF16)
                dk = kdot(grads, qh, ((0,), (0,)))
                dk = dk + leaving * kdot(vh, result[h, m], ((1,), (1,)))
                scores = (kdot(qh, kh, ((1,), (1,))) * within).astype(BF16)
                grad_v = kdot(scores, oh, ((0,), (0,))) + leaving * kdot(kh, result[h, m])
                dv[r, at] = grad_v.astype(BF16)
                dkp[r, at] = turned_back(dk, r, width, h)

    def inputs(first, last):
        @pl.loop(first, last)
        def _(t):
            r = pl.ds(pl.multiple_of(t * TILE, TILE), TILE)
            acc = kdot(dqp[...], w1[r, 0:width], ((1,), (1,)))
            acc += kdot(dkp[...], w1[r, width : 2 * width], ((1,), (1,)))
            acc += kdot(dv[...], w2[r, 0:width], ((1,), (1,)))
            acc += kdot(u[...], w2[r, width : 2 * width], ((1,), (1,)))
            hid[:, cols(t * TILE, TILE)] = acc

    def inputs_rows():
        def body(at):
            value = dy[at, :].astype(F32)
            scale = lax.rsqrt(jnp.mean(value * value, axis=-1, keepdims=True) + EPSILON)
            normed = value * scale
            grad = hid[at, :]
            mean = jnp.mean(grad * normed, axis=-1, keepdims=True)
            dz[at, :] = (dh[at, :] + scale * (grad - normed * mean)).astype(BF16)

        row_tiles(body)
        load("grad_x", dz, grad_x_o)

    def work(n):
        if n == 0:
            weigh.tables(cosine, sine, seg_col, seg_row)
            ready("a2t", "p1", "p2")
        elif n == 1:
            up()
        elif n == 2:
            middle(0, 2)
        elif n == 3:
            middle(2, 4)
            ready("hid")
            middle_rows()
        elif n == 4:
            mix()
            ready("q")
        elif n == 5:
            load("qp", qp_i, s.at[:, pl.ds(0, width)])
            load("kp", kp_i, s.at[:, pl.ds(width, width)])
            outer()
        elif n == 6:
            ready("k", "v", "state", "qp", "kp", "mixed")
            attend_queries(0, H // 2)
        elif n == 7:
            attend_queries(H // 2, H)
            scan.totals_out()
        elif n == 8:
            ready("gt", "a1t")
        elif n == 9:
            scan.forward()
            scan.results_out()
        elif n == 11:
            scan.finish()
            attend_keys(0, H // 2)
            attend_keys(H // 2, H)
            ready("wq", "wv", "x")
        elif n == 13:
            inputs(0, 2)
        elif n == 14:
            inputs(2, 4)
        elif n == 15:
            inputs_rows()

    ready("dyt", "s")
    for n in range(steps):
        if n < count:
            give_half(n)
        allowed(n)
        if n < count:
            go(n, 0)
        if 0 <= n - 1 < count:
            merge(n - 1)
        if n - 1 - 1 * LAG in range(count):
            halve(n - 1 - 1 * LAG)
        if n - 1 - 2 * LAG in range(count):
            quarter(n - 1 - 2 * LAG)
        if n - 1 - 3 * LAG in range(count):
            along(n - 1 - 3 * LAG)
        if n - 1 - 4 * LAG in range(count):
            end(n - 1 - 4 * LAG)
        freed(n)
        work(n)
    for n in range(count - 3, count):
        for t in range(13):
            if of(n, t) and (t > 0 or n > count - 3):
                move(n, t).wait_send()
        final_copy(n).wait()
    ready("grad_x")


def run_backward(lengths, decay_rate, x, dy, kept):
    rows, width = x.shape
    hidden_size = kept[2].shape[1]
    part = width // 32
    row = jax.ShapeDtypeStruct((rows, width), BF16)
    outs = (
        [row] * 2
        + [jax.ShapeDtypeStruct((part, width), F32)] * 5
        + [jax.ShapeDtypeStruct((part, hidden_size), F32)] * 3
    )
    rv = pltpu.VMEM((rows, width), BF16)
    fv = pltpu.VMEM((rows, width), F32)
    tv = pltpu.VMEM((rows, hidden_size), BF16)
    wv = pltpu.VMEM((width, hidden_size), BF16)
    n = 1024
    h = n // 2
    scratch = (
        [pltpu.VMEM((hidden_size, width), BF16), wv, wv, tv, tv, tv, rv, fv, fv]
        + [rv] * 9
        + [pltpu.VMEM((H, 2, DH, DH), BF16)]
        + table_scratch(rows)
        + [pltpu.VMEM((width, rows), BF16)] * 4
        + scan_scratch()
        + [
            pltpu.VMEM((2, 512, n), BF16),
            pltpu.VMEM((2, 512, n), BF16),
            pltpu.VMEM((3, 2, 2, 2, 2, 32, n), BF16),
            pltpu.VMEM((3, 2, 2, 2, 32, h), BF16),
            pltpu.VMEM((3, 2, 2, 2, 32, h), BF16),
            pltpu.VMEM((3, 2, 2, 2, 32, h), BF16),
            pltpu.VMEM((3, 2, 2, 2, 32, h), BF16),
            pltpu.VMEM((3, 2, 2, 2, 32, h), BF16),
            pltpu.VMEM((3, 2, 2, 32, 2 * h), BF16),
            pltpu.VMEM((3, 2, 32, 2 * h), BF16),
            pltpu.VMEM((3, 2, 32, 2 * h), BF16),
            pltpu.VMEM((3, 32, 2 * h), BF16),
            pltpu.VMEM((3, 32, n), F32),
            pltpu.VMEM((3, 2, 2, 2, 32, UPRIGHT), BF16),
            pltpu.VMEM((3, 2, 2, 2, 32, UPRIGHT), BF16),
            pltpu.VMEM((3, 2, 2, 32, UPRIGHT), BF16),
            pltpu.VMEM((3, 2, 2, 32, UPRIGHT), BF16),
            pltpu.VMEM((3, 2, 32, UPRIGHT // 2), BF16),
            pltpu.VMEM((3, 2, 32, UPRIGHT // 2), BF16),
            pltpu.VMEM((3, 2, 32, UPRIGHT // 2), BF16),
            pltpu.VMEM((3, 2, 32, UPRIGHT // 2), BF16),
            pltpu.VMEM((3, 2, 32, UPRIGHT // 2), BF16),
        ]
        + [pltpu.SemaphoreType.DMA((39,))] * 2
        + [pltpu.SemaphoreType.REGULAR((5,))]
        + [pltpu.SemaphoreType.DMA((28,)), pltpu.SemaphoreType.DMA((3,))]
        + [pltpu.SemaphoreType.DMA((13,))] * 2
    )
    return pl.pallas_call(
        backward_kernel,
        out_shape=outs,
        in_specs=[SMEM, SMEM] + [ANY] * (2 + len(kept)),
        out_specs=[ANY] * len(outs),
        scratch_shapes=scratch,
        compiler_params=pltpu.CompilerParams(
            collective_id=1, has_side_effects=True, vmem_limit_bytes=VMEM_BYTES
        ),
        name="backward",
    )(lengths, decay_rate, x, dy, *kept)


def hand_over_kernel(*refs):
    count = (len(refs) - 2) // 3
    sources, targets, held = (refs[i * count : (i + 1) * count] for i in range(3))
    sems_in, sems_out = refs[3 * count :]
    fetches = [
        pltpu.make_async_copy(src, dst, sems_in.at[i])
        for i, (src, dst) in enumerate(zip(sources, held))
    ]
    for fetch in fetches:
        fetch.start()
    stores = []
    for i in range(count):
        fetches[i].wait()
        store = pltpu.make_async_copy(held[i], targets[i], sems_out.at[i])
        store.start()
        stores.append(store)
    for store in stores:
        store.wait()


def hand_over(arrays):
    return pl.pallas_call(
        hand_over_kernel,
        out_shape=[jax.ShapeDtypeStruct(a.shape, a.dtype) for a in arrays],
        in_specs=[ANY] * len(arrays),
        out_specs=[ANY] * len(arrays),
        scratch_shapes=[pltpu.VMEM(a.shape, a.dtype) for a in arrays]
        + [pltpu.SemaphoreType.DMA((len(arrays),))] * 2,
        name="hand_over",
    )(*arrays)


def local_fast(tokens, cotangent, lengths, decay_rate, *weights):
    mb, chunk, width = tokens.shape
    x = tokens.reshape(mb * chunk, width)
    dy = cotangent.reshape(mb * chunk, width)
    kept = run_forward(lengths, decay_rate, x, dy, weights)
    mixed, grad_x, *grads = hand_over(run_backward(lengths, decay_rate, x, dy, kept))
    return (mixed.reshape(tokens.shape), grad_x.reshape(tokens.shape), *grads[:-1], grads[-1].T)


def solution(mesh):
    rows = P(None, AXES, None)
    in_specs = (rows, rows, P(), P()) + (P("fsdp", None),) * 7 + (P(None, "fsdp"),)
    out_specs = (rows, rows) + (P(AXES, None),) * 7 + (P(None, AXES),)
    fast = mesh.shape["fsdp"] == 8 and mesh.shape["head"] == 4
    local = local_fast if fast else local_any
    return jax.shard_map(local, mesh=mesh, in_specs=in_specs, out_specs=out_specs, check_vma=False)
```
